256 devices in a mesh: leaf: 8 (over z), node: 32 (over x, y, core).
Axes of the slice: x: 4, y: 4, z: 8, core: 2. Of those that a mesh axis runs over, the one named last changes fastest.
Arguments:
- query_tree: bfloat16 [32768, 4096], P(('leaf', 'node')), may hold values from -6 to 6
- output_tree: bfloat16 [32768, 4096], P(('leaf', 'node')), may hold values from -6 to 6
- cotangent_tree: bfloat16 [32768, 4096], P(('leaf', 'node')), may hold values from -36 to 36
- log_norm_tree: float32 [32, 32768], P(None, ('leaf', 'node')), may hold values from 6.5 to 8
- key_value_tree: bfloat16 [32768, 1024], P(('leaf', 'node')), may hold values from -6 to 6
- query_root: bfloat16 [256, 4096], P(('leaf', 'node')), may hold values from -6 to 6
- output_root: bfloat16 [256, 4096], P(('leaf', 'node')), may hold values from -6 to 6
- cotangent_root: bfloat16 [256, 4096], P(('leaf', 'node')), may hold values from -36 to 36
- log_norm_root: float32 [32, 256], P(None, ('leaf', 'node')), may hold values from 6.5 to 8
- key_value_root: bfloat16 [256, 1024], P(('leaf', 'node')), may hold values from -6 to 6
- parent: int32 [8, 24], P('leaf'), may hold values from 0 to 22, as said below
- node_length: int32 [8, 24], P('leaf'), may hold values from 1 to 512, 4096 in all within a row
Outputs:
- grad_query_tree: float32 [32768, 4096], P(('leaf', 'node'))
- grad_query_root: float32 [256, 4096], P(('leaf', 'node'))
- grad_pairs_tree: float32 [32768, 1024], P(('leaf', 'node'))
- grad_pairs_root: float32 [256, 1024], P(('leaf', 'node'))
The draws below stay inside these ranges and needn't reach their ends.
Inputs may be any that keep to these rules, and one draw needn't show every extreme that they name: Each row lists, for the nodes of one subtree in the order of their token rows, the position of each node's parent in that row; entry 0 is 0 and marks the subtree's top node; every other node's parent comes before it; the last node's parent is the node just before it. `node_length`: each row holds the token rows of one subtree's nodes, in the same node order as `parent`, summing to 4096.
All inputs are finite; a program needn't handle non-finite values.
Results may differ from the reference program's by a relative error of at most 0.003.
Values may be sent and summed in bfloat16 or wider, within the bound.
No kernel may reach another device: no remote copies, remote signals or barrier semaphores. Data moves between devices by JAX's collectives and lax.ppermute only.
A program may use at most 256 MiB of HBM per device.

```python
import math
import jax
import jax.numpy as jnp
import numpy as np
from jax import lax

HD = 128
QH = 32
KH = 4
NODES = 24
GROUP = 8
QW = 4096
KW = 512
TREES = 8
SUB_TOK = 4096
ALL_TOK = 32768
ROOT = 256


def draw_parent(key, part):
    key = jax.random.fold_in(key, 7)
    labels = jnp.arange(NODES, dtype=jnp.int32)
    ceiling = jnp.maximum(labels, 1)
    picks = jax.random.randint(key, (TREES, NODES), 0, ceiling[None, :])
    picks = jnp.where(labels[None, :] == 0, 0, picks)
    picks = jnp.where(labels[None, :] == NODES - 1, NODES - 2, picks)
    return picks.astype(jnp.int32)


def steps_of(rng, extent, shards, low, top_value):
    def one(position, blocks):
        draws = jax.random.uniform(jax.random.fold_in(jax.random.fold_in(rng, 6), position), (blocks,), jnp.float32, low / len(shards), top_value / len(shards))
        return jnp.repeat(jnp.exp(draws), extent[position] // blocks).reshape((-1,) + (1,) * (len(extent) - position - 1))

    gain = one(*shards[0])
    for cut in shards[1:]:
        gain = gain * one(*cut)
    return gain


def profile(count, total, limit, skew):
    weights = [(1 << 20) // math.isqrt(rank ** skew) + 1 for rank in range(2, count + 1)]
    surplus, holding = total - limit - (count - 1), [1] * (count - 1)
    while surplus > 0:
        candidates = [i for i in range(count - 1) if holding[i] < limit]
        mass, remaining = sum([weights[i] for i in candidates]), surplus
        for i in candidates:
            more = min(limit - holding[i], max(1, remaining * weights[i] // mass), surplus)
            holding[i] = holding[i] + more
            surplus = surplus - more
    return np.array([limit] + holding)


def uneven_parts(key, number_of, total, limit, lean):
    if number_of == 2:
        one = jax.random.randint(key, (), max(1, total - limit), min(limit, total - 1) + 1)
        return jnp.stack([one, total - one])
    sizes = jnp.asarray(profile(number_of, total, limit, lean), jnp.int32)
    couples = (number_of - 1) // 2
    giver, receiver = sizes[1:1 + 2 * couples:2], sizes[2:2 + 2 * couples:2]
    room = jnp.minimum(giver - 1, limit - receiver)
    moved = jax.random.randint(jax.random.fold_in(key, 1), (couples,), 0, 1 << 20) % (room + 1)
    sizes = sizes.at[1:1 + 2 * couples:2].set(giver - moved).at[2:2 + 2 * couples:2].set(receiver + moved)
    return sizes[jax.random.permutation(jax.random.fold_in(key, 2), number_of)]


def scatter_about(own_key, dims, width, most, cuts=(), held_as=jnp.bfloat16):
    gain = steps_of(own_key, dims, cuts, -0.22, 0.18) if cuts else 1.0
    drawn = jax.random.normal(own_key, dims, jnp.float32) * width * gain
    return jnp.minimum(jnp.maximum(drawn, -most), most).astype(held_as)


def setup_inputs(seed: int = 0) -> dict:
    streams_of = jax.random.split(jax.random.key(seed), 13)
    query_tree = scatter_about(streams_of[0], (ALL_TOK, QW), 1.0, 6.0, ((0, 256),))
    output_tree = scatter_about(streams_of[1], (ALL_TOK, QW), 1.0, 6.0, ((0, 256),))
    cotangent_tree = scatter_about(streams_of[2], (ALL_TOK, QW), 6.0, 36.0, ((0, 256),))
    log_norm_tree = jnp.clip(6.5 + 1.5 * jax.random.uniform(streams_of[3], (QH, ALL_TOK), jnp.float32) ** steps_of(streams_of[3], (QH, ALL_TOK), ((1, 256),), -0.2, 0.2), 6.5, 8.0)
    key_value_tree = scatter_about(streams_of[4], (ALL_TOK, 2 * KW), 1.0, 6.0, ((0, 256),))
    query_root = scatter_about(streams_of[5], (ROOT, QW), 1.0, 6.0, ((0, 256),))
    output_root = scatter_about(streams_of[6], (ROOT, QW), 1.0, 6.0, ((0, 256),))
    cotangent_root = scatter_about(streams_of[7], (ROOT, QW), 6.0, 36.0, ((0, 256),))
    log_norm_root = jnp.clip(6.5 + 1.5 * jax.random.uniform(streams_of[8], (QH, ROOT), jnp.float32) ** steps_of(streams_of[8], (QH, ROOT), ((1, 256),), -0.2, 0.2), 6.5, 8.0)
    key_value_root = scatter_about(streams_of[9], (ROOT, 2 * KW), 1.0, 6.0, ((0, 256),))
    parent = draw_parent(jax.random.fold_in(streams_of[12], 71), 0)
    node_length = jax.vmap(lambda own: uneven_parts(own, NODES, SUB_TOK, SUB_TOK // 8, 0))(jax.random.split(streams_of[11], TREES)).reshape((TREES, NODES)).astype(jnp.int32)
    return dict(query_tree=query_tree, output_tree=output_tree, cotangent_tree=cotangent_tree, log_norm_tree=log_norm_tree, key_value_tree=key_value_tree, query_root=query_root, output_root=output_root, cotangent_root=cotangent_root, log_norm_root=log_norm_root, key_value_root=key_value_root, parent=parent, node_length=node_length)


def ancestry_table(parent_row):
    node_total = parent_row.shape[0]
    labels = jnp.arange(node_total, dtype=jnp.int32)
    parent_link = ((parent_row[None, :] == labels[:, None]) & (labels[None, :] > 0)).astype(jnp.float32)
    identity = jnp.eye(node_total, dtype=jnp.float32)

    def extend(loop_index, reach_table):
        return jnp.minimum(identity + jnp.dot(reach_table, parent_link, preferred_element_type=jnp.float32), 1.0)

    return lax.fori_loop(0, node_total, extend, identity)


def node_members(length_row, positions):
    node_ends = jnp.cumsum(length_row).astype(jnp.int32)
    node_starts = node_ends - length_row
    inside = (positions[:, None] >= node_starts[None, :]) & (positions[:, None] < node_ends[None, :])
    return inside.astype(jnp.float32)


def tree_seen(members_query, members_key, ancestry, query_pos, key_pos):
    key_reach = jnp.dot(members_key, ancestry, preferred_element_type=jnp.float32)
    linked = jnp.dot(members_query, key_reach.T, preferred_element_type=jnp.float32)
    return (linked > 0.5) & (key_pos[None, :] <= query_pos[:, None])


def head_terms(queries, output, cotangent, log_norm, key_part, value_part, visible):
    row_count = queries.shape[0]
    head_count = log_norm.shape[0]
    head_width = key_part.shape[1]
    factor = head_width ** -0.5

    def to_rows(matrix):
        return matrix.reshape(row_count, head_count, head_width).transpose(1, 0, 2).reshape(head_count * row_count, head_width)

    query_rows = to_rows(queries)
    output_rows = to_rows(output)
    grad_rows = to_rows(cotangent)
    scores = jnp.dot(query_rows, key_part.T, preferred_element_type=jnp.float32).reshape(head_count, row_count, -1)
    prob_full = jnp.where(visible[None], jnp.exp(factor * scores - log_norm[:, :, None]), 0.0)
    prob_low = prob_full.astype(jnp.bfloat16).reshape(head_count * row_count, -1)
    grad_prob = jnp.dot(grad_rows, value_part.T, preferred_element_type=jnp.float32).reshape(head_count, row_count, -1)
    row_delta = jnp.sum(grad_rows.astype(jnp.float32) * output_rows.astype(jnp.float32), axis=1).reshape(head_count, row_count, 1)
    dscore = (prob_full * (grad_prob - row_delta)).astype(jnp.bfloat16).reshape(head_count * row_count, -1)
    dquery = factor * jnp.dot(dscore, key_part, preferred_element_type=jnp.float32)
    dquery = dquery.reshape(head_count, row_count, head_width).transpose(1, 0, 2).reshape(row_count, head_count * head_width)
    grad_key = factor * lax.dot_general(dscore, query_rows, (((0,), (0,)), ((), ())), preferred_element_type=jnp.float32)
    dvalue = lax.dot_general(prob_low, grad_rows, (((0,), (0,)), ((), ())), preferred_element_type=jnp.float32)
    return dquery, grad_key, dvalue


def all_heads(queries, output, cotangent, log_norm, key_value, visible):
    group_span = GROUP * HD
    kv_width = KH * HD
    query_grads, key_grads, value_grads = [], [], []
    for head_group in range(KH):
        first_col = head_group * group_span
        dquery, grad_key, dvalue = head_terms(
            queries[:, first_col:first_col + group_span],
            output[:, first_col:first_col + group_span],
            cotangent[:, first_col:first_col + group_span],
            log_norm[head_group * GROUP:(head_group + 1) * GROUP],
            key_value[:, head_group * HD:(head_group + 1) * HD],
            key_value[:, kv_width + head_group * HD:kv_width + (head_group + 1) * HD],
            visible)
        query_grads.append(dquery)
        key_grads.append(grad_key)
        value_grads.append(dvalue)
    return jnp.concatenate(query_grads, axis=1), jnp.concatenate(key_grads + value_grads, axis=1)


def reference(query_tree, output_tree, cotangent_tree, log_norm_tree, key_value_tree, query_root, output_root, cotangent_root, log_norm_root, key_value_root, parent, node_length):
    block_rows = min(512, SUB_TOK)

    def one_tree(pieces):
        queries, output, cotangent, log_norm, key_value, parent_row, length_row = pieces
        ancestry = ancestry_table(parent_row)
        positions = jnp.arange(SUB_TOK, dtype=jnp.int32)
        members = node_members(length_row, positions)
        query_grad = jnp.zeros((SUB_TOK, QW), jnp.float32)
        tree_grad = jnp.zeros((SUB_TOK, 2 * KW), jnp.float32)
        root_grad = jnp.zeros((ROOT, 2 * KW), jnp.float32)
        for first_row in range(0, SUB_TOK, block_rows):
            finish = first_row + block_rows
            visible = tree_seen(members[first_row:finish], members[:finish], ancestry, positions[first_row:finish], positions[:finish])
            visible = jnp.concatenate([jnp.ones((block_rows, ROOT), jnp.bool_), visible], axis=1)
            joined = jnp.concatenate([key_value_root, key_value[:finish]], axis=0)
            block_query, block_pairs = all_heads(queries[first_row:finish], output[first_row:finish], cotangent[first_row:finish], log_norm[:, first_row:finish], joined, visible)
            query_grad = query_grad.at[first_row:finish].set(block_query)
            root_grad = root_grad + block_pairs[:ROOT]
            tree_grad = tree_grad.at[:finish].add(block_pairs[ROOT:])
        return query_grad, tree_grad, root_grad

    stacked = (query_tree.reshape(TREES, SUB_TOK, QW),
               output_tree.reshape(TREES, SUB_TOK, QW),
               cotangent_tree.reshape(TREES, SUB_TOK, QW),
               log_norm_tree.reshape(QH, TREES, SUB_TOK).transpose(1, 0, 2),
               key_value_tree.reshape(TREES, SUB_TOK, 2 * KW),
               parent, node_length)
    query_grads, tree_grads, root_grads = lax.map(one_tree, stacked)
    root_pos = jnp.arange(ROOT, dtype=jnp.int32)
    root_visible = root_pos[None, :] <= root_pos[:, None]
    root_query, root_pairs = all_heads(query_root, output_root, cotangent_root, log_norm_root, key_value_root, root_visible)
    return (query_grads.reshape(ALL_TOK, QW), root_query, tree_grads.reshape(ALL_TOK, 2 * KW), jnp.sum(root_grads, axis=0) + root_pairs)
```

```python
import math

import jax
import jax.numpy as jnp
from jax import lax
from jax.experimental import pallas as pl
from jax.experimental.pallas import tpu as pltpu
from jax.sharding import PartitionSpec as P

HD = 128
NODES = 24
BLK = 128
TREE_BLOCKS = 32
FACTOR = HD ** (-0.5)
LOG2E = math.log2(math.e)
SCALE2 = FACTOR * LOG2E
BF = jnp.bfloat16
F4 = jnp.float32
Q0, D0, R0, T0, MSG = 0, 512, 1024, 1040, 1088
PAIR = 144
VMEM_LIMIT = 48 * 1024 * 1024


def params():
    return pltpu.CompilerParams(vmem_limit_bytes=VMEM_LIMIT)


def perm(dx, dy, dc):
    pairs = []
    for x in range(4):
        for y in range(4):
            for c in range(2):
                target = ((x + dx) % 4) * 8 + ((y + dy) % 4) * 2 + (c ^ dc)
                pairs.append((x * 8 + y * 2 + c, target))
    return pairs


def shift(array, dx=0, dy=0, dc=0):
    return lax.ppermute(array, "node", perm(dx, dy, dc))


def shift_leaf(array, step):
    return lax.ppermute(array, "leaf", [(z, (z + step) % 8) for z in range(8)])


def nt(left, right):
    return lax.dot_general(left, right, (((1,), (1,)), ((), ())), preferred_element_type=F4)


def nn(left, right):
    return lax.dot_general(left, right, (((1,), (0,)), ((), ())), preferred_element_type=F4)


def iota(shape, dim):
    return lax.broadcasted_iota(jnp.int32, shape, dim)


def flip(c, dc):
    return c if dc == 0 else 1 - c


def smem():
    return pl.BlockSpec(memory_space=pltpu.SMEM)


def vmem():
    return pl.BlockSpec(memory_space=pltpu.VMEM)


def tables_kernel(ids, parent, length, kbit, qanc, lists, counts, start, anc, kmask, qmask):
    x, y, c = ids[0], ids[1], ids[2]
    for block in range(TREE_BLOCKS):
        kmask[block] = 0
        qmask[block] = 0
    total = jnp.int32(0)
    for n in range(NODES):
        start[n] = total
        bits = jnp.int32(1 << n)
        if n > 0:
            bits = bits | anc[parent[0, n]]
        anc[n] = bits
        first = total // BLK
        total = total + length[0, n]
        last = (total - 1) // BLK

        def mark(block, carry):
            kmask[block] = kmask[block] | jnp.int32(1 << n)
            qmask[block] = qmask[block] | bits
            return carry

        lax.fori_loop(first, last + 1, mark, 0)
    positions = iota((TREE_BLOCKS, BLK), 0) * BLK + iota((TREE_BLOCKS, BLK), 1)
    table = jnp.zeros((TREE_BLOCKS, BLK), jnp.int32)
    own_bits = jnp.zeros((TREE_BLOCKS, BLK), jnp.int32)
    for n in range(NODES):
        inside = positions >= start[n]
        table = jnp.where(inside, anc[n], table)
        own_bits = jnp.where(inside, jnp.int32(1 << n), own_bits)
    qanc[...] = table
    for block in range(TREE_BLOCKS):
        row = jnp.broadcast_to(own_bits[block : block + 1, :], (BLK, BLK))
        kbit[block] = row.T
    kbit[TREE_BLOCKS] = jnp.zeros((BLK, BLK), jnp.int32)
    for i in range(8):
        mine = (lax.rem(x - i // 2 + 4, 4)) * 8 + y * 2 + flip(c, i % 2)
        seen = qmask[mine]

        def scan(block, found):
            hit = (seen & kmask[block]) != 0
            lists[i, found] = block
            return found + hit.astype(jnp.int32)

        found = lax.fori_loop(0, mine + 1, scan, jnp.int32(0))
        lists[i, found] = TREE_BLOCKS
        counts[i] = (found + 1) // 2


def make_tables(ids, parent, length):
    return pl.pallas_call(
        tables_kernel,
        in_specs=[smem(), smem(), smem()],
        out_specs=[vmem(), vmem(), smem(), smem()],
        out_shape=[
            jax.ShapeDtypeStruct((TREE_BLOCKS + 1, BLK, BLK), jnp.int32),
            jax.ShapeDtypeStruct((TREE_BLOCKS, BLK), jnp.int32),
            jax.ShapeDtypeStruct((8, 40), jnp.int32),
            jax.ShapeDtypeStruct((8,), jnp.int32),
        ],
        scratch_shapes=[
            pltpu.SMEM((NODES,), jnp.int32),
            pltpu.SMEM((NODES,), jnp.int32),
            pltpu.SMEM((TREE_BLOCKS,), jnp.int32),
            pltpu.SMEM((TREE_BLOCKS,), jnp.int32),
        ],
        compiler_params=params(),
        cost_estimate=pl.CostEstimate(
            flops=10**6, bytes_accessed=4 * 10**6, transcendentals=0
        ),
        name="tables",
    )(ids, parent, length)


def pack_pairs_kernel(pairs, root, out):
    for c in range(2):
        for x in range(4):
            cols = slice(c * 512 + x * HD, c * 512 + (x + 1) * HD)
            part = pairs[:, cols]
            tail = jnp.concatenate([root[:, cols], jnp.zeros((8, HD), F4)], axis=0)
            tail = tail.astype(BF)
            for y in range(4):
                out[x * 8 + y * 2 + c, 0:BLK, :] = part
                out[x * 8 + y * 2 + c, BLK:PAIR, :] = tail


def pack_pairs(pairs, root):
    return pl.pallas_call(
        pack_pairs_kernel,
        in_specs=[vmem(), vmem()],
        out_specs=vmem(),
        out_shape=jax.ShapeDtypeStruct((TREE_BLOCKS, PAIR, HD), BF),
        compiler_params=params(),
        name="pack_pairs",
    )(pairs, root)


def split3(value):
    high = value.astype(BF)
    rest = value - high.astype(F4)
    middle = rest.astype(BF)
    low = (rest - middle.astype(F4)).astype(BF)
    return jnp.concatenate([high, middle, low], axis=0)


def pack_rows_kernel(
    ids, query, output, cotangent, norm, rquery, routput, rcotangent, rnorm, keep, send
):
    x, c = ids[0], ids[2]
    for i in range(8):
        k, dc = i // 2, i % 2
        dest = lax.rem(x + k, 4) * 2 + flip(c, dc)
        out = send if dc else keep
        deltas = []
        for h in range(4):
            cols = pl.ds(pl.multiple_of(dest * 512 + h * HD, HD), HD)
            out[k, Q0 + h * BLK : Q0 + (h + 1) * BLK, :] = query[:, cols]
            grad = cotangent[:, cols]
            out[k, D0 + h * BLK : D0 + (h + 1) * BLK, :] = grad
            product = grad.astype(F4) * output[:, cols].astype(F4)
            deltas.append(jnp.sum(product.T, axis=0, keepdims=True))
        rgrad = rcotangent[dest]
        rdelta = jnp.sum(rgrad * routput[dest], axis=1, keepdims=True)
        place = iota((4, HD), 1) == iota((4, HD), 0) + i * 4
        rnorm_row = jnp.sum(
            jnp.where(place, rnorm[dest] * LOG2E, 0.0), axis=0, keepdims=True
        )
        rdelta_row = jnp.sum(
            jnp.where(place, jnp.broadcast_to(rdelta, (4, HD)), 0.0), axis=0, keepdims=True
        )
        rows = jnp.concatenate(
            [norm[dest] * LOG2E]
            + deltas
            + [rnorm_row, rdelta_row, jnp.zeros((6, HD), F4)],
            axis=0,
        )
        out[k, T0 : T0 + 48, :] = split3(rows)
        tile = jnp.concatenate([rquery[dest], rgrad, jnp.zeros((8, HD), F4)], axis=0)
        out[k, R0 : R0 + 16, :] = tile.astype(BF)


def pack_rows(ids, query, output, cotangent, norm, rquery, routput, rcotangent, rnorm):
    return pl.pallas_call(
        pack_rows_kernel,
        in_specs=[smem()] + [vmem()] * 8,
        out_specs=[vmem()] * 2,
        out_shape=[jax.ShapeDtypeStruct((4, MSG, HD), BF)] * 2,
        compiler_params=params(),
        name="pack_rows",
    )(ids, query, output, cotangent, norm, rquery, routput, rcotangent, rnorm)


def merge_rows_kernel(keep, other, *outs):
    for k in range(4):
        outs[k][0] = keep[k]
        outs[k][1] = other[k]


def merge_rows(keep, other):
    return pl.pallas_call(
        merge_rows_kernel,
        in_specs=[vmem()] * 2,
        out_specs=[vmem()] * 4,
        out_shape=[jax.ShapeDtypeStruct((2, MSG, HD), BF)] * 4,
        compiler_params=params(),
        name="merge_rows",
    )(keep, other)


def unsplit(rows):
    wide = rows.astype(F4)
    return wide[0:16] + wide[16:32] + wide[32:48]


def root_kernel(ids, own, other, *refs):
    msgs, refs = refs[0:4], refs[4:]
    dq_out, roots, keys, values, keys_t, rkeys, root_rows = refs
    x, y, c, z = ids[0], ids[1], ids[2], ids[3]

    def load(key_ref, value_ref):
        for block in range(TREE_BLOCKS):
            part = key_ref[block, 0:BLK, :]
            keys[block] = part
            keys_t[block] = part.astype(F4).T.astype(BF)
            values[block] = value_ref[block, 0:BLK, :]
            for s, ref in ((0, key_ref), (1, value_ref)):
                tail = ref[block, BLK:PAIR, :].astype(F4)
                for kz in range(8):
                    rkeys[s, kz, block : block + 1, :] = tail[kz : kz + 1]

    @pl.when(c == 0)
    def _():
        load(own, other)

    @pl.when(c != 0)
    def _():
        load(other, own)

    keys[TREE_BLOCKS] = jnp.zeros((BLK, HD), BF)
    keys_t[TREE_BLOCKS] = jnp.zeros((BLK, HD), BF)
    values[TREE_BLOCKS] = jnp.zeros((BLK, HD), BF)

    key = rkeys[0].reshape(256, HD)
    value = rkeys[1].reshape(256, HD).astype(BF)
    key_t = key.T.astype(BF)
    key = key.astype(BF)
    dk = jnp.zeros((256, HD), F4)
    dv = jnp.zeros((256, HD), F4)
    root_rows[...] = jnp.zeros(root_rows.shape, F4)
    special = jnp.zeros((16, HD), F4)
    for i in range(8):
        msg, dc = msgs[i // 2], i % 2
        terms = unsplit(msg[dc, T0 : T0 + 48, :])
        special = special + terms
        tile = msg[dc, R0 : R0 + 16, :].astype(F4)
        root_rows[0, i * 4 : i * 4 + 4, :] = tile[0:4]
        root_rows[1, i * 4 : i * 4 + 4, :] = tile[4:8]
        for h in range(4):
            query = msg[dc, Q0 + h * BLK : Q0 + (h + 1) * BLK, :]
            grad = msg[dc, D0 + h * BLK : D0 + (h + 1) * BLK, :]
            prob = jnp.exp2(nt(key, query) * SCALE2 - terms[h : h + 1, :])
            dscore = (prob * (nt(value, grad) - terms[4 + h : 5 + h, :])).astype(BF)
            dv = dv + nn(prob.astype(BF), grad)
            dk = dk + nn(dscore, query)
            dq_out[i, :, h * BLK : (h + 1) * BLK] = nn(key_t, dscore)
    query = root_rows[0].astype(BF)
    grad = root_rows[1].astype(BF)
    lane, row = iota((256, HD), 1), iota((256, HD), 0)
    source = lane // 4
    source_x = lax.rem(x - source // 2 + 16, 4)
    source_c = jnp.where(source % 2 == 0, c, 1 - c)
    query_pos = z * 32 + source_x * 8 + y * 2 + source_c
    key_pos = lax.rem(z - row // 32 + 8, 8) * 32 + row % 32
    mask = (lane < 32) & (key_pos <= query_pos)
    prob = jnp.where(mask, jnp.exp2(nt(key, query) * SCALE2 - special[8:9, :]), 0.0)
    dscore = (prob * (nt(value, grad) - special[9:10, :])).astype(BF)
    dv = dv + nn(prob.astype(BF), grad)
    dk = dk + nn(dscore, query)
    dq_out[8, :, 0:BLK] = nn(key_t, dscore)
    roots[:, 0] = dk.reshape(8, 32, HD)
    roots[:, 1] = dv.reshape(8, 32, HD)


def root_part(ids, own, other, msgs):
    blocks = jax.ShapeDtypeStruct((TREE_BLOCKS + 1, BLK, HD), BF)
    return pl.pallas_call(
        root_kernel,
        in_specs=[smem()] + [vmem()] * 6,
        out_specs=[vmem()] * 5,
        out_shape=[
            jax.ShapeDtypeStruct((9, HD, 512), F4),
            jax.ShapeDtypeStruct((8, 2, 32, HD), F4),
            blocks,
            blocks,
            blocks,
        ],
        scratch_shapes=[
            pltpu.VMEM((2, 8, 32, HD), F4),
            pltpu.VMEM((2, HD, HD), F4),
        ],
        compiler_params=params(),
        cost_estimate=pl.CostEstimate(
            flops=2 * 10**9, bytes_accessed=10**7, transcendentals=10**6
        ),
        name="root_part",
    )(ids, own, other, *msgs)


def tree_body(ids, lists, counts, kbit, qanc, keys, values, keys_t, dq_root, msgs, ks, outs,
              acc, dk, dv):
    x, y, c = ids[0], ids[1], ids[2]
    dk[...] = jnp.zeros(dk.shape, F4)
    dv[...] = jnp.zeros(dv.shape, F4)
    root_dq = dq_root[8, :, 0:BLK].T * FACTOR
    pad = jnp.zeros((12, HD), F4)
    base = iota((BLK, BLK), 0)
    for slot, k in enumerate(ks):
        msg, out = msgs[slot], outs[slot]
        for dc in range(2):
            tile = root_dq[8 * k + 4 * dc : 8 * k + 4 * dc + 4]
            out[dc, 512:528, :] = jnp.concatenate([tile, pad], axis=0).astype(BF)

        def query_block(dc, carry):
            i = k * 2 + dc
            mine = lax.rem(x - k + 4, 4) * 8 + y * 2 + jnp.where(dc == 0, c, 1 - c)
            anc_row = jnp.broadcast_to(qanc[pl.ds(mine, 1), :], (2 * BLK, BLK))
            query_pos = iota((2 * BLK, BLK), 1) + mine * BLK
            terms = unsplit(msg[dc, T0 : T0 + 48, :])
            acc[...] = dq_root[i]

            def pair(j, inner):
                b0, b1 = lists[i, 2 * j], lists[i, 2 * j + 1]
                key = jnp.concatenate([keys[b0], keys[b1]], axis=0)
                value = jnp.concatenate([values[b0], values[b1]], axis=0)
                key_t = jnp.concatenate([keys_t[b0], keys_t[b1]], axis=1)
                bits = jnp.concatenate([kbit[b0], kbit[b1]], axis=0)
                key_pos = jnp.concatenate([base + b0 * BLK, base + b1 * BLK], axis=0)
                mask = ((bits & anc_row) != 0) & (key_pos <= query_pos)
                dk_part = jnp.zeros((2 * BLK, HD), F4)
                dv_part = jnp.zeros((2 * BLK, HD), F4)
                for h in range(4):
                    query = msg[dc, Q0 + h * BLK : Q0 + (h + 1) * BLK, :]
                    grad = msg[dc, D0 + h * BLK : D0 + (h + 1) * BLK, :]
                    score = nt(key, query)
                    prob = jnp.where(
                        mask, jnp.exp2(score * SCALE2 - terms[h : h + 1, :]), 0.0
                    )
                    grad_prob = nt(value, grad)
                    dscore = (prob * (grad_prob - terms[4 + h : 5 + h, :])).astype(BF)
                    dv_part = dv_part + nn(prob.astype(BF), grad)
                    dk_part = dk_part + nn(dscore, query)
                    cols = slice(h * BLK, (h + 1) * BLK)
                    acc[:, cols] = acc[:, cols] + nn(key_t, dscore)
                dk[b0] = dk[b0] + dk_part[0:BLK]
                dv[b0] = dv[b0] + dv_part[0:BLK]
                dk[b1] = dk[b1] + dk_part[BLK:]
                dv[b1] = dv[b1] + dv_part[BLK:]
                return inner

            lax.fori_loop(0, counts[i], pair, 0)
            for h in range(4):
                done = acc[:, h * BLK : (h + 1) * BLK].T * FACTOR
                out[dc, h * BLK : (h + 1) * BLK, :] = done.astype(BF)
            return carry

        lax.fori_loop(0, 2, query_block, 0)


def first_kernel(ids, lists, counts, kbit, qanc, keys, values, keys_t, dq_root, m0, m1,
                 o0, o1, dk, dv, acc):
    tree_body(ids, lists, counts, kbit, qanc, keys, values, keys_t, dq_root, (m0, m1), (1, 2),
              (o0, o1), acc, dk, dv)


def last_kernel(ids, lists, counts, kbit, qanc, keys, values, keys_t, dq_root, m0, m1, dk0, dv0,
                roots, o0, o1, keep, send, acc, dk, dv):
    tree_body(ids, lists, counts, kbit, qanc, keys, values, keys_t, dq_root, (m0, m1), (3, 0),
              (o0, o1), acc, dk, dv)

    def store(dk_to, dv_to):
        for block in range(TREE_BLOCKS):
            dk_to[block, 0:BLK, :] = dk[block] + dk0[block]
            dv_to[block, 0:BLK, :] = dv[block] + dv0[block]
            for s, to in ((0, dk_to), (1, dv_to)):
                row = jnp.broadcast_to(roots[s, block : block + 1, :], (16, HD))
                to[block, BLK:PAIR, :] = jnp.where(iota((16, HD), 0) == 0, row, 0.0)

    @pl.when(ids[2] == 0)
    def _():
        store(keep, send)

    @pl.when(ids[2] != 0)
    def _():
        store(send, keep)


def tree_part(kernel, name, shared, msgs, extra):
    part = jax.ShapeDtypeStruct((2, 528, HD), BF)
    sums = jax.ShapeDtypeStruct((TREE_BLOCKS + 1, BLK, HD), F4)
    scratch = pltpu.VMEM((TREE_BLOCKS + 1, BLK, HD), F4)
    final = jax.ShapeDtypeStruct((TREE_BLOCKS, PAIR, HD), F4)
    last = len(extra) > 0
    return pl.pallas_call(
        kernel,
        in_specs=[smem()] * 3 + [vmem()] * (6 + len(msgs) + len(extra)),
        out_specs=[vmem()] * 4,
        out_shape=[part, part] + ([final, final] if last else [sums, sums]),
        scratch_shapes=[pltpu.VMEM((HD, 512), F4)] + ([scratch, scratch] if last else []),
        compiler_params=params(),
        cost_estimate=pl.CostEstimate(
            flops=5 * 10**9, bytes_accessed=16 * 10**6, transcendentals=4 * 10**6
        ),
        name=name,
    )(*shared, *msgs, *extra)


def unpack_query_kernel(ids, *refs):
    x, c = ids[0], ids[2]
    straight, crossed, out, root_out = refs[0:4], refs[4], refs[5], refs[6]
    for i in range(8):
        k, dc = i // 2, i % 2
        dest = lax.rem(x + k, 4) * 2 + flip(c, dc)
        part = crossed[k] if dc else straight[k][0]
        for h in range(4):
            cols = pl.ds(pl.multiple_of(dest * 512 + h * HD, HD), HD)
            out[:, cols] = part[h * BLK : (h + 1) * BLK, :].astype(F4)
        root_out[dest] = part[512:528, :].astype(F4)[0:4]


def unpack_query(ids, parts, crossed):
    return pl.pallas_call(
        unpack_query_kernel,
        in_specs=[smem()] + [vmem()] * 5,
        out_specs=[vmem()] * 2,
        out_shape=[
            jax.ShapeDtypeStruct((BLK, 4096), F4),
            jax.ShapeDtypeStruct((8, 4, HD), F4),
        ],
        compiler_params=params(),
        name="unpack_query",
    )(ids, *parts, crossed)


def unpack_pairs_kernel(parts, out, root_out):
    for c in range(2):
        for x in range(4):
            total = parts[x * 8 + c].astype(F4)
            for y in range(1, 4):
                total = total + parts[x * 8 + y * 2 + c].astype(F4)
            if c == 0:
                total = total * FACTOR
            cols = slice(c * 512 + x * HD, c * 512 + (x + 1) * HD)
            out[:, cols] = total[0:BLK]
            root_out[:, cols] = total[BLK : BLK + 1]


def unpack_pairs(parts):
    return pl.pallas_call(
        unpack_pairs_kernel,
        in_specs=[vmem()],
        out_specs=[vmem()] * 2,
        out_shape=[
            jax.ShapeDtypeStruct((BLK, 1024), F4),
            jax.ShapeDtypeStruct((1, 1024), F4),
        ],
        compiler_params=params(),
        name="unpack_pairs",
    )(parts)


def shards(
    query_tree,
    output_tree,
    cotangent_tree,
    log_norm_tree,
    key_value_tree,
    query_root,
    output_root,
    cotangent_root,
    log_norm_root,
    key_value_root,
    parent,
    node_length,
):
    node = lax.axis_index("node")
    leaf = lax.axis_index("leaf")
    ids = jnp.stack([node // 8, node // 2 % 4, node % 2, leaf]).astype(jnp.int32)

    root_pairs = key_value_root
    for step in (1, 2, 4):
        root_pairs = jnp.concatenate([root_pairs, shift_leaf(root_pairs, step)], axis=0)

    keep, send = pack_rows(
        ids,
        query_tree,
        output_tree,
        cotangent_tree,
        log_norm_tree.reshape(8, 4, BLK),
        query_root.astype(F4).reshape(8, 4, HD),
        output_root.astype(F4).reshape(8, 4, HD),
        cotangent_root.astype(F4).reshape(8, 4, HD),
        log_norm_root.reshape(8, 4, 1),
    )
    merged = merge_rows(keep, shift(send, dc=1))
    packed = pack_pairs(key_value_tree, root_pairs.astype(F4))
    packed, *merged = lax.optimization_barrier((packed, *merged))
    msgs = [merged[0]] + [shift(merged[k], dx=k) for k in range(1, 4)]
    own = lax.all_to_all(packed, "node", 0, 0, tiled=True)
    other = shift(own, dc=1)
    kbit, qanc, lists, counts = make_tables(ids, parent, node_length)

    dq_root, roots, keys, values, keys_t = root_part(ids, own, other, msgs)
    shared = (ids, lists, counts, kbit, qanc, keys, values, keys_t, dq_root)
    part1, part2, dk0, dv0 = tree_part(first_kernel, "tree_first", shared, msgs[1:3], ())
    roots = roots[0:2] + sum(shift_leaf(roots[2 * a : 2 * a + 2], -2 * a) for a in range(1, 4))
    roots = roots[0] + shift_leaf(roots[1], -1)
    part3, part0, keep, send = tree_part(
        last_kernel, "tree_last", shared, (msgs[3], msgs[0]), (dk0, dv0, roots)
    )
    back = [part0] + [shift(part, dx=-k) for k, part in ((1, part1), (2, part2), (3, part3))]

    total = (keep + shift(send, dc=1)).astype(BF)
    grads = lax.all_to_all(total, "node", 0, 0, tiled=True)
    grad_pairs, grad_root = unpack_pairs(grads)

    crossed = shift(jnp.stack([part[1] for part in back], axis=0), dc=1)
    grad_query, grad_query_root = unpack_query(ids, back, crossed)
    return grad_query, grad_query_root.reshape(1, 4096), grad_pairs, grad_root


def solution(mesh):
    rows = P(("leaf", "node"), None)
    lanes = P(None, ("leaf", "node"))
    tree = P("leaf", None)
    return jax.shard_map(
        shards,
        mesh=mesh,
        in_specs=(rows, rows, rows, lanes, rows, rows, rows, rows, lanes, rows, tree, tree),
        out_specs=(rows, rows, rows, rows),
        check_vma=False,
    )
```

```python
import math

import jax
import jax.numpy as jnp
from jax import lax
from jax.experimental import pallas as pl
from jax.experimental.pallas import tpu as pltpu
from jax.sharding import PartitionSpec as P

HD = 128
NODES = 24
BLK = 128
TREE_BLOCKS = 32
FACTOR = HD ** (-0.5)
LOG2E = math.log2(math.e)
SCALE2 = FACTOR * LOG2E
BF = jnp.bfloat16
F4 = jnp.float32
Q0, D0, R0, T0, MSG = 0, 512, 1024, 1040, 1088
PAIR = 144
VMEM_LIMIT = 48 * 1024 * 1024


def params():
    return pltpu.CompilerParams(vmem_limit_bytes=VMEM_LIMIT)


def perm(dx, dy, dc):
    pairs = []
    for x in range(4):
        for y in range(4):
            for c in range(2):
                target = ((x + dx) % 4) * 8 + ((y + dy) % 4) * 2 + (c ^ dc)
                pairs.append((x * 8 + y * 2 + c, target))
    return pairs


def shift(array, dx=0, dy=0, dc=0):
    return lax.ppermute(array, "node", perm(dx, dy, dc))


def shift_leaf(array, step):
    return lax.ppermute(array, "leaf", [(z, (z + step) % 8) for z in range(8)])


def nt(left, right):
    return lax.dot_general(left, right, (((1,), (1,)), ((), ())), preferred_element_type=F4)


def nn(left, right):
    return lax.dot_general(left, right, (((1,), (0,)), ((), ())), preferred_element_type=F4)


def iota(shape, dim):
    return lax.broadcasted_iota(jnp.int32, shape, dim)


def flip(c, dc):
    return c if dc == 0 else 1 - c


def smem():
    return pl.BlockSpec(memory_space=pltpu.SMEM)


def vmem():
    return pl.BlockSpec(memory_space=pltpu.VMEM)


def tables_kernel(ids, parent, length, kbit, qanc, lists, counts, start, anc, kmask, qmask):
    x, y, c = ids[0], ids[1], ids[2]
    for block in range(TREE_BLOCKS):
        kmask[block] = 0
        qmask[block] = 0
    total = jnp.int32(0)
    for n in range(NODES):
        start[n] = total
        bits = jnp.int32(1 << n)
        if n > 0:
            bits = bits | anc[parent[0, n]]
        anc[n] = bits
        first = total // BLK
        total = total + length[0, n]
        last = (total - 1) // BLK

        def mark(block, carry):
            kmask[block] = kmask[block] | jnp.int32(1 << n)
            qmask[block] = qmask[block] | bits
            return carry

        lax.fori_loop(first, last + 1, mark, 0)
    positions = iota((TREE_BLOCKS, BLK), 0) * BLK + iota((TREE_BLOCKS, BLK), 1)
    table = jnp.zeros((TREE_BLOCKS, BLK), jnp.int32)
    own_bits = jnp.zeros((TREE_BLOCKS, BLK), jnp.int32)
    for n in range(NODES):
        inside = positions >= start[n]
        table = jnp.where(inside, anc[n], table)
        own_bits = jnp.where(inside, jnp.int32(1 << n), own_bits)
    qanc[...] = table
    for block in range(TREE_BLOCKS):
        row = jnp.broadcast_to(own_bits[block : block + 1, :], (BLK, BLK))
        kbit[block] = row.T
    kbit[TREE_BLOCKS] = jnp.zeros((BLK, BLK), jnp.int32)
    for i in range(8):
        mine = (lax.rem(x - i // 2 + 4, 4)) * 8 + y * 2 + flip(c, i % 2)
        seen = qmask[mine]

        def scan(block, found):
            hit = (seen & kmask[block]) != 0
            lists[i, found] = block
            return found + hit.astype(jnp.int32)

        found = lax.fori_loop(0, mine + 1, scan, jnp.int32(0))
        lists[i, found] = TREE_BLOCKS
        counts[i] = (found + 1) // 2


def make_tables(ids, parent, length):
    return pl.pallas_call(
        tables_kernel,
        in_specs=[smem(), smem(), smem()],
        out_specs=[vmem(), vmem(), smem(), smem()],
        out_shape=[
            jax.ShapeDtypeStruct((TREE_BLOCKS + 1, BLK, BLK), jnp.int32),
            jax.ShapeDtypeStruct((TREE_BLOCKS, BLK), jnp.int32),
            jax.ShapeDtypeStruct((8, 40), jnp.int32),
            jax.ShapeDtypeStruct((8,), jnp.int32),
        ],
        scratch_shapes=[
            pltpu.SMEM((NODES,), jnp.int32),
            pltpu.SMEM((NODES,), jnp.int32),
            pltpu.SMEM((TREE_BLOCKS,), jnp.int32),
            pltpu.SMEM((TREE_BLOCKS,), jnp.int32),
        ],
        compiler_params=params(),
        cost_estimate=pl.CostEstimate(
            flops=10**6, bytes_accessed=4 * 10**6, transcendentals=0
        ),
        name="tables",
    )(ids, parent, length)


def pack_pairs_kernel(pairs, out):
    for c in range(2):
        for x in range(4):
            cols = slice(c * 512 + x * HD, c * 512 + (x + 1) * HD)
            out[x * 2 + c] = pairs[:, cols]


def pack_pairs(pairs):
    return pl.pallas_call(
        pack_pairs_kernel,
        in_specs=[vmem()],
        out_specs=vmem(),
        out_shape=jax.ShapeDtypeStruct((8, BLK, HD), BF),
        compiler_params=params(),
        name="pack_pairs",
    )(pairs)


def pack_root_kernel(root, out):
    for c in range(2):
        for x in range(4):
            cols = slice(c * 512 + x * HD, c * 512 + (x + 1) * HD)
            part = root[:, cols].astype(F4)
            part = jnp.concatenate([part, jnp.zeros((8, HD), F4)], axis=0).astype(BF)
            for y in range(4):
                out[x * 8 + y * 2 + c] = part


def pack_root(root):
    return pl.pallas_call(
        pack_root_kernel,
        in_specs=[vmem()],
        out_specs=vmem(),
        out_shape=jax.ShapeDtypeStruct((TREE_BLOCKS, 16, HD), BF),
        compiler_params=params(),
        name="pack_root",
    )(root)


def split3(value):
    high = value.astype(BF)
    rest = value - high.astype(F4)
    middle = rest.astype(BF)
    low = (rest - middle.astype(F4)).astype(BF)
    return jnp.concatenate([high, middle, low], axis=0)


def pack_rows_kernel(
    ids, query, output, cotangent, norm, rquery, routput, rcotangent, rnorm, keep, send
):
    x, c = ids[0], ids[2]
    for i in range(8):
        k, dc = i // 2, i % 2
        dest = lax.rem(x + k, 4) * 2 + flip(c, dc)
        out = send if dc else keep
        deltas = []
        for h in range(4):
            cols = pl.ds(pl.multiple_of(dest * 512 + h * HD, HD), HD)
            out[k, Q0 + h * BLK : Q0 + (h + 1) * BLK, :] = query[:, cols]
            grad = cotangent[:, cols]
            out[k, D0 + h * BLK : D0 + (h + 1) * BLK, :] = grad
            product = grad.astype(F4) * output[:, cols].astype(F4)
            deltas.append(jnp.sum(product.T, axis=0, keepdims=True))
        lane = iota((1, HD), 1)
        rnorm_row = jnp.zeros((1, HD), F4)
        rdelta_row = jnp.zeros((1, HD), F4)
        rquery_rows, rgrad_rows = [], []
        for h in range(4):
            cols = pl.ds(pl.multiple_of(dest * 512 + h * HD, HD), HD)
            rgrad = rcotangent[:, cols].astype(F4)
            rquery_rows.append(rquery[:, cols].astype(F4))
            rgrad_rows.append(rgrad)
            rdelta = jnp.sum(rgrad * routput[:, cols].astype(F4), axis=1, keepdims=True)
            here = lane == i * 4 + h
            rnorm_row = jnp.where(here, rnorm[dest * 4 + h] * LOG2E, rnorm_row)
            rdelta_row = jnp.where(here, jnp.broadcast_to(rdelta, (1, HD)), rdelta_row)
        rows = jnp.concatenate(
            [norm[pl.ds(dest * 4, 4), :] * LOG2E]
            + deltas
            + [rnorm_row, rdelta_row, jnp.zeros((6, HD), F4)],
            axis=0,
        )
        out[k, T0 : T0 + 48, :] = split3(rows)
        tile = jnp.concatenate(rquery_rows + rgrad_rows + [jnp.zeros((8, HD), F4)], axis=0)
        out[k, R0 : R0 + 16, :] = tile.astype(BF)


def pack_rows(ids, query, output, cotangent, norm, rquery, routput, rcotangent, rnorm):
    return pl.pallas_call(
        pack_rows_kernel,
        in_specs=[smem()] + [vmem()] * 7 + [smem()],
        out_specs=[vmem()] * 2,
        out_shape=[jax.ShapeDtypeStruct((4, MSG, HD), BF)] * 2,
        compiler_params=params(),
        name="pack_rows",
    )(ids, query, output, cotangent, norm, rquery, routput, rcotangent, rnorm)


def merge_rows_kernel(keep, other, *outs):
    for k in range(4):
        outs[k][0] = keep[k]
        outs[k][1] = other[k]


def merge_rows(keep, other):
    return pl.pallas_call(
        merge_rows_kernel,
        in_specs=[vmem()] * 2,
        out_specs=[vmem()] * 4,
        out_shape=[jax.ShapeDtypeStruct((2, MSG, HD), BF)] * 4,
        compiler_params=params(),
        name="merge_rows",
    )(keep, other)


def unsplit(rows):
    wide = rows.astype(F4)
    return wide[0:16] + wide[16:32] + wide[32:48]


def place(y, ky, block):
    return (block // 2) * 8 + lax.rem(y - ky + 4, 4) * 2 + block % 2


def root_kernel(ids, own, other, root_own, root_other, *refs):
    msgs, refs = refs[0:4], refs[4:]
    dq_out, roots, keys, values, keys_t, root_rows, turned = refs
    x, y, c, z = ids[0], ids[1], ids[2], ids[3]
    first = c == 0

    def load(key_ref, value_ref):
        for ky in range(4):
            for block in range(8):
                to = place(y, ky, block)
                part = key_ref[ky, block]
                keys[to] = part
                keys_t[to] = part.astype(F4).T.astype(BF)
                values[to] = value_ref[ky, block]

    @pl.when(first)
    def _():
        load(own, other)

    @pl.when(c != 0)
    def _():
        load(other, own)

    keys[TREE_BLOCKS] = jnp.zeros((BLK, HD), BF)
    keys_t[TREE_BLOCKS] = jnp.zeros((BLK, HD), BF)
    values[TREE_BLOCKS] = jnp.zeros((BLK, HD), BF)

    rows_own = root_own[...].astype(F4)[:, 0:8, :].reshape(256, HD)
    rows_other = root_other[...].astype(F4)[:, 0:8, :].reshape(256, HD)
    key = jnp.where(first, rows_own, rows_other)
    value = jnp.where(first, rows_other, rows_own).astype(BF)
    key_t = key.T.astype(BF)
    key = key.astype(BF)
    dk = jnp.zeros((256, HD), F4)
    dv = jnp.zeros((256, HD), F4)
    root_rows[...] = jnp.zeros(root_rows.shape, F4)
    special = jnp.zeros((16, HD), F4)
    for i in range(8):
        msg, dc = msgs[i // 2], i % 2
        terms = unsplit(msg[dc, T0 : T0 + 48, :])
        special = special + terms
        tile = msg[dc, R0 : R0 + 16, :].astype(F4)
        root_rows[0, i * 4 : i * 4 + 4, :] = tile[0:4]
        root_rows[1, i * 4 : i * 4 + 4, :] = tile[4:8]
        query = msg[dc, Q0 : Q0 + 512, :]
        grad = msg[dc, D0 : D0 + 512, :]
        prob = jnp.exp2(nt(key, query) * SCALE2 - lanes_of(terms, 0))
        dscore = (prob * (nt(value, grad) - lanes_of(terms, 4))).astype(BF)
        dv = dv + nn(prob.astype(BF), grad)
        dk = dk + nn(dscore, query)
        dq_out[i] = nn(key_t, dscore)
    query = root_rows[0].astype(BF)
    grad = root_rows[1].astype(BF)
    lane, row = iota((256, HD), 1), iota((256, HD), 0)
    source = lane // 4
    source_x = lax.rem(x - source // 2 + 16, 4)
    source_c = jnp.where(source % 2 == 0, c, 1 - c)
    query_pos = z * 32 + source_x * 8 + y * 2 + source_c
    key_pos = lax.rem(z - row % 8 + 8, 8) * 32 + row // 8
    mask = (lane < 32) & (key_pos <= query_pos)
    prob = jnp.where(mask, jnp.exp2(nt(key, query) * SCALE2 - special[8:9, :]), 0.0)
    dscore = (prob * (nt(value, grad) - special[9:10, :])).astype(BF)
    dv = dv + nn(prob.astype(BF), grad)
    dk = dk + nn(dscore, query)
    dq_out[8, :, 0:BLK] = nn(key_t, dscore)
    turned[0] = dk.reshape(TREE_BLOCKS, 8, HD)
    turned[1] = dv.reshape(TREE_BLOCKS, 8, HD)
    for ky in range(4):
        for block in range(8):
            at = place(y, ky, block)
            for s in range(2):
                part = turned[s, at]
                for kz in range(8):
                    to = ky * 8 + block
                    roots[kz, s, to : to + 1, :] = part[kz : kz + 1]


def lanes_of(terms, start):
    return jnp.concatenate([terms[start + h : start + h + 1, :] for h in range(4)], axis=1)


def root_part(ids, own, other, root_own, root_other, msgs):
    blocks = jax.ShapeDtypeStruct((TREE_BLOCKS + 1, BLK, HD), BF)
    return pl.pallas_call(
        root_kernel,
        in_specs=[smem()] + [vmem()] * 8,
        out_specs=[vmem()] * 5,
        out_shape=[
            jax.ShapeDtypeStruct((9, HD, 512), F4),
            jax.ShapeDtypeStruct((8, 2, 32, HD), F4),
            blocks,
            blocks,
            blocks,
        ],
        scratch_shapes=[
            pltpu.VMEM((2, HD, HD), F4),
            pltpu.VMEM((2, TREE_BLOCKS, 8, HD), F4),
        ],
        compiler_params=params(),
        cost_estimate=pl.CostEstimate(
            flops=2 * 10**9, bytes_accessed=10**7, transcendentals=10**6
        ),
        name="root_part",
    )(ids, own, other, root_own, root_other, *msgs)


def tree_body(ids, lists, counts, kbit, qanc, keys, values, keys_t, dq_root, msgs, ks, outs,
              acc, dk, dv):
    x, y, c = ids[0], ids[1], ids[2]
    dk[...] = jnp.zeros(dk.shape, F4)
    dv[...] = jnp.zeros(dv.shape, F4)
    root_dq = dq_root[8, :, 0:BLK].T * FACTOR
    pad = jnp.zeros((12, HD), F4)
    base = iota((BLK, BLK), 0)
    for slot, k in enumerate(ks):
        msg, out = msgs[slot], outs[slot]
        for dc in range(2):
            tile = root_dq[8 * k + 4 * dc : 8 * k + 4 * dc + 4]
            out[dc, 512:528, :] = jnp.concatenate([tile, pad], axis=0).astype(BF)

        def query_block(dc, carry):
            i = k * 2 + dc
            mine = lax.rem(x - k + 4, 4) * 8 + y * 2 + jnp.where(dc == 0, c, 1 - c)
            anc_row = jnp.broadcast_to(qanc[pl.ds(mine, 1), :], (2 * BLK, BLK))
            query_pos = iota((2 * BLK, BLK), 1) + mine * BLK
            terms = unsplit(msg[dc, T0 : T0 + 48, :])
            acc[...] = dq_root[i]

            norm, delta = lanes_of(terms, 0), lanes_of(terms, 4)

            def unit(j):
                b0, b1 = lists[i, 2 * j], lists[i, 2 * j + 1]
                key = jnp.concatenate([keys[b0], keys[b1]], axis=0)
                value = jnp.concatenate([values[b0], values[b1]], axis=0)
                key_t = jnp.concatenate([keys_t[b0], keys_t[b1]], axis=1)
                bits = jnp.concatenate([kbit[b0], kbit[b1]], axis=0)
                key_pos = jnp.concatenate([base + b0 * BLK, base + b1 * BLK], axis=0)
                mask = ((bits & anc_row) != 0) & (key_pos <= query_pos)
                mask = jnp.concatenate([mask] * 4, axis=1)
                query = msg[dc, Q0 : Q0 + 512, :]
                grad = msg[dc, D0 : D0 + 512, :]
                prob = jnp.where(mask, jnp.exp2(nt(key, query) * SCALE2 - norm), 0.0)
                dscore = (prob * (nt(value, grad) - delta)).astype(BF)
                dv_part = nn(prob.astype(BF), grad)
                dk_part = nn(dscore, query)
                acc[...] = acc[...] + nn(key_t, dscore)
                dk[b0] = dk[b0] + dk_part[0:BLK]
                dv[b0] = dv[b0] + dv_part[0:BLK]
                dk[b1] = dk[b1] + dk_part[BLK:]
                dv[b1] = dv[b1] + dv_part[BLK:]

            def two(j, inner):
                unit(2 * j)
                unit(2 * j + 1)
                return inner

            count = counts[i]
            lax.fori_loop(0, count // 2, two, 0)

            @pl.when(count % 2 == 1)
            def _():
                unit(count - 1)

            for h in range(4):
                done = acc[:, h * BLK : (h + 1) * BLK].T * FACTOR
                out[dc, h * BLK : (h + 1) * BLK, :] = done.astype(BF)
            return carry

        lax.fori_loop(0, 2, query_block, 0)


def first_kernel(ids, lists, counts, kbit, qanc, keys, values, keys_t, dq_root, m0, m1,
                 o0, o1, dk, dv, acc):
    tree_body(ids, lists, counts, kbit, qanc, keys, values, keys_t, dq_root, (m0, m1), (1, 2),
              (o0, o1), acc, dk, dv)


def last_kernel(ids, lists, counts, kbit, qanc, keys, values, keys_t, dq_root, m0, m1, dk0, dv0,
                o0, o1, keep, send, acc, dk, dv):
    tree_body(ids, lists, counts, kbit, qanc, keys, values, keys_t, dq_root, (m0, m1), (3, 0),
              (o0, o1), acc, dk, dv)

    def store(dk_to, dv_to):
        for ky in range(4):
            for block in range(8):
                at = place(ids[1], ky, block)
                dk_to[ky * 8 + block] = dk[at] + dk0[at]
                dv_to[ky * 8 + block] = dv[at] + dv0[at]

    @pl.when(ids[2] == 0)
    def _():
        store(keep, send)

    @pl.when(ids[2] != 0)
    def _():
        store(send, keep)


def tree_part(kernel, name, shared, msgs, extra):
    part = jax.ShapeDtypeStruct((2, 528, HD), BF)
    sums = jax.ShapeDtypeStruct((TREE_BLOCKS + 1, BLK, HD), F4)
    scratch = pltpu.VMEM((TREE_BLOCKS + 1, BLK, HD), F4)
    final = jax.ShapeDtypeStruct((TREE_BLOCKS, BLK, HD), F4)
    last = len(extra) > 0
    return pl.pallas_call(
        kernel,
        in_specs=[smem()] * 3 + [vmem()] * (6 + len(msgs) + len(extra)),
        out_specs=[vmem()] * 4,
        out_shape=[part, part] + ([final, final] if last else [sums, sums]),
        scratch_shapes=[pltpu.VMEM((HD, 512), F4)] + ([scratch, scratch] if last else []),
        compiler_params=params(),
        cost_estimate=pl.CostEstimate(
            flops=5 * 10**9, bytes_accessed=16 * 10**6, transcendentals=4 * 10**6
        ),
        name=name,
    )(*shared, *msgs, *extra)


def unpack_query_kernel(ids, *refs):
    x, c = ids[0], ids[2]
    straight, crossed, out, root_out = refs[0:4], refs[4], refs[5], refs[6]
    for i in range(8):
        k, dc = i // 2, i % 2
        dest = lax.rem(x + k, 4) * 2 + flip(c, dc)
        part = crossed[k] if dc else straight[k][0]
        for h in range(4):
            cols = pl.ds(pl.multiple_of(dest * 512 + h * HD, HD), HD)
            out[:, cols] = part[h * BLK : (h + 1) * BLK, :].astype(F4)
        root_out[dest] = part[512:528, :].astype(F4)[0:4]


def unpack_query(ids, parts, crossed):
    return pl.pallas_call(
        unpack_query_kernel,
        in_specs=[smem()] + [vmem()] * 5,
        out_specs=[vmem()] * 2,
        out_shape=[
            jax.ShapeDtypeStruct((BLK, 4096), F4),
            jax.ShapeDtypeStruct((8, 4, HD), F4),
        ],
        compiler_params=params(),
        name="unpack_query",
    )(ids, *parts, crossed)


def join_cores_kernel(keep, other, root_keep, root_other, stay, *outs):
    rows = root_keep[...] + root_other[...]
    for block in range(TREE_BLOCKS):
        ky, at = block // 8, block % 8
        total = keep[block] + other[block]
        row = jnp.broadcast_to(rows[block : block + 1, :], (16, HD))
        tail = jnp.where(iota((16, HD), 0) == 0, row, 0.0)
        if ky == 0:
            stay[at, 0:BLK, :] = total
            stay[at, BLK:PAIR, :] = tail
        else:
            outs[ky - 1][at, 0:BLK, :] = total.astype(BF)
            outs[ky - 1][at, BLK:PAIR, :] = tail.astype(BF)


def join_cores(keep, other, root_keep, root_other):
    return pl.pallas_call(
        join_cores_kernel,
        in_specs=[vmem()] * 4,
        out_specs=[vmem()] * 4,
        out_shape=[jax.ShapeDtypeStruct((8, PAIR, HD), F4)]
        + [jax.ShapeDtypeStruct((8, PAIR, HD), BF)] * 3,
        compiler_params=params(),
        name="join_cores",
    )(keep, other, root_keep, root_other)


def sum_pairs_kernel(stay, r1, r2, r3, out):
    for block in range(8):
        rest = r1[block].astype(F4) + r2[block].astype(F4) + r3[block].astype(F4)
        out[block] = (stay[block] + rest)[0 : BLK + 8]


def sum_pairs(stay, received):
    return pl.pallas_call(
        sum_pairs_kernel,
        in_specs=[vmem()] * 4,
        out_specs=vmem(),
        out_shape=jax.ShapeDtypeStruct((8, BLK + 8, HD), F4),
        compiler_params=params(),
        name="sum_pairs",
    )(stay, *received)


def unpack_pairs_kernel(parts, out, root_out):
    for c in range(2):
        for x in range(4):
            total = parts[x * 2 + c]
            if c == 0:
                total = total * FACTOR
            cols = slice(c * 512 + x * HD, c * 512 + (x + 1) * HD)
            out[:, cols] = total[0:BLK]
            root_out[:, cols] = total[BLK : BLK + 1]


def unpack_pairs(parts):
    return pl.pallas_call(
        unpack_pairs_kernel,
        in_specs=[vmem()],
        out_specs=[vmem()] * 2,
        out_shape=[
            jax.ShapeDtypeStruct((BLK, 1024), F4),
            jax.ShapeDtypeStruct((1, 1024), F4),
        ],
        compiler_params=params(),
        name="unpack_pairs",
    )(parts)


def across(array):
    groups = [[x * 8 + y * 2 + c for x in range(4) for c in range(2)] for y in range(4)]
    return lax.all_to_all(array, "node", 0, 0, axis_index_groups=groups, tiled=True)


def shards(
    query_tree,
    output_tree,
    cotangent_tree,
    log_norm_tree,
    key_value_tree,
    query_root,
    output_root,
    cotangent_root,
    log_norm_root,
    key_value_root,
    parent,
    node_length,
):
    node = lax.axis_index("node")
    leaf = lax.axis_index("leaf")
    ids = jnp.stack([node // 8, node // 2 % 4, node % 2, leaf]).astype(jnp.int32)

    together = lax.optimization_barrier

    joined = across(pack_pairs(key_value_tree))
    root_rows = key_value_root
    for step in (1, 2, 4):
        root_rows = jnp.concatenate([root_rows, shift_leaf(root_rows, step)], axis=0)
    keep, send = pack_rows(
        ids,
        query_tree,
        output_tree,
        cotangent_tree,
        log_norm_tree,
        query_root,
        output_root,
        cotangent_root,
        log_norm_root.reshape(32),
    )
    merged = merge_rows(keep, shift(send, dc=1))
    joined, root_rows, *merged = together((joined, root_rows, *merged))

    msg1, msg3 = shift(merged[1], dx=1), shift(merged[3], dx=3)
    own = [joined] + [shift(joined, dy=ky) for ky in range(1, 4)]
    root_own = lax.all_to_all(pack_root(root_rows), "node", 0, 0, tiled=True)
    msg1, msg3, root_own, merged[2], *own = together((msg1, msg3, root_own, merged[2], *own))

    msgs = [merged[0], msg1, shift(merged[2], dx=2), msg3]
    own = jnp.stack(own, axis=0)
    other, root_other = shift(own, dc=1), shift(root_own, dc=1)
    kbit, qanc, lists, counts = make_tables(ids, parent, node_length)
    dq_root, roots, keys, values, keys_t = root_part(
        ids, own, other, root_own, root_other, msgs
    )
    shared = (ids, lists, counts, kbit, qanc, keys, values, keys_t, dq_root)

    part1, part2, dk0, dv0 = tree_part(first_kernel, "tree_first", shared, msgs[1:3], ())
    moved = [shift_leaf(roots[2 * a : 2 * a + 2], -2 * a) for a in range(1, 4)]
    part1, part2, dk0, dv0, *moved = together((part1, part2, dk0, dv0, *moved))

    roots = roots[0:2] + moved[0] + moved[1] + moved[2]
    root_far = shift_leaf(roots[1], -1)
    back1, back2 = shift(part1, dx=-1), shift(part2, dx=-2)
    part3, part0, keep, send = tree_part(
        last_kernel, "tree_last", shared, (msgs[3], msgs[0]), (dk0, dv0)
    )
    back1, back2, part3, part0, keep, send, root_far = together(
        (back1, back2, part3, part0, keep, send, root_far)
    )
    roots = roots[0] + root_far

    back3 = shift(part3, dx=-3)
    first = node % 2 == 0
    root_send = jnp.where(first, roots[1], roots[0])
    root_keep = jnp.where(first, roots[0], roots[1])
    stay, *low = join_cores(keep, shift(send, dc=1), root_keep, shift(root_send, dc=1))
    received = [shift(low[ky - 1], dy=-ky) for ky in range(1, 4)]
    back3, stay, *received = together((back3, stay, *received))
    grads = across(sum_pairs(stay, received))

    back = [part0, back1, back2, back3]
    crossed = shift(jnp.stack([part[1] for part in back], axis=0), dc=1)
    grad_pairs, grad_root = unpack_pairs(grads)
    grad_query, grad_query_root = unpack_query(ids, back, crossed)
    return grad_query, grad_query_root.reshape(1, 4096), grad_pairs, grad_root


def solution(mesh):
    rows = P(("leaf", "node"), None)
    lanes = P(None, ("leaf", "node"))
    tree = P("leaf", None)
    return jax.shard_map(
        shards,
        mesh=mesh,
        in_specs=(rows, rows, rows, lanes, rows, rows, rows, rows, lanes, rows, tree, tree),
        out_specs=(rows, rows, rows, rows),
        check_vma=False,
    )
```

```python
import math

import jax
import jax.numpy as jnp
from jax import lax
from jax.experimental import pallas as pl
from jax.experimental.pallas import tpu as pltpu
from jax.sharding import PartitionSpec as P

HD = 128
NODES = 24
BLK = 128
TREE_BLOCKS = 32
FACTOR = HD ** (-0.5)
LOG2E = math.log2(math.e)
SCALE2 = FACTOR * LOG2E
BF = jnp.bfloat16
F4 = jnp.float32
Q0, D0, R0, T0, MSG = 0, 512, 1024, 1040, 1088
PAIR = 144
VMEM_LIMIT = 24 * 1024 * 1024


def params(limit=VMEM_LIMIT):
    return pltpu.CompilerParams(vmem_limit_bytes=limit)


def perm(dx, dy, dc):
    pairs = []
    for x in range(4):
        for y in range(4):
            for c in range(2):
                target = ((x + dx) % 4) * 8 + ((y + dy) % 4) * 2 + (c ^ dc)
                pairs.append((x * 8 + y * 2 + c, target))
    return pairs


def shift(array, dx=0, dy=0, dc=0):
    return lax.ppermute(array, "node", perm(dx, dy, dc))


def shift_leaf(array, step):
    return lax.ppermute(array, "leaf", [(z, (z + step) % 8) for z in range(8)])


def nt(left, right):
    return lax.dot_general(left, right, (((1,), (1,)), ((), ())), preferred_element_type=F4)


def nn(left, right):
    return lax.dot_general(left, right, (((1,), (0,)), ((), ())), preferred_element_type=F4)


def iota(shape, dim):
    return lax.broadcasted_iota(jnp.int32, shape, dim)


def flip(c, dc):
    return c if dc == 0 else 1 - c


def smem():
    return pl.BlockSpec(memory_space=pltpu.SMEM)


def vmem():
    return pl.BlockSpec(memory_space=pltpu.VMEM)


def tables_kernel(ids, parent, length, kbit, qanc, lists, counts, start, anc, kmask, qmask):
    x, y, c = ids[0], ids[1], ids[2]
    for block in range(TREE_BLOCKS):
        kmask[block] = 0
        qmask[block] = 0
    total = jnp.int32(0)
    for n in range(NODES):
        start[n] = total
        bits = jnp.int32(1 << n)
        if n > 0:
            bits = bits | anc[parent[0, n]]
        anc[n] = bits
        first = total // BLK
        total = total + length[0, n]
        last = (total - 1) // BLK

        def mark(block, carry):
            kmask[block] = kmask[block] | jnp.int32(1 << n)
            qmask[block] = qmask[block] | bits
            return carry

        lax.fori_loop(first, last + 1, mark, 0)
    positions = iota((TREE_BLOCKS, BLK), 0) * BLK + iota((TREE_BLOCKS, BLK), 1)
    table = jnp.zeros((TREE_BLOCKS, BLK), jnp.int32)
    own_bits = jnp.zeros((TREE_BLOCKS, BLK), jnp.int32)
    for n in range(NODES):
        inside = positions >= start[n]
        table = jnp.where(inside, anc[n], table)
        own_bits = jnp.where(inside, jnp.int32(1 << n), own_bits)
    qanc[...] = table
    for block in range(TREE_BLOCKS):
        row = jnp.broadcast_to(own_bits[block : block + 1, :], (BLK, BLK))
        kbit[block] = row.T
    kbit[TREE_BLOCKS] = jnp.zeros((BLK, BLK), jnp.int32)
    for i in range(8):
        mine = (lax.rem(x - i // 2 + 4, 4)) * 8 + y * 2 + flip(c, i % 2)
        seen = qmask[mine]

        def scan(block, found):
            hit = (seen & kmask[block]) != 0
            lists[i, found] = block
            return found + hit.astype(jnp.int32)

        found = lax.fori_loop(0, mine + 1, scan, jnp.int32(0))
        lists[i, found] = TREE_BLOCKS
        counts[i] = (found + 1) // 2


def make_tables(ids, parent, length):
    return pl.pallas_call(
        tables_kernel,
        in_specs=[smem(), smem(), smem()],
        out_specs=[vmem(), vmem(), smem(), smem()],
        out_shape=[
            jax.ShapeDtypeStruct((TREE_BLOCKS + 1, BLK, BLK), jnp.int32),
            jax.ShapeDtypeStruct((TREE_BLOCKS, BLK), jnp.int32),
            jax.ShapeDtypeStruct((8, 40), jnp.int32),
            jax.ShapeDtypeStruct((8,), jnp.int32),
        ],
        scratch_shapes=[
            pltpu.SMEM((NODES,), jnp.int32),
            pltpu.SMEM((NODES,), jnp.int32),
            pltpu.SMEM((TREE_BLOCKS,), jnp.int32),
            pltpu.SMEM((TREE_BLOCKS,), jnp.int32),
        ],
        compiler_params=params(),
        cost_estimate=pl.CostEstimate(
            flops=10**6, bytes_accessed=4 * 10**6, transcendentals=0
        ),
        name="tables",
    )(ids, parent, length)


def pack_pairs_kernel(pairs, root, out):
    for c in range(2):
        for x in range(4):
            cols = slice(c * 512 + x * HD, c * 512 + (x + 1) * HD)
            out[x * 2 + c, 0:BLK, :] = pairs[:, cols]
            row = jnp.broadcast_to(root[:, cols].astype(F4), (16, HD))
            tail = jnp.where(iota((16, HD), 0) == 0, row, 0.0)
            out[x * 2 + c, BLK:PAIR, :] = tail.astype(BF)


def pack_pairs(pairs, root):
    return pl.pallas_call(
        pack_pairs_kernel,
        in_specs=[vmem()] * 2,
        out_specs=vmem(),
        out_shape=jax.ShapeDtypeStruct((8, PAIR, HD), BF),
        compiler_params=params(),
        name="pack_pairs",
    )(pairs, root)


def split3(value):
    high = value.astype(BF)
    rest = value - high.astype(F4)
    middle = rest.astype(BF)
    low = (rest - middle.astype(F4)).astype(BF)
    return jnp.concatenate([high, middle, low], axis=0)


def pack_rows_kernel(ids, *refs):
    sources, keep, send, held, sems = refs[0:8], refs[8], refs[9], refs[10:18], refs[18]
    copies = [
        pltpu.make_async_copy(source, target, sems.at[n])
        for n, (source, target) in enumerate(zip(sources, held))
    ]
    for copy in copies:
        copy.start()
    for copy in copies:
        copy.wait()
    query, output, cotangent, norm, rquery, routput, rcotangent, rnorm = held
    x, c = ids[0], ids[2]
    norms = rnorm[...] * LOG2E
    for i in range(8):
        k, dc = i // 2, i % 2
        dest = lax.rem(x + k, 4) * 2 + flip(c, dc)
        out = send if dc else keep
        deltas = []
        for h in range(4):
            cols = pl.ds(pl.multiple_of(dest * 512 + h * HD, HD), HD)
            out[k, Q0 + h * BLK : Q0 + (h + 1) * BLK, :] = query[:, cols]
            grad = cotangent[:, cols]
            out[k, D0 + h * BLK : D0 + (h + 1) * BLK, :] = grad
            product = grad.astype(F4) * output[:, cols].astype(F4)
            deltas.append(jnp.sum(product.T, axis=0, keepdims=True))
        lane = iota((1, HD), 1)
        rnorm_row = jnp.zeros((1, HD), F4)
        rdelta_row = jnp.zeros((1, HD), F4)
        rquery_rows, rgrad_rows = [], []
        for h in range(4):
            cols = pl.ds(pl.multiple_of(dest * 512 + h * HD, HD), HD)
            rgrad = rcotangent[:, cols].astype(F4)
            rquery_rows.append(rquery[:, cols].astype(F4))
            rgrad_rows.append(rgrad)
            rdelta = jnp.sum(rgrad * routput[:, cols].astype(F4), axis=1, keepdims=True)
            here = lane == i * 4 + h
            mine = jnp.where(iota((1, 32), 1) == dest * 4 + h, norms, 0.0)
            mine = jnp.broadcast_to(jnp.sum(mine, axis=1, keepdims=True), (1, HD))
            rnorm_row = jnp.where(here, mine, rnorm_row)
            rdelta_row = jnp.where(here, jnp.broadcast_to(rdelta, (1, HD)), rdelta_row)
        rows = jnp.concatenate(
            [norm[pl.ds(dest * 4, 4), :] * LOG2E]
            + deltas
            + [rnorm_row, rdelta_row, jnp.zeros((6, HD), F4)],
            axis=0,
        )
        out[k, T0 : T0 + 48, :] = split3(rows)
        tile = jnp.concatenate(rquery_rows + rgrad_rows + [jnp.zeros((8, HD), F4)], axis=0)
        out[k, R0 : R0 + 16, :] = tile.astype(BF)


def pack_rows(ids, query, output, cotangent, norm, rquery, routput, rcotangent, rnorm):
    return pl.pallas_call(
        pack_rows_kernel,
        in_specs=[smem()] + [pl.BlockSpec(memory_space=pl.ANY)] * 8,
        out_specs=[vmem()] * 2,
        out_shape=[jax.ShapeDtypeStruct((4, MSG, HD), BF)] * 2,
        scratch_shapes=[pltpu.VMEM((BLK, 4096), BF)] * 3
        + [pltpu.VMEM((32, BLK), F4)]
        + [pltpu.VMEM((1, 4096), BF)] * 3
        + [pltpu.VMEM((1, 32), F4), pltpu.SemaphoreType.DMA((8,))],
        compiler_params=params(60 * 1024 * 1024),
        name="pack_rows",
    )(ids, query, output, cotangent, norm, rquery, routput, rcotangent, rnorm)


def merge_rows_kernel(keep, other, *outs):
    for k in range(4):
        outs[k][0] = keep[k]
        outs[k][1] = other[k]


def merge_rows(keep, other):
    return pl.pallas_call(
        merge_rows_kernel,
        in_specs=[vmem()] * 2,
        out_specs=[vmem()] * 4,
        out_shape=[jax.ShapeDtypeStruct((2, MSG, HD), BF)] * 4,
        compiler_params=params(),
        name="merge_rows",
    )(keep, other)


def unsplit(rows):
    wide = rows.astype(F4)
    return wide[0:16] + wide[16:32] + wide[32:48]


def place(y, ky, block):
    return (block // 2) * 8 + lax.rem(y - ky + 4, 4) * 2 + block % 2


def root_kernel(ids, own, other, root_own, root_other, *refs):
    msgs, refs = refs[0:4], refs[4:]
    dq_out, roots, keys, values, keys_t, root_rows = refs
    x, y, c, z = ids[0], ids[1], ids[2], ids[3]
    first = c == 0

    def load(key_ref, value_ref):
        for ky in range(4):
            for block in range(8):
                to = place(y, ky, block)
                part = key_ref[ky, block, 0:BLK, :]
                keys[to] = part
                keys_t[to] = part.astype(F4).T.astype(BF)
                values[to] = value_ref[ky, block, 0:BLK, :]

    @pl.when(first)
    def _():
        load(own, other)

    @pl.when(c != 0)
    def _():
        load(other, own)

    keys[TREE_BLOCKS] = jnp.zeros((BLK, HD), BF)
    keys_t[TREE_BLOCKS] = jnp.zeros((BLK, HD), BF)
    values[TREE_BLOCKS] = jnp.zeros((BLK, HD), BF)

    rows_own = root_own[...].astype(F4)
    rows_other = root_other[...].astype(F4)
    key = jnp.where(first, rows_own, rows_other)
    value = jnp.where(first, rows_other, rows_own).astype(BF)
    key_t = key.T.astype(BF)
    key = key.astype(BF)
    dk = jnp.zeros((256, HD), F4)
    dv = jnp.zeros((256, HD), F4)
    root_rows[...] = jnp.zeros(root_rows.shape, F4)
    special = jnp.zeros((16, HD), F4)
    for i in range(8):
        msg, dc = msgs[i // 2], i % 2
        terms = unsplit(msg[dc, T0 : T0 + 48, :])
        special = special + terms
        tile = msg[dc, R0 : R0 + 16, :].astype(F4)
        root_rows[0, i * 4 : i * 4 + 4, :] = tile[0:4]
        root_rows[1, i * 4 : i * 4 + 4, :] = tile[4:8]
        query = msg[dc, Q0 : Q0 + 512, :]
        grad = msg[dc, D0 : D0 + 512, :]
        prob = jnp.exp2(nt(key, query) * SCALE2 - lanes_of(terms, 0))
        dscore = (prob * (nt(value, grad) - lanes_of(terms, 4))).astype(BF)
        dv = dv + nn(prob.astype(BF), grad)
        dk = dk + nn(dscore, query)
        dq_out[i] = nn(key_t, dscore)
    query = root_rows[0].astype(BF)
    grad = root_rows[1].astype(BF)
    lane, row = iota((256, HD), 1), iota((256, HD), 0)
    source = lane // 4
    source_x = lax.rem(x - source // 2 + 16, 4)
    source_c = jnp.where(source % 2 == 0, c, 1 - c)
    query_pos = z * 32 + source_x * 8 + y * 2 + source_c
    block = row % 8
    key_y = lax.rem(y - row % 32 // 8 + 4, 4)
    key_z = lax.rem(z - row // 32 + 8, 8)
    key_pos = key_z * 32 + (block // 2) * 8 + key_y * 2 + block % 2
    mask = (lane < 32) & (key_pos <= query_pos)
    prob = jnp.where(mask, jnp.exp2(nt(key, query) * SCALE2 - special[8:9, :]), 0.0)
    dscore = (prob * (nt(value, grad) - special[9:10, :])).astype(BF)
    dv = dv + nn(prob.astype(BF), grad)
    dk = dk + nn(dscore, query)
    dq_out[8, :, 0:BLK] = nn(key_t, dscore)
    for kz in range(8):
        to = lax.rem(z - kz + 8, 8)
        roots[to, 0] = dk[kz * 32 : kz * 32 + 32]
        roots[to, 1] = dv[kz * 32 : kz * 32 + 32]


def lanes_of(terms, start):
    return jnp.concatenate([terms[start + h : start + h + 1, :] for h in range(4)], axis=1)


def root_part(ids, own, other, root_own, root_other, msgs):
    blocks = jax.ShapeDtypeStruct((TREE_BLOCKS + 1, BLK, HD), BF)
    return pl.pallas_call(
        root_kernel,
        in_specs=[smem()] + [vmem()] * 8,
        out_specs=[vmem()] * 5,
        out_shape=[
            jax.ShapeDtypeStruct((9, HD, 512), F4),
            jax.ShapeDtypeStruct((8, 2, 32, HD), F4),
            blocks,
            blocks,
            blocks,
        ],
        scratch_shapes=[pltpu.VMEM((2, HD, HD), F4)],
        compiler_params=params(),
        cost_estimate=pl.CostEstimate(
            flops=2 * 10**9, bytes_accessed=10**7, transcendentals=10**6
        ),
        name="root_part",
    )(ids, own, other, root_own, root_other, *msgs)


def tree_body(ids, lists, counts, kbit, qanc, keys, values, keys_t, dq_root, msgs, ks, outs,
              acc, dk, dv):
    x, y, c = ids[0], ids[1], ids[2]
    dk[...] = jnp.zeros(dk.shape, F4)
    dv[...] = jnp.zeros(dv.shape, F4)
    root_dq = dq_root[8, :, 0:BLK].T * FACTOR
    pad = jnp.zeros((12, HD), F4)
    base = iota((BLK, BLK), 0)
    for slot, k in enumerate(ks):
        msg, out = msgs[slot], outs[slot]
        for dc in range(2):
            tile = root_dq[8 * k + 4 * dc : 8 * k + 4 * dc + 4]
            out[dc, 512:528, :] = jnp.concatenate([tile, pad], axis=0).astype(BF)

        def query_block(dc, carry):
            i = k * 2 + dc
            mine = lax.rem(x - k + 4, 4) * 8 + y * 2 + jnp.where(dc == 0, c, 1 - c)
            anc_row = jnp.broadcast_to(qanc[pl.ds(mine, 1), :], (2 * BLK, BLK))
            query_pos = iota((2 * BLK, BLK), 1) + mine * BLK
            terms = unsplit(msg[dc, T0 : T0 + 48, :])
            acc[...] = dq_root[i]

            norm, delta = lanes_of(terms, 0), lanes_of(terms, 4)

            def unit(j):
                b0, b1 = lists[i, 2 * j], lists[i, 2 * j + 1]
                key = jnp.concatenate([keys[b0], keys[b1]], axis=0)
                value = jnp.concatenate([values[b0], values[b1]], axis=0)
                key_t = jnp.concatenate([keys_t[b0], keys_t[b1]], axis=1)
                bits = jnp.concatenate([kbit[b0], kbit[b1]], axis=0)
                key_pos = jnp.concatenate([base + b0 * BLK, base + b1 * BLK], axis=0)
                mask = ((bits & anc_row) != 0) & (key_pos <= query_pos)
                mask = jnp.concatenate([mask] * 4, axis=1)
                query = msg[dc, Q0 : Q0 + 512, :]
                grad = msg[dc, D0 : D0 + 512, :]
                prob = jnp.where(mask, jnp.exp2(nt(key, query) * SCALE2 - norm), 0.0)
                dscore = (prob * (nt(value, grad) - delta)).astype(BF)
                dv_part = nn(prob.astype(BF), grad)
                dk_part = nn(dscore, query)
                acc[...] = acc[...] + nn(key_t, dscore)
                dk[b0] = dk[b0] + dk_part[0:BLK]
                dv[b0] = dv[b0] + dv_part[0:BLK]
                dk[b1] = dk[b1] + dk_part[BLK:]
                dv[b1] = dv[b1] + dv_part[BLK:]

            def two(j, inner):
                unit(2 * j)
                unit(2 * j + 1)
                return inner

            count = counts[i]
            lax.fori_loop(0, count // 2, two, 0)

            @pl.when(count % 2 == 1)
            def _():
                unit(count - 1)

            for h in range(4):
                done = acc[:, h * BLK : (h + 1) * BLK].T * FACTOR
                out[dc, h * BLK : (h + 1) * BLK, :] = done.astype(BF)
            return carry

        lax.fori_loop(0, 2, query_block, 0)


def first_kernel(ids, lists, counts, kbit, qanc, keys, values, keys_t, dq_root, m0, m1,
                 o0, o1, dk, dv, acc):
    tree_body(ids, lists, counts, kbit, qanc, keys, values, keys_t, dq_root, (m0, m1), (1, 2),
              (o0, o1), acc, dk, dv)


def last_kernel(ids, lists, counts, kbit, qanc, keys, values, keys_t, dq_root, m0, m1, dk0, dv0,
                o0, o1, keep, send, acc, dk, dv):
    tree_body(ids, lists, counts, kbit, qanc, keys, values, keys_t, dq_root, (m0, m1), (3, 0),
              (o0, o1), acc, dk, dv)

    def store(dk_to, dv_to):
        for ky in range(4):
            for block in range(8):
                at = place(ids[1], ky, block)
                dk_to[ky * 8 + block] = dk[at] + dk0[at]
                dv_to[ky * 8 + block] = dv[at] + dv0[at]

    @pl.when(ids[2] == 0)
    def _():
        store(keep, send)

    @pl.when(ids[2] != 0)
    def _():
        store(send, keep)


def tree_part(kernel, name, shared, msgs, extra):
    part = jax.ShapeDtypeStruct((2, 528, HD), BF)
    sums = jax.ShapeDtypeStruct((TREE_BLOCKS + 1, BLK, HD), F4)
    scratch = pltpu.VMEM((TREE_BLOCKS + 1, BLK, HD), F4)
    final = jax.ShapeDtypeStruct((TREE_BLOCKS, BLK, HD), F4)
    last = len(extra) > 0
    return pl.pallas_call(
        kernel,
        in_specs=[smem()] * 3 + [vmem()] * (6 + len(msgs) + len(extra)),
        out_specs=[vmem()] * 4,
        out_shape=[part, part] + ([final, final] if last else [sums, sums]),
        scratch_shapes=[pltpu.VMEM((HD, 512), F4)] + ([scratch, scratch] if last else []),
        compiler_params=params(),
        cost_estimate=pl.CostEstimate(
            flops=5 * 10**9, bytes_accessed=16 * 10**6, transcendentals=4 * 10**6
        ),
        name=name,
    )(*shared, *msgs, *extra)


def unpack_query_kernel(ids, *refs):
    x, c = ids[0], ids[2]
    straight, crossed, out, root_out = refs[0:4], refs[4], refs[5], refs[6]
    for i in range(8):
        k, dc = i // 2, i % 2
        dest = lax.rem(x + k, 4) * 2 + flip(c, dc)
        part = crossed[k] if dc else straight[k][0]
        for h in range(4):
            cols = pl.ds(pl.multiple_of(dest * 512 + h * HD, HD), HD)
            out[:, cols] = part[h * BLK : (h + 1) * BLK, :].astype(F4)
        root_out[dest] = part[512:528, :].astype(F4)[0:4]


def unpack_query(ids, parts, crossed):
    return pl.pallas_call(
        unpack_query_kernel,
        in_specs=[smem()] + [vmem()] * 5,
        out_specs=[vmem()] * 2,
        out_shape=[
            jax.ShapeDtypeStruct((BLK, 4096), F4),
            jax.ShapeDtypeStruct((8, 4, HD), F4),
        ],
        compiler_params=params(),
        name="unpack_query",
    )(ids, *parts, crossed)


def join_cores_kernel(keep, other, root_keep, root_other, stay, *outs):
    rows = root_keep[...] + root_other[...]
    for block in range(TREE_BLOCKS):
        ky, at = block // 8, block % 8
        total = keep[block] + other[block]
        row = jnp.broadcast_to(rows[block : block + 1, :], (16, HD))
        tail = jnp.where(iota((16, HD), 0) == 0, row, 0.0)
        if ky == 0:
            stay[at, 0:BLK, :] = total
            stay[at, BLK:PAIR, :] = tail
        else:
            outs[ky - 1][at, 0:BLK, :] = total.astype(BF)
            outs[ky - 1][at, BLK:PAIR, :] = tail.astype(BF)


def join_cores(keep, other, root_keep, root_other):
    return pl.pallas_call(
        join_cores_kernel,
        in_specs=[vmem()] * 4,
        out_specs=[vmem()] * 4,
        out_shape=[jax.ShapeDtypeStruct((8, PAIR, HD), F4)]
        + [jax.ShapeDtypeStruct((8, PAIR, HD), BF)] * 3,
        compiler_params=params(),
        name="join_cores",
    )(keep, other, root_keep, root_other)


def sum_pairs_kernel(stay, r1, r2, r3, out):
    for block in range(8):
        rest = r1[block].astype(F4) + r2[block].astype(F4) + r3[block].astype(F4)
        out[block] = (stay[block] + rest)[0 : BLK + 8]


def sum_pairs(stay, received):
    return pl.pallas_call(
        sum_pairs_kernel,
        in_specs=[vmem()] * 4,
        out_specs=vmem(),
        out_shape=jax.ShapeDtypeStruct((8, BLK + 8, HD), F4),
        compiler_params=params(),
        name="sum_pairs",
    )(stay, *received)


def unpack_pairs_kernel(parts, out, root_out):
    for c in range(2):
        for x in range(4):
            total = parts[x * 2 + c]
            if c == 0:
                total = total * FACTOR
            cols = slice(c * 512 + x * HD, c * 512 + (x + 1) * HD)
            out[:, cols] = total[0:BLK]
            root_out[:, cols] = total[BLK : BLK + 1]


def unpack_pairs(parts):
    return pl.pallas_call(
        unpack_pairs_kernel,
        in_specs=[vmem()],
        out_specs=[vmem()] * 2,
        out_shape=[
            jax.ShapeDtypeStruct((BLK, 1024), F4),
            jax.ShapeDtypeStruct((1, 1024), F4),
        ],
        compiler_params=params(),
        name="unpack_pairs",
    )(parts)


def across(array):
    groups = [[x * 8 + y * 2 + c for x in range(4) for c in range(2)] for y in range(4)]
    return lax.all_to_all(array, "node", 0, 0, axis_index_groups=groups, tiled=True)


def shards(
    query_tree,
    output_tree,
    cotangent_tree,
    log_norm_tree,
    key_value_tree,
    query_root,
    output_root,
    cotangent_root,
    log_norm_root,
    key_value_root,
    parent,
    node_length,
):
    node = lax.axis_index("node")
    leaf = lax.axis_index("leaf")
    ids = jnp.stack([node // 8, node // 2 % 4, node % 2, leaf]).astype(jnp.int32)

    together = lax.optimization_barrier

    joined = across(pack_pairs(key_value_tree, key_value_root))
    joined, ids = together((joined, ids))
    keep, send = pack_rows(
        ids,
        query_tree,
        output_tree,
        cotangent_tree,
        log_norm_tree,
        query_root,
        output_root,
        cotangent_root,
        log_norm_root.reshape(1, 32),
    )
    merged = merge_rows(keep, shift(send, dc=1))
    joined, *merged = together((joined, *merged))

    msg1, msg3 = shift(merged[1], dx=1), shift(merged[3], dx=3)
    own = [joined] + [shift(joined, dy=ky) for ky in range(1, 4)]
    msg1, msg3, merged[2], *own = together((msg1, msg3, merged[2], *own))

    msgs = [merged[0], msg1, shift(merged[2], dx=2), msg3]
    own = jnp.stack(own, axis=0)
    root_own = own[:, :, BLK, :].reshape(TREE_BLOCKS, HD)
    for step in (1, 2, 4):
        root_own = jnp.concatenate([root_own, shift_leaf(root_own, step)], axis=0)
    other, root_other = shift(own, dc=1), shift(root_own, dc=1)
    kbit, qanc, lists, counts = make_tables(ids, parent, node_length)
    dq_root, roots, keys, values, keys_t = root_part(
        ids, own, other, root_own, root_other, msgs
    )
    shared = (ids, lists, counts, kbit, qanc, keys, values, keys_t, dq_root)

    part1, part2, dk0, dv0 = tree_part(first_kernel, "tree_first", shared, msgs[1:3], ())
    roots = lax.all_to_all(roots, "leaf", 0, 0, tiled=True)
    part1, part2, dk0, dv0, roots = together((part1, part2, dk0, dv0, roots))

    back1, back2 = shift(part1, dx=-1), shift(part2, dx=-2)
    part3, part0, keep, send = tree_part(
        last_kernel, "tree_last", shared, (msgs[3], msgs[0]), (dk0, dv0)
    )
    first = node % 2 == 0
    roots = jnp.sum(roots, axis=0)
    root_send = jnp.where(first, roots[1], roots[0])
    root_keep = jnp.where(first, roots[0], roots[1])
    root_other = shift(root_send, dc=1)
    back1, back2, part3, part0, keep, send, root_keep, root_other = together(
        (back1, back2, part3, part0, keep, send, root_keep, root_other)
    )

    back3 = shift(part3, dx=-3)
    stay, *low = join_cores(keep, shift(send, dc=1), root_keep, root_other)
    received = [shift(low[ky - 1], dy=-ky) for ky in range(1, 4)]
    back3, stay, *received = together((back3, stay, *received))
    grads = across(sum_pairs(stay, received))

    back = [part0, back1, back2, back3]
    crossed = shift(jnp.stack([part[1] for part in back], axis=0), dc=1)
    grad_pairs, grad_root = unpack_pairs(grads)
    grad_query, grad_query_root = unpack_query(ids, back, crossed)
    return grad_query, grad_query_root.reshape(1, 4096), grad_pairs, grad_root


def solution(mesh):
    rows = P(("leaf", "node"), None)
    lanes = P(None, ("leaf", "node"))
    tree = P("leaf", None)
    return jax.shard_map(
        shards,
        mesh=mesh,
        in_specs=(rows, rows, rows, lanes, rows, rows, rows, rows, lanes, rows, tree, tree),
        out_specs=(rows, rows, rows, rows),
        check_vma=False,
    )
```

```python
import math

import jax
import jax.numpy as jnp
from jax import lax
from jax.experimental import pallas as pl
from jax.experimental.pallas import tpu as pltpu
from jax.sharding import Mesh
from jax.sharding import PartitionSpec as P

HD = 128
NODES = 24
BLK = 128
TREE_BLOCKS = 32
FACTOR = HD ** (-0.5)
LOG2E = math.log2(math.e)
SCALE2 = FACTOR * LOG2E
BF = jnp.bfloat16
F4 = jnp.float32
Q0, D0, R0, T0, MSG = 0, 512, 1024, 1040, 1088
PAIR = 144
VMEM_LIMIT = 24 * 1024 * 1024


def params(limit=VMEM_LIMIT):
    return pltpu.CompilerParams(vmem_limit_bytes=limit)


def perm(dx, dy, dc):
    pairs = []
    for x in range(4):
        for y in range(4):
            for c in range(2):
                target = ((x + dx) % 4) * 8 + ((y + dy) % 4) * 2 + (c ^ dc)
                pairs.append((x * 8 + y * 2 + c, target))
    return pairs


def shift(array, dx=0, dy=0, dc=0):
    return lax.ppermute(array, ("x", "y", "core"), perm(dx, dy, dc))


def nt(left, right):
    return lax.dot_general(left, right, (((1,), (1,)), ((), ())), preferred_element_type=F4)


def nn(left, right):
    return lax.dot_general(left, right, (((1,), (0,)), ((), ())), preferred_element_type=F4)


def iota(shape, dim):
    return lax.broadcasted_iota(jnp.int32, shape, dim)


def flip(c, dc):
    return c if dc == 0 else 1 - c


def smem():
    return pl.BlockSpec(memory_space=pltpu.SMEM)


def vmem():
    return pl.BlockSpec(memory_space=pltpu.VMEM)


def tables_kernel(ids, parent, length, kbit, qanc, lists, counts, start, anc, kmask, qmask):
    x, y, c = ids[0], ids[1], ids[2]
    for block in range(TREE_BLOCKS):
        kmask[block] = 0
        qmask[block] = 0
    total = jnp.int32(0)
    for n in range(NODES):
        start[n] = total
        bits = jnp.int32(1 << n)
        if n > 0:
            bits = bits | anc[parent[0, n]]
        anc[n] = bits
        first = total // BLK
        total = total + length[0, n]
        last = (total - 1) // BLK

        def mark(block, carry):
            kmask[block] = kmask[block] | jnp.int32(1 << n)
            qmask[block] = qmask[block] | bits
            return carry

        lax.fori_loop(first, last + 1, mark, 0)
    positions = iota((TREE_BLOCKS, BLK), 0) * BLK + iota((TREE_BLOCKS, BLK), 1)
    table = jnp.zeros((TREE_BLOCKS, BLK), jnp.int32)
    own_bits = jnp.zeros((TREE_BLOCKS, BLK), jnp.int32)
    for n in range(NODES):
        inside = positions >= start[n]
        table = jnp.where(inside, anc[n], table)
        own_bits = jnp.where(inside, jnp.int32(1 << n), own_bits)
    qanc[...] = table
    for block in range(TREE_BLOCKS):
        row = jnp.broadcast_to(own_bits[block : block + 1, :], (BLK, BLK))
        kbit[block] = row.T
    kbit[TREE_BLOCKS] = jnp.zeros((BLK, BLK), jnp.int32)
    for i in range(8):
        mine = (lax.rem(x - i // 2 + 4, 4)) * 8 + y * 2 + flip(c, i % 2)
        seen = qmask[mine]

        def scan(block, found):
            hit = (seen & kmask[block]) != 0
            lists[i, found] = block
            return found + hit.astype(jnp.int32)

        found = lax.fori_loop(0, mine + 1, scan, jnp.int32(0))
        lists[i, found] = TREE_BLOCKS
        counts[i] = (found + 1) // 2


def make_tables(ids, parent, length):
    return pl.pallas_call(
        tables_kernel,
        in_specs=[smem(), smem(), smem()],
        out_specs=[vmem(), vmem(), smem(), smem()],
        out_shape=[
            jax.ShapeDtypeStruct((TREE_BLOCKS + 1, BLK, BLK), jnp.int32),
            jax.ShapeDtypeStruct((TREE_BLOCKS, BLK), jnp.int32),
            jax.ShapeDtypeStruct((8, 40), jnp.int32),
            jax.ShapeDtypeStruct((8,), jnp.int32),
        ],
        scratch_shapes=[
            pltpu.SMEM((NODES,), jnp.int32),
            pltpu.SMEM((NODES,), jnp.int32),
            pltpu.SMEM((TREE_BLOCKS,), jnp.int32),
            pltpu.SMEM((TREE_BLOCKS,), jnp.int32),
        ],
        compiler_params=params(),
        cost_estimate=pl.CostEstimate(
            flops=10**6, bytes_accessed=4 * 10**6, transcendentals=0
        ),
        name="tables",
    )(ids, parent, length)


def pack_pairs_kernel(pairs, root, out):
    for c in range(2):
        for x in range(4):
            cols = slice(c * 512 + x * HD, c * 512 + (x + 1) * HD)
            out[x * 2 + c, 0:BLK, :] = pairs[:, cols]
            row = jnp.broadcast_to(root[:, cols].astype(F4), (16, HD))
            tail = jnp.where(iota((16, HD), 0) == 0, row, 0.0)
            out[x * 2 + c, BLK:PAIR, :] = tail.astype(BF)


def pack_pairs(pairs, root):
    return pl.pallas_call(
        pack_pairs_kernel,
        in_specs=[vmem()] * 2,
        out_specs=vmem(),
        out_shape=jax.ShapeDtypeStruct((8, PAIR, HD), BF),
        compiler_params=params(),
        name="pack_pairs",
    )(pairs, root)


def split3(value):
    high = value.astype(BF)
    rest = value - high.astype(F4)
    middle = rest.astype(BF)
    low = (rest - middle.astype(F4)).astype(BF)
    return jnp.concatenate([high, middle, low], axis=0)


def pack_rows_kernel(ids, *refs):
    sources, keep, send, held, sems = refs[0:8], refs[8], refs[9], refs[10:18], refs[18]
    copies = [
        pltpu.make_async_copy(source, target, sems.at[n])
        for n, (source, target) in enumerate(zip(sources, held))
    ]
    for copy in copies:
        copy.start()
    for copy in copies:
        copy.wait()
    query, output, cotangent, norm, rquery, routput, rcotangent, rnorm = held
    x, c = ids[0], ids[2]
    norms = rnorm[...] * LOG2E
    for i in range(8):
        k, dc = i // 2, i % 2
        dest = lax.rem(x + k, 4) * 2 + flip(c, dc)
        out = send if dc else keep
        deltas = []
        for h in range(4):
            cols = pl.ds(pl.multiple_of(dest * 512 + h * HD, HD), HD)
            out[k, Q0 + h * BLK : Q0 + (h + 1) * BLK, :] = query[:, cols]
            grad = cotangent[:, cols]
            out[k, D0 + h * BLK : D0 + (h + 1) * BLK, :] = grad
            product = grad.astype(F4) * output[:, cols].astype(F4)
            deltas.append(jnp.sum(product.T, axis=0, keepdims=True))
        lane = iota((1, HD), 1)
        rnorm_row = jnp.zeros((1, HD), F4)
        rdelta_row = jnp.zeros((1, HD), F4)
        rquery_rows, rgrad_rows = [], []
        for h in range(4):
            cols = pl.ds(pl.multiple_of(dest * 512 + h * HD, HD), HD)
            rgrad = rcotangent[:, cols].astype(F4)
            rquery_rows.append(rquery[:, cols].astype(F4))
            rgrad_rows.append(rgrad)
            rdelta = jnp.sum(rgrad * routput[:, cols].astype(F4), axis=1, keepdims=True)
            here = lane == i * 4 + h
            mine = jnp.where(iota((1, 32), 1) == dest * 4 + h, norms, 0.0)
            mine = jnp.broadcast_to(jnp.sum(mine, axis=1, keepdims=True), (1, HD))
            rnorm_row = jnp.where(here, mine, rnorm_row)
            rdelta_row = jnp.where(here, jnp.broadcast_to(rdelta, (1, HD)), rdelta_row)
        rows = jnp.concatenate(
            [norm[pl.ds(dest * 4, 4), :] * LOG2E]
            + deltas
            + [rnorm_row, rdelta_row, jnp.zeros((6, HD), F4)],
            axis=0,
        )
        out[k, T0 : T0 + 48, :] = split3(rows)
        tile = jnp.concatenate(rquery_rows + rgrad_rows + [jnp.zeros((8, HD), F4)], axis=0)
        out[k, R0 : R0 + 16, :] = tile.astype(BF)


def pack_rows(ids, query, output, cotangent, norm, rquery, routput, rcotangent, rnorm):
    return pl.pallas_call(
        pack_rows_kernel,
        in_specs=[smem()] + [pl.BlockSpec(memory_space=pl.ANY)] * 8,
        out_specs=[vmem()] * 2,
        out_shape=[jax.ShapeDtypeStruct((4, MSG, HD), BF)] * 2,
        scratch_shapes=[pltpu.VMEM((BLK, 4096), BF)] * 3
        + [pltpu.VMEM((32, BLK), F4)]
        + [pltpu.VMEM((1, 4096), BF)] * 3
        + [pltpu.VMEM((1, 32), F4), pltpu.SemaphoreType.DMA((8,))],
        compiler_params=params(60 * 1024 * 1024),
        name="pack_rows",
    )(ids, query, output, cotangent, norm, rquery, routput, rcotangent, rnorm)


def merge_rows_kernel(keep, other, *outs):
    for k in range(4):
        outs[k][0] = keep[k]
        outs[k][1] = other[k]


def merge_rows(keep, other):
    return pl.pallas_call(
        merge_rows_kernel,
        in_specs=[vmem()] * 2,
        out_specs=[vmem()] * 4,
        out_shape=[jax.ShapeDtypeStruct((2, MSG, HD), BF)] * 4,
        compiler_params=params(),
        name="merge_rows",
    )(keep, other)


def unsplit(rows):
    wide = rows.astype(F4)
    return wide[0:16] + wide[16:32] + wide[32:48]


def pack_root_kernel(joined, out):
    tile = jnp.zeros((16, HD), F4)
    for block in range(8):
        row = joined[block, BLK:PAIR, :].astype(F4)[0:1]
        tile = jnp.where(iota((16, HD), 0) == block, jnp.broadcast_to(row, (16, HD)), tile)
    for target in range(32):
        out[target] = tile.astype(BF)


def pack_root(joined):
    return pl.pallas_call(
        pack_root_kernel,
        in_specs=[vmem()],
        out_specs=vmem(),
        out_shape=jax.ShapeDtypeStruct((32, 16, HD), BF),
        compiler_params=params(),
        name="pack_root",
    )(joined)


def place(y, ky, block):
    return (block // 2) * 8 + lax.rem(y - ky + 4, 4) * 2 + block % 2


def lanes_of(terms, start):
    return jnp.concatenate([terms[start + h : start + h + 1, :] for h in range(4)], axis=1)


def compute_kernel(ids, lists, counts, kbit, qanc, own, other, root_own, root_other, *refs):
    msgs, outs, refs = refs[0:4], refs[4:8], refs[8:]
    keep, send, root_keep, root_send, refs = *refs[0:4], refs[4:]
    keys, values, keys_t, root_rows, acc, dk, dv, rkey, rvalue, rkey_t, rdk, rdv = refs
    x, y, c, z = ids[0], ids[1], ids[2], ids[3]
    first = c == 0

    def load(key_ref, value_ref):
        for ky in range(4):
            for block in range(8):
                to = place(y, ky, block)
                part = key_ref[ky, block, 0:BLK, :]
                keys[to] = part
                keys_t[to] = part.astype(F4).T.astype(BF)
                values[to] = value_ref[ky, block, 0:BLK, :]

    @pl.when(first)
    def _():
        load(own, other)

    @pl.when(c != 0)
    def _():
        load(other, own)

    keys[TREE_BLOCKS] = jnp.zeros((BLK, HD), BF)
    keys_t[TREE_BLOCKS] = jnp.zeros((BLK, HD), BF)
    values[TREE_BLOCKS] = jnp.zeros((BLK, HD), BF)
    dk[...] = jnp.zeros(dk.shape, F4)
    dv[...] = jnp.zeros(dv.shape, F4)

    rows_own = root_own[...].astype(F4)[:, 0:8, :].reshape(256, HD)
    rows_other = root_other[...].astype(F4)[:, 0:8, :].reshape(256, HD)
    key_wide = jnp.where(first, rows_own, rows_other)
    rvalue[...] = jnp.where(first, rows_other, rows_own).astype(BF)
    rkey_t[...] = key_wide.T.astype(BF)
    rkey[...] = key_wide.astype(BF)

    root_rows[...] = jnp.zeros(root_rows.shape, F4)
    special = jnp.zeros((16, HD), F4)
    for i in range(8):
        msg, dc = msgs[i // 2], i % 2
        special = special + unsplit(msg[dc, T0 : T0 + 48, :])
        tile = msg[dc, R0 : R0 + 16, :].astype(F4)
        root_rows[0, i * 4 : i * 4 + 4, :] = tile[0:4]
        root_rows[1, i * 4 : i * 4 + 4, :] = tile[4:8]
    query = root_rows[0].astype(BF)
    grad = root_rows[1].astype(BF)
    lane, row = iota((256, HD), 1), iota((256, HD), 0)
    source = lane // 4
    source_x = lax.rem(x - source // 2 + 16, 4)
    source_c = jnp.where(source % 2 == 0, c, 1 - c)
    root_query_pos = z * 32 + source_x * 8 + y * 2 + source_c
    at = row // 8
    root_key_pos = (at // 4) * 32 + (row % 8 // 2) * 8 + (at % 4) * 2 + row % 2
    mask = (lane < 32) & (root_key_pos <= root_query_pos)
    prob = jnp.where(mask, jnp.exp2(nt(rkey[...], query) * SCALE2 - special[8:9, :]), 0.0)
    dscore = (prob * (nt(rvalue[...], grad) - special[9:10, :])).astype(BF)
    rdv[...] = nn(prob.astype(BF), grad)
    rdk[...] = nn(dscore, query)
    root_dq = nn(rkey_t[...], dscore).T * FACTOR

    pad = jnp.zeros((12, HD), F4)
    base = iota((BLK, BLK), 0)
    for k in range(4):
        msg, out = msgs[k], outs[k]
        for dc in range(2):
            tile = root_dq[8 * k + 4 * dc : 8 * k + 4 * dc + 4]
            out[dc, 512:528, :] = jnp.concatenate([tile, pad], axis=0).astype(BF)

        def query_block(dc, carry):
            i = k * 2 + dc
            mine = lax.rem(x - k + 4, 4) * 8 + y * 2 + jnp.where(dc == 0, c, 1 - c)
            anc_row = jnp.broadcast_to(qanc[pl.ds(mine, 1), :], (2 * BLK, BLK))
            query_pos = iota((2 * BLK, BLK), 1) + mine * BLK
            terms = unsplit(msg[dc, T0 : T0 + 48, :])
            norm, delta = lanes_of(terms, 0), lanes_of(terms, 4)

            def gradients(key, value, key_t, mask):
                query = msg[dc, Q0 : Q0 + 512, :]
                grad = msg[dc, D0 : D0 + 512, :]
                prob = jnp.exp2(nt(key, query) * SCALE2 - norm)
                if mask is not None:
                    prob = jnp.where(jnp.concatenate([mask] * 4, axis=1), prob, 0.0)
                dscore = (prob * (nt(value, grad) - delta)).astype(BF)
                return nn(dscore, query), nn(prob.astype(BF), grad), nn(key_t, dscore)

            dk_part, dv_part, dq_part = gradients(rkey[...], rvalue[...], rkey_t[...], None)
            rdk[...] = rdk[...] + dk_part
            rdv[...] = rdv[...] + dv_part
            acc[...] = dq_part

            def unit(j):
                b0, b1 = lists[i, 2 * j], lists[i, 2 * j + 1]
                key = jnp.concatenate([keys[b0], keys[b1]], axis=0)
                value = jnp.concatenate([values[b0], values[b1]], axis=0)
                key_t = jnp.concatenate([keys_t[b0], keys_t[b1]], axis=1)
                bits = jnp.concatenate([kbit[b0], kbit[b1]], axis=0)
                key_pos = jnp.concatenate([base + b0 * BLK, base + b1 * BLK], axis=0)
                mask = ((bits & anc_row) != 0) & (key_pos <= query_pos)
                dk_part, dv_part, dq_part = gradients(key, value, key_t, mask)
                acc[...] = acc[...] + dq_part
                dk[b0] = dk[b0] + dk_part[0:BLK]
                dv[b0] = dv[b0] + dv_part[0:BLK]
                dk[b1] = dk[b1] + dk_part[BLK:]
                dv[b1] = dv[b1] + dv_part[BLK:]

            def two(j, inner):
                unit(2 * j)
                unit(2 * j + 1)
                return inner

            count = counts[i]
            lax.fori_loop(0, count // 2, two, 0)

            @pl.when(count % 2 == 1)
            def _():
                unit(count - 1)

            for h in range(4):
                done = acc[:, h * BLK : (h + 1) * BLK].T * FACTOR
                out[dc, h * BLK : (h + 1) * BLK, :] = done.astype(BF)
            return carry

        lax.fori_loop(0, 2, query_block, 0)

    def store(keep_from, send_from, root_keep_from, root_send_from):
        for ky in range(4):
            for block in range(8):
                at = place(y, ky, block)
                keep[ky * 8 + block] = keep_from[at]
                send[ky * 8 + block] = send_from[at].astype(BF)
        root_keep[...] = root_keep_from[...].reshape(32, 8, HD)
        root_send[...] = root_send_from[...].reshape(32, 8, HD)

    @pl.when(first)
    def _():
        store(dk, dv, rdk, rdv)

    @pl.when(c != 0)
    def _():
        store(dv, dk, rdv, rdk)


def compute(ids, lists, counts, kbit, qanc, own, other, root_own, root_other, msgs):
    half = (TREE_BLOCKS, BLK, HD)
    blocks = pltpu.VMEM((TREE_BLOCKS + 1, BLK, HD), BF)
    sums = pltpu.VMEM((TREE_BLOCKS + 1, BLK, HD), F4)
    return pl.pallas_call(
        compute_kernel,
        in_specs=[smem()] * 3 + [vmem()] * 10,
        out_specs=[vmem()] * 8,
        out_shape=[jax.ShapeDtypeStruct((2, 528, HD), BF)] * 4
        + [jax.ShapeDtypeStruct(half, F4), jax.ShapeDtypeStruct(half, BF)]
        + [jax.ShapeDtypeStruct((32, 8, HD), F4)] * 2,
        scratch_shapes=[
            blocks,
            blocks,
            blocks,
            pltpu.VMEM((2, HD, HD), F4),
            pltpu.VMEM((HD, 512), F4),
            sums,
            sums,
            pltpu.VMEM((256, HD), BF),
            pltpu.VMEM((256, HD), BF),
            pltpu.VMEM((HD, 256), BF),
            pltpu.VMEM((256, HD), F4),
            pltpu.VMEM((256, HD), F4),
        ],
        compiler_params=params(32 * 1024 * 1024),
        cost_estimate=pl.CostEstimate(
            flops=10**10, bytes_accessed=16 * 10**6, transcendentals=8 * 10**6
        ),
        name="compute",
    )(ids, lists, counts, kbit, qanc, own, other, root_own, root_other, *msgs)


def unpack_query_kernel(ids, *refs):
    x, c = ids[0], ids[2]
    straight, crossed, out, root_out = refs[0:4], refs[4], refs[5], refs[6]
    for i in range(8):
        k, dc = i // 2, i % 2
        dest = lax.rem(x + k, 4) * 2 + flip(c, dc)
        part = crossed[k] if dc else straight[k][0]
        for h in range(4):
            cols = pl.ds(pl.multiple_of(dest * 512 + h * HD, HD), HD)
            out[:, cols] = part[h * BLK : (h + 1) * BLK, :].astype(F4)
        root_out[dest] = part[512:528, :].astype(F4)[0:4]


def unpack_query(ids, parts, crossed):
    return pl.pallas_call(
        unpack_query_kernel,
        in_specs=[smem()] + [vmem()] * 5,
        out_specs=[vmem()] * 2,
        out_shape=[
            jax.ShapeDtypeStruct((BLK, 4096), F4),
            jax.ShapeDtypeStruct((8, 4, HD), F4),
        ],
        compiler_params=params(),
        name="unpack_query",
    )(ids, *parts, crossed)


def join_cores_kernel(keep, other, stay, *outs):
    for block in range(TREE_BLOCKS):
        ky, at = block // 8, block % 8
        total = keep[block] + other[block].astype(F4)
        if ky == 0:
            stay[at] = total
        else:
            outs[ky - 1][at] = total.astype(BF)


def join_cores(keep, other):
    return pl.pallas_call(
        join_cores_kernel,
        in_specs=[vmem()] * 2,
        out_specs=[vmem()] * 4,
        out_shape=[jax.ShapeDtypeStruct((8, BLK, HD), F4)]
        + [jax.ShapeDtypeStruct((8, BLK, HD), BF)] * 3,
        compiler_params=params(),
        name="join_cores",
    )(keep, other)


def sum_pairs_kernel(stay, r1, r2, r3, roots, out):
    total = roots[0]
    for n in range(1, 32):
        total = total + roots[n]
    for block in range(8):
        rest = r1[block].astype(F4) + r2[block].astype(F4) + r3[block].astype(F4)
        out[block, 0:BLK, :] = stay[block] + rest
        out[block, BLK : BLK + 8, :] = jnp.broadcast_to(total[block : block + 1], (8, HD))


def sum_pairs(stay, received, roots):
    return pl.pallas_call(
        sum_pairs_kernel,
        in_specs=[vmem()] * 5,
        out_specs=vmem(),
        out_shape=jax.ShapeDtypeStruct((8, BLK + 8, HD), F4),
        compiler_params=params(),
        name="sum_pairs",
    )(stay, *received, roots)


def unpack_pairs_kernel(parts, out, root_out):
    for c in range(2):
        for x in range(4):
            total = parts[x * 2 + c]
            if c == 0:
                total = total * FACTOR
            cols = slice(c * 512 + x * HD, c * 512 + (x + 1) * HD)
            out[:, cols] = total[0:BLK]
            root_out[:, cols] = total[BLK : BLK + 1]


def unpack_pairs(parts):
    return pl.pallas_call(
        unpack_pairs_kernel,
        in_specs=[vmem()],
        out_specs=[vmem()] * 2,
        out_shape=[
            jax.ShapeDtypeStruct((BLK, 1024), F4),
            jax.ShapeDtypeStruct((1, 1024), F4),
        ],
        compiler_params=params(),
        name="unpack_pairs",
    )(parts)


def across(array):
    return lax.all_to_all(array, ("x", "core"), 0, 0, tiled=True)


def along(array):
    return lax.all_to_all(array, ("leaf", "y"), 0, 0, tiled=True)


def shards(
    query_tree,
    output_tree,
    cotangent_tree,
    log_norm_tree,
    key_value_tree,
    query_root,
    output_root,
    cotangent_root,
    log_norm_root,
    key_value_root,
    parent,
    node_length,
):
    ids = jnp.stack([lax.axis_index(name) for name in ("x", "y", "core", "leaf")])
    ids = ids.astype(jnp.int32)
    together = lax.optimization_barrier

    joined = across(pack_pairs(key_value_tree, key_value_root))
    joined, ids = together((joined, ids))
    keep, send = pack_rows(
        ids,
        query_tree,
        output_tree,
        cotangent_tree,
        log_norm_tree,
        query_root,
        output_root,
        cotangent_root,
        log_norm_root.reshape(1, 32),
    )
    merged = merge_rows(keep, shift(send, dc=1))
    joined, *merged = together((joined, *merged))

    msg1, msg3 = shift(merged[1], dx=1), shift(merged[3], dx=3)
    own = [joined] + [shift(joined, dy=ky) for ky in range(1, 4)]
    root_own = along(pack_root(joined))
    msg1, msg3, merged[2], root_own, *own = together(
        (msg1, msg3, merged[2], root_own, *own)
    )

    msgs = [merged[0], msg1, shift(merged[2], dx=2), msg3]
    own = jnp.stack(own, axis=0)
    other, root_other = shift(own, dc=1), shift(root_own, dc=1)
    kbit, qanc, lists, counts = make_tables(ids, parent, node_length)
    *parts, keep, send, root_keep, root_send = compute(
        ids, lists, counts, kbit, qanc, own, other, root_own, root_other, msgs
    )

    stay, *low = join_cores(keep, shift(send, dc=1))
    root_sums = root_keep + shift(root_send, dc=1)
    stay, root_sums, *rest = together((stay, root_sums, *low, *parts))
    low, parts = rest[0:3], rest[3:7]

    received = [shift(low[ky - 1], dy=-ky) for ky in range(1, 4)]
    back1, back3 = shift(parts[1], dx=-1), shift(parts[3], dx=-3)
    roots = along(root_sums)
    stay, roots, back1, back3, part2, *received = together(
        (stay, roots, back1, back3, parts[2], *received)
    )

    grads = across(sum_pairs(stay, received, roots))
    back2 = shift(part2, dx=-2)
    grads, back2 = together((grads, back2))

    back = [parts[0], back1, back2, back3]
    crossed = shift(jnp.stack([part[1] for part in back], axis=0), dc=1)
    grad_pairs, grad_root = unpack_pairs(grads)
    grad_query, grad_query_root = unpack_query(ids, back, crossed)
    return grad_query, grad_query_root.reshape(1, 4096), grad_pairs, grad_root


def solution(mesh):
    axes = ("leaf", "x", "y", "core")
    finer = Mesh(mesh.devices.reshape(8, 4, 4, 2), axes)
    rows = P(axes, None)
    lanes = P(None, axes)
    tree = P("leaf", None)
    return jax.shard_map(
        shards,
        mesh=finer,
        in_specs=(rows, rows, rows, lanes, rows, rows, rows, rows, lanes, rows, tree, tree),
        out_specs=(rows, rows, rows, rows),
        check_vma=False,
    )
```

```python
import math

import jax
import jax.numpy as jnp
from jax import lax
from jax.experimental import pallas as pl
from jax.experimental.pallas import tpu as pltpu
from jax.sharding import Mesh
from jax.sharding import PartitionSpec as P

HD = 128
NODES = 24
BLK = 128
TREE_BLOCKS = 32
FACTOR = HD ** (-0.5)
LOG2E = math.log2(math.e)
SCALE2 = FACTOR * LOG2E
BF = jnp.bfloat16
F4 = jnp.float32
Q0, D0, R0, T0, MSG = 0, 512, 1024, 1040, 1088
PAIR = 144
VMEM_LIMIT = 24 * 1024 * 1024


def params(limit=VMEM_LIMIT):
    return pltpu.CompilerParams(vmem_limit_bytes=limit)


def perm(dx, dy, dc):
    pairs = []
    for x in range(4):
        for y in range(4):
            for c in range(2):
                target = ((x + dx) % 4) * 8 + ((y + dy) % 4) * 2 + (c ^ dc)
                pairs.append((x * 8 + y * 2 + c, target))
    return pairs


def shift(array, dx=0, dy=0, dc=0):
    return lax.ppermute(array, ("x", "y", "core"), perm(dx, dy, dc))


def nt(left, right):
    return lax.dot_general(left, right, (((1,), (1,)), ((), ())), preferred_element_type=F4)


def nn(left, right):
    return lax.dot_general(left, right, (((1,), (0,)), ((), ())), preferred_element_type=F4)


def iota(shape, dim):
    return lax.broadcasted_iota(jnp.int32, shape, dim)


def flip(c, dc):
    return c if dc == 0 else 1 - c


def smem():
    return pl.BlockSpec(memory_space=pltpu.SMEM)


def vmem():
    return pl.BlockSpec(memory_space=pltpu.VMEM)


def tables_kernel(ids, parent, length, kbit, qanc, lists, counts, start, anc, kmask, qmask):
    x, y, c = ids[0], ids[1], ids[2]
    for block in range(TREE_BLOCKS):
        kmask[block] = 0
        qmask[block] = 0
    total = jnp.int32(0)
    for n in range(NODES):
        start[n] = total
        bits = jnp.int32(1 << n)
        if n > 0:
            bits = bits | anc[parent[0, n]]
        anc[n] = bits
        first = total // BLK
        total = total + length[0, n]
        last = (total - 1) // BLK

        def mark(block, carry):
            kmask[block] = kmask[block] | jnp.int32(1 << n)
            qmask[block] = qmask[block] | bits
            return carry

        lax.fori_loop(first, last + 1, mark, 0)
    positions = iota((TREE_BLOCKS, BLK), 0) * BLK + iota((TREE_BLOCKS, BLK), 1)
    table = jnp.zeros((TREE_BLOCKS, BLK), jnp.int32)
    own_bits = jnp.zeros((TREE_BLOCKS, BLK), jnp.int32)
    for n in range(NODES):
        inside = positions >= start[n]
        table = jnp.where(inside, anc[n], table)
        own_bits = jnp.where(inside, jnp.int32(1 << n), own_bits)
    qanc[...] = table
    for block in range(TREE_BLOCKS):
        row = jnp.broadcast_to(own_bits[block : block + 1, :], (BLK, BLK))
        kbit[block] = row.T
    kbit[TREE_BLOCKS] = jnp.zeros((BLK, BLK), jnp.int32)
    for i in range(8):
        mine = (lax.rem(x - i // 2 + 4, 4)) * 8 + y * 2 + flip(c, i % 2)
        seen = qmask[mine]

        def scan(block, found):
            hit = (seen & kmask[block]) != 0
            lists[i, found] = block
            return found + hit.astype(jnp.int32)

        found = lax.fori_loop(0, mine + 1, scan, jnp.int32(0))
        lists[i, found] = TREE_BLOCKS
        counts[i] = (found + 1) // 2


def make_tables(ids, parent, length):
    return pl.pallas_call(
        tables_kernel,
        in_specs=[smem(), smem(), smem()],
        out_specs=[vmem(), vmem(), smem(), smem()],
        out_shape=[
            jax.ShapeDtypeStruct((TREE_BLOCKS + 1, BLK, BLK), jnp.int32),
            jax.ShapeDtypeStruct((TREE_BLOCKS, BLK), jnp.int32),
            jax.ShapeDtypeStruct((8, 40), jnp.int32),
            jax.ShapeDtypeStruct((8,), jnp.int32),
        ],
        scratch_shapes=[
            pltpu.SMEM((NODES,), jnp.int32),
            pltpu.SMEM((NODES,), jnp.int32),
            pltpu.SMEM((TREE_BLOCKS,), jnp.int32),
            pltpu.SMEM((TREE_BLOCKS,), jnp.int32),
        ],
        compiler_params=params(),
        cost_estimate=pl.CostEstimate(
            flops=10**6, bytes_accessed=4 * 10**6, transcendentals=0
        ),
        name="tables",
    )(ids, parent, length)


def pack_pairs_kernel(ids, pairs, root, *outs):
    x, c = ids[0], ids[2]
    for k in range(4):
        for s in range(2):
            col = flip(c, s) * 4 + lax.rem(x + k, 4)
            cols = pl.ds(pl.multiple_of(col * HD, HD), HD)
            outs[k][s, 0:BLK, :] = pairs[:, cols]
            row = jnp.broadcast_to(root[:, cols].astype(F4), (16, HD))
            tail = jnp.where(iota((16, HD), 0) == 0, row, 0.0)
            outs[k][s, BLK:PAIR, :] = tail.astype(BF)


def pack_pairs(ids, pairs, root):
    return pl.pallas_call(
        pack_pairs_kernel,
        in_specs=[smem()] + [vmem()] * 2,
        out_specs=[vmem()] * 4,
        out_shape=[jax.ShapeDtypeStruct((2, PAIR, HD), BF)] * 4,
        compiler_params=params(),
        name="pack_pairs",
    )(ids, pairs, root)


def split3(value):
    high = value.astype(BF)
    rest = value - high.astype(F4)
    middle = rest.astype(BF)
    low = (rest - middle.astype(F4)).astype(BF)
    return jnp.concatenate([high, middle, low], axis=0)


def pack_rows_kernel(ids, *refs):
    sources, keep, send, held, sems = refs[0:8], refs[8], refs[9], refs[10:18], refs[18]
    x, c = ids[0], ids[2]

    def target(i):
        return lax.rem(x + i // 2, 4) * 2 + flip(c, i % 2)

    small = [
        pltpu.make_async_copy(sources[n], held[n], sems.at[8, n - 3]) for n in range(3, 8)
    ]
    pieces = []
    for i in range(8):
        cols = pl.ds(pl.multiple_of(target(i) * 512, 512), 512)
        pieces.append(
            [
                pltpu.make_async_copy(sources[n].at[:, cols], held[n].at[:, cols], sems.at[i, n])
                for n in range(3)
            ]
        )
    for copy in small + sum(pieces, []):
        copy.start()
    for copy in small:
        copy.wait()
    query, output, cotangent, norm, rquery, routput, rcotangent, rnorm = held
    norms = rnorm[...] * LOG2E
    for i in range(8):
        k, dc = i // 2, i % 2
        dest = target(i)
        out = send if dc else keep
        for copy in pieces[i]:
            copy.wait()
        deltas = []
        for h in range(4):
            cols = pl.ds(pl.multiple_of(dest * 512 + h * HD, HD), HD)
            out[k, Q0 + h * BLK : Q0 + (h + 1) * BLK, :] = query[:, cols]
            grad = cotangent[:, cols]
            out[k, D0 + h * BLK : D0 + (h + 1) * BLK, :] = grad
            product = grad.astype(F4) * output[:, cols].astype(F4)
            deltas.append(jnp.sum(product.T, axis=0, keepdims=True))
        lane = iota((1, HD), 1)
        rnorm_row = jnp.zeros((1, HD), F4)
        rdelta_row = jnp.zeros((1, HD), F4)
        rquery_rows, rgrad_rows = [], []
        for h in range(4):
            cols = pl.ds(pl.multiple_of(dest * 512 + h * HD, HD), HD)
            rgrad = rcotangent[:, cols].astype(F4)
            rquery_rows.append(rquery[:, cols].astype(F4))
            rgrad_rows.append(rgrad)
            rdelta = jnp.sum(rgrad * routput[:, cols].astype(F4), axis=1, keepdims=True)
            here = lane == i * 4 + h
            mine = jnp.where(iota((1, 32), 1) == dest * 4 + h, norms, 0.0)
            mine = jnp.broadcast_to(jnp.sum(mine, axis=1, keepdims=True), (1, HD))
            rnorm_row = jnp.where(here, mine, rnorm_row)
            rdelta_row = jnp.where(here, jnp.broadcast_to(rdelta, (1, HD)), rdelta_row)
        rows = jnp.concatenate(
            [norm[pl.ds(dest * 4, 4), :] * LOG2E]
            + deltas
            + [rnorm_row, rdelta_row, jnp.zeros((6, HD), F4)],
            axis=0,
        )
        out[k, T0 : T0 + 48, :] = split3(rows)
        tile = jnp.concatenate(rquery_rows + rgrad_rows + [jnp.zeros((8, HD), F4)], axis=0)
        out[k, R0 : R0 + 16, :] = tile.astype(BF)


def pack_rows(ids, query, output, cotangent, norm, rquery, routput, rcotangent, rnorm):
    return pl.pallas_call(
        pack_rows_kernel,
        in_specs=[smem()] + [pl.BlockSpec(memory_space=pl.ANY)] * 8,
        out_specs=[vmem()] * 2,
        out_shape=[jax.ShapeDtypeStruct((4, MSG, HD), BF)] * 2,
        scratch_shapes=[pltpu.VMEM((BLK, 4096), BF)] * 3
        + [pltpu.VMEM((32, BLK), F4)]
        + [pltpu.VMEM((1, 4096), BF)] * 3
        + [pltpu.VMEM((1, 32), F4), pltpu.SemaphoreType.DMA((9, 5))],
        compiler_params=params(60 * 1024 * 1024),
        name="pack_rows",
    )(ids, query, output, cotangent, norm, rquery, routput, rcotangent, rnorm)


def merge_rows_kernel(keep, other, *outs):
    for k in range(4):
        outs[k][0] = keep[k]
        outs[k][1] = other[k]


def merge_rows(keep, other):
    return pl.pallas_call(
        merge_rows_kernel,
        in_specs=[vmem()] * 2,
        out_specs=[vmem()] * 4,
        out_shape=[jax.ShapeDtypeStruct((2, MSG, HD), BF)] * 4,
        compiler_params=params(),
        name="merge_rows",
    )(keep, other)


def unsplit(rows):
    wide = rows.astype(F4)
    return wide[0:16] + wide[16:32] + wide[32:48]


def join_pairs_kernel(ids, g0, g1, g2, g3, crossed, out, root_out):
    x, c = ids[0], ids[2]
    tile = jnp.zeros((16, HD), F4)
    for k, straight in enumerate((g0, g1, g2, g3)):
        for dc in range(2):
            block = lax.rem(x - k + 4, 4) * 2 + flip(c, dc)
            part = crossed[k] if dc else straight[0]
            out[block] = part[0:BLK]
            row = jnp.broadcast_to(part[BLK:PAIR].astype(F4)[0:1], (16, HD))
            tile = jnp.where(iota((16, HD), 0) == block, row, tile)
    for target in range(32):
        root_out[target] = tile.astype(BF)


def join_pairs(ids, parts, crossed):
    return pl.pallas_call(
        join_pairs_kernel,
        in_specs=[smem()] + [vmem()] * 5,
        out_specs=[vmem()] * 2,
        out_shape=[
            jax.ShapeDtypeStruct((8, BLK, HD), BF),
            jax.ShapeDtypeStruct((32, 16, HD), BF),
        ],
        compiler_params=params(),
        name="join_pairs",
    )(ids, *parts, crossed)


def place(y, ky, block):
    return (block // 2) * 8 + lax.rem(y - ky + 4, 4) * 2 + block % 2


def lanes_of(terms, start):
    return jnp.concatenate([terms[start + h : start + h + 1, :] for h in range(4)], axis=1)


def compute_kernel(ids, lists, counts, kbit, qanc, own, other, root_own, root_other, *refs):
    msgs, outs, refs = refs[0:4], refs[4:8], refs[8:]
    keep, send, root_keep, root_send, refs = *refs[0:4], refs[4:]
    keys, values, keys_t, root_rows, acc, dk, dv, rkey, rvalue, rkey_t, rdk, rdv = refs
    x, y, c, z = ids[0], ids[1], ids[2], ids[3]
    first = c == 0

    def load(key_ref, value_ref):
        for ky in range(4):
            for block in range(8):
                to = place(y, ky, block)
                part = key_ref[ky, block]
                keys[to] = part
                keys_t[to] = part.astype(F4).T.astype(BF)
                values[to] = value_ref[ky, block]

    @pl.when(first)
    def _():
        load(own, other)

    @pl.when(c != 0)
    def _():
        load(other, own)

    keys[TREE_BLOCKS] = jnp.zeros((BLK, HD), BF)
    keys_t[TREE_BLOCKS] = jnp.zeros((BLK, HD), BF)
    values[TREE_BLOCKS] = jnp.zeros((BLK, HD), BF)
    dk[...] = jnp.zeros(dk.shape, F4)
    dv[...] = jnp.zeros(dv.shape, F4)

    rows_own = root_own[...].astype(F4)[:, 0:8, :].reshape(256, HD)
    rows_other = root_other[...].astype(F4)[:, 0:8, :].reshape(256, HD)
    key_wide = jnp.where(first, rows_own, rows_other)
    rvalue[...] = jnp.where(first, rows_other, rows_own).astype(BF)
    rkey_t[...] = key_wide.T.astype(BF)
    rkey[...] = key_wide.astype(BF)

    root_rows[...] = jnp.zeros(root_rows.shape, F4)
    special = jnp.zeros((16, HD), F4)
    for i in range(8):
        msg, dc = msgs[i // 2], i % 2
        special = special + unsplit(msg[dc, T0 : T0 + 48, :])
        tile = msg[dc, R0 : R0 + 16, :].astype(F4)
        root_rows[0, i * 4 : i * 4 + 4, :] = tile[0:4]
        root_rows[1, i * 4 : i * 4 + 4, :] = tile[4:8]
    query = root_rows[0].astype(BF)
    grad = root_rows[1].astype(BF)
    lane, row = iota((256, HD), 1), iota((256, HD), 0)
    source = lane // 4
    source_x = lax.rem(x - source // 2 + 16, 4)
    source_c = jnp.where(source % 2 == 0, c, 1 - c)
    root_query_pos = z * 32 + source_x * 8 + y * 2 + source_c
    at = row // 8
    root_key_pos = (at // 4) * 32 + (row % 8 // 2) * 8 + (at % 4) * 2 + row % 2
    mask = (lane < 32) & (root_key_pos <= root_query_pos)
    prob = jnp.where(mask, jnp.exp2(nt(rkey[...], query) * SCALE2 - special[8:9, :]), 0.0)
    dscore = (prob * (nt(rvalue[...], grad) - special[9:10, :])).astype(BF)
    rdv[...] = nn(prob.astype(BF), grad)
    rdk[...] = nn(dscore, query)
    root_dq = nn(rkey_t[...], dscore).T * FACTOR

    pad = jnp.zeros((12, HD), F4)
    base = iota((BLK, BLK), 0)
    for k in range(4):
        msg, out = msgs[k], outs[k]
        for dc in range(2):
            tile = root_dq[8 * k + 4 * dc : 8 * k + 4 * dc + 4]
            out[dc, 512:528, :] = jnp.concatenate([tile, pad], axis=0).astype(BF)

        def query_block(dc, carry):
            i = k * 2 + dc
            mine = lax.rem(x - k + 4, 4) * 8 + y * 2 + jnp.where(dc == 0, c, 1 - c)
            anc_row = jnp.broadcast_to(qanc[pl.ds(mine, 1), :], (BLK, BLK))
            query_pos = iota((BLK, BLK), 1) + mine * BLK
            terms = unsplit(msg[dc, T0 : T0 + 48, :])
            norm, delta = lanes_of(terms, 0), lanes_of(terms, 4)

            def gradients(key, value, key_t, mask):
                query = msg[dc, Q0 : Q0 + 512, :]
                grad = msg[dc, D0 : D0 + 512, :]
                prob = jnp.exp2(nt(key, query) * SCALE2 - norm)
                if mask is not None:
                    prob = jnp.where(jnp.concatenate([mask] * 4, axis=1), prob, 0.0)
                dscore = (prob * (nt(value, grad) - delta)).astype(BF)
                return nn(dscore, query), nn(prob.astype(BF), grad), nn(key_t, dscore)

            dk_part, dv_part, dq_part = gradients(rkey[...], rvalue[...], rkey_t[...], None)
            rdk[...] = rdk[...] + dk_part
            rdv[...] = rdv[...] + dv_part
            acc[...] = dq_part

            def unit(start, width):
                at = [lists[i, start + n] for n in range(width)]
                key = jnp.concatenate([keys[b] for b in at], axis=0)
                value = jnp.concatenate([values[b] for b in at], axis=0)
                key_t = jnp.concatenate([keys_t[b] for b in at], axis=1)
                masks = [
                    ((kbit[b] & anc_row) != 0) & (base + b * BLK <= query_pos) for b in at
                ]
                mask = jnp.concatenate(masks, axis=0)
                dk_part, dv_part, dq_part = gradients(key, value, key_t, mask)
                acc[...] = acc[...] + dq_part
                for n, b in enumerate(at):
                    dk[b] = dk[b] + dk_part[n * BLK : (n + 1) * BLK]
                    dv[b] = dv[b] + dv_part[n * BLK : (n + 1) * BLK]

            def four(j, inner):
                unit(4 * j, 4)
                return inner

            count = counts[i]
            lax.fori_loop(0, count // 2, four, 0)

            @pl.when(count % 2 == 1)
            def _():
                unit(2 * count - 2, 2)

            for h in range(4):
                done = acc[:, h * BLK : (h + 1) * BLK].T * FACTOR
                out[dc, h * BLK : (h + 1) * BLK, :] = done.astype(BF)
            return carry

        lax.fori_loop(0, 2, query_block, 0)

    def store(keep_from, send_from, root_keep_from, root_send_from):
        for ky in range(4):
            for block in range(8):
                at = place(y, ky, block)
                keep[ky * 8 + block] = keep_from[at]
                send[ky * 8 + block] = send_from[at].astype(BF)
        root_keep[...] = root_keep_from[...].reshape(32, 8, HD)
        root_send[...] = root_send_from[...].reshape(32, 8, HD)

    @pl.when(first)
    def _():
        store(dk, dv, rdk, rdv)

    @pl.when(c != 0)
    def _():
        store(dv, dk, rdv, rdk)


def compute(ids, lists, counts, kbit, qanc, own, other, root_own, root_other, msgs):
    half = (TREE_BLOCKS, BLK, HD)
    blocks = pltpu.VMEM((TREE_BLOCKS + 1, BLK, HD), BF)
    sums = pltpu.VMEM((TREE_BLOCKS + 1, BLK, HD), F4)
    return pl.pallas_call(
        compute_kernel,
        in_specs=[smem()] * 3 + [vmem()] * 10,
        out_specs=[vmem()] * 8,
        out_shape=[jax.ShapeDtypeStruct((2, 528, HD), BF)] * 4
        + [jax.ShapeDtypeStruct(half, F4), jax.ShapeDtypeStruct(half, BF)]
        + [jax.ShapeDtypeStruct((32, 8, HD), F4)] * 2,
        scratch_shapes=[
            blocks,
            blocks,
            blocks,
            pltpu.VMEM((2, HD, HD), F4),
            pltpu.VMEM((HD, 512), F4),
            sums,
            sums,
            pltpu.VMEM((256, HD), BF),
            pltpu.VMEM((256, HD), BF),
            pltpu.VMEM((HD, 256), BF),
            pltpu.VMEM((256, HD), F4),
            pltpu.VMEM((256, HD), F4),
        ],
        compiler_params=params(32 * 1024 * 1024),
        cost_estimate=pl.CostEstimate(
            flops=10**10, bytes_accessed=16 * 10**6, transcendentals=8 * 10**6
        ),
        name="compute",
    )(ids, lists, counts, kbit, qanc, own, other, root_own, root_other, *msgs)


def unpack_query_kernel(ids, *refs):
    x, c = ids[0], ids[2]
    straight, crossed, out, root_out = refs[0:4], refs[4], refs[5], refs[6]
    for i in range(8):
        k, dc = i // 2, i % 2
        dest = lax.rem(x + k, 4) * 2 + flip(c, dc)
        part = crossed[k] if dc else straight[k][0]
        for h in range(4):
            cols = pl.ds(pl.multiple_of(dest * 512 + h * HD, HD), HD)
            out[:, cols] = part[h * BLK : (h + 1) * BLK, :].astype(F4)
        root_out[dest] = part[512:528, :].astype(F4)[0:4]


def unpack_query(ids, parts, crossed):
    return pl.pallas_call(
        unpack_query_kernel,
        in_specs=[smem()] + [vmem()] * 5,
        out_specs=[vmem()] * 2,
        out_shape=[
            jax.ShapeDtypeStruct((BLK, 4096), F4),
            jax.ShapeDtypeStruct((8, 4, HD), F4),
        ],
        compiler_params=params(),
        name="unpack_query",
    )(ids, *parts, crossed)


def join_cores_kernel(keep, other, stay, *outs):
    for block in range(TREE_BLOCKS):
        ky, at = block // 8, block % 8
        total = keep[block] + other[block].astype(F4)
        if ky == 0:
            stay[at] = total
        else:
            outs[ky - 1][at] = total.astype(BF)


def join_cores(keep, other):
    return pl.pallas_call(
        join_cores_kernel,
        in_specs=[vmem()] * 2,
        out_specs=[vmem()] * 4,
        out_shape=[jax.ShapeDtypeStruct((8, BLK, HD), F4)]
        + [jax.ShapeDtypeStruct((8, BLK, HD), BF)] * 3,
        compiler_params=params(),
        name="join_cores",
    )(keep, other)


def sum_pairs_kernel(ids, stay, r1, r2, r3, roots, o0, o1, o2, o3, held):
    x, c = ids[0], ids[2]
    total = roots[0]
    for n in range(1, 32):
        total = total + roots[n]
    held[...] = total
    for k, out in enumerate((o0, o1, o2, o3)):
        for dc in range(2):
            block = lax.rem(x + k, 4) * 2 + flip(c, dc)
            rest = r1[block].astype(F4) + r2[block].astype(F4) + r3[block].astype(F4)
            out[dc, 0:BLK, :] = stay[block] + rest
            row = held[pl.ds(block, 1), :]
            out[dc, BLK : BLK + 8, :] = jnp.broadcast_to(row, (8, HD))


def sum_pairs(ids, stay, received, roots):
    return pl.pallas_call(
        sum_pairs_kernel,
        in_specs=[smem()] + [vmem()] * 5,
        out_specs=[vmem()] * 4,
        out_shape=[jax.ShapeDtypeStruct((2, BLK + 8, HD), F4)] * 4,
        scratch_shapes=[pltpu.VMEM((8, HD), F4)],
        compiler_params=params(),
        name="sum_pairs",
    )(ids, stay, *received, roots)


def unpack_pairs_kernel(ids, g0, g1, g2, g3, crossed, out, root_out):
    x, c = ids[0], ids[2]
    for k, straight in enumerate((g0, g1, g2, g3)):
        for dc in range(2):
            kind = flip(c, dc)
            part = crossed[k] if dc else straight[0]
            scale = jnp.where(kind == 0, FACTOR, 1.0).astype(F4)
            col = kind * 512 + lax.rem(x - k + 4, 4) * HD
            cols = pl.ds(pl.multiple_of(col, HD), HD)
            out[:, cols] = part[0:BLK] * scale
            root_out[:, cols] = part[BLK : BLK + 1] * scale


def unpack_pairs(ids, parts, crossed):
    return pl.pallas_call(
        unpack_pairs_kernel,
        in_specs=[smem()] + [vmem()] * 5,
        out_specs=[vmem()] * 2,
        out_shape=[
            jax.ShapeDtypeStruct((BLK, 1024), F4),
            jax.ShapeDtypeStruct((1, 1024), F4),
        ],
        compiler_params=params(),
        name="unpack_pairs",
    )(ids, *parts, crossed)


def along(array):
    return lax.all_to_all(array, ("leaf", "y"), 0, 0, tiled=True)


def shards(
    query_tree,
    output_tree,
    cotangent_tree,
    log_norm_tree,
    key_value_tree,
    query_root,
    output_root,
    cotangent_root,
    log_norm_root,
    key_value_root,
    parent,
    node_length,
):
    ids = jnp.stack([lax.axis_index(name) for name in ("x", "y", "core", "leaf")])
    ids = ids.astype(jnp.int32)
    together = lax.optimization_barrier

    pair_parts = pack_pairs(ids, key_value_tree, key_value_root)
    pair_parts = [pair_parts[0]] + [shift(pair_parts[k], dx=k) for k in range(1, 4)]
    keep, send = pack_rows(
        ids,
        query_tree,
        output_tree,
        cotangent_tree,
        log_norm_tree,
        query_root,
        output_root,
        cotangent_root,
        log_norm_root.reshape(1, 32),
    )
    keep, send, *pair_parts = together((keep, send, *pair_parts))

    merged = merge_rows(keep, shift(send, dc=1))
    crossed = shift(jnp.stack([part[1] for part in pair_parts], axis=0), dc=1)
    joined, root_rows = join_pairs(ids, pair_parts, crossed)
    joined, root_rows, *merged = together((joined, root_rows, *merged))

    msg1, msg3 = shift(merged[1], dx=1), shift(merged[3], dx=3)
    own = [joined] + [shift(joined, dy=ky) for ky in range(1, 4)]
    root_own = along(root_rows)
    msg1, msg3, merged[2], root_own, *own = together(
        (msg1, msg3, merged[2], root_own, *own)
    )

    msgs = [merged[0], msg1, shift(merged[2], dx=2), msg3]
    own = jnp.stack(own, axis=0)
    other, root_other = shift(own, dc=1), shift(root_own, dc=1)
    kbit, qanc, lists, counts = make_tables(ids, parent, node_length)
    *parts, keep, send, root_keep, root_send = compute(
        ids, lists, counts, kbit, qanc, own, other, root_own, root_other, msgs
    )

    stay, *low = join_cores(keep, shift(send, dc=1))
    root_sums = root_keep + shift(root_send, dc=1)
    stay, root_sums, *rest = together((stay, root_sums, *low, *parts))
    low, parts = rest[0:3], rest[3:7]

    received = [shift(low[ky - 1], dy=-ky) for ky in range(1, 4)]
    back2 = shift(parts[2], dx=-2)
    roots = along(root_sums)
    stay, roots, back2, part1, part3, *received = together(
        (stay, roots, back2, parts[1], parts[3], *received)
    )

    sums = sum_pairs(ids, stay, received, roots)
    sums = [sums[0]] + [shift(sums[k], dx=k) for k in range(1, 4)]
    back1, back3 = shift(part1, dx=-1), shift(part3, dx=-3)
    back1, back3, *sums = together((back1, back3, *sums))

    back = [parts[0], back1, back2, back3]
    crossed = shift(jnp.stack([part[1] for part in back], axis=0), dc=1)
    crossed_sums = shift(jnp.stack([part[1] for part in sums], axis=0), dc=1)
    grad_pairs, grad_root = unpack_pairs(ids, sums, crossed_sums)
    grad_query, grad_query_root = unpack_query(ids, back, crossed)
    return grad_query, grad_query_root.reshape(1, 4096), grad_pairs, grad_root


def solution(mesh):
    axes = ("leaf", "x", "y", "core")
    finer = Mesh(mesh.devices.reshape(8, 4, 4, 2), axes)
    rows = P(axes, None)
    lanes = P(None, axes)
    tree = P("leaf", None)
    return jax.shard_map(
        shards,
        mesh=finer,
        in_specs=(rows, rows, rows, lanes, rows, rows, rows, rows, lanes, rows, tree, tree),
        out_specs=(rows, rows, rows, rows),
        check_vma=False,
    )
```

```python
import math

import jax
import jax.numpy as jnp
from jax import lax
from jax.experimental import pallas as pl
from jax.experimental.pallas import tpu as pltpu
from jax.sharding import Mesh
from jax.sharding import PartitionSpec as P

HD = 128
NODES = 24
BLK = 128
ROOT_BIT = 1 << 24
TREE_BLOCKS = 32
ALL_BLOCKS = 35
ROOT_BLOCK = 33
FACTOR = HD ** (-0.5)
LOG2E = math.log2(math.e)
SCALE2 = FACTOR * LOG2E
BF = jnp.bfloat16
F4 = jnp.float32
Q0, D0, R0, T0, MSG = 0, 512, 1024, 1040, 1088
PAIR = 144
VMEM_LIMIT = 24 * 1024 * 1024


def params(limit=VMEM_LIMIT):
    return pltpu.CompilerParams(vmem_limit_bytes=limit)


def perm(dx, dy, dc):
    pairs = []
    for x in range(4):
        for y in range(4):
            for c in range(2):
                target = ((x + dx) % 4) * 8 + ((y + dy) % 4) * 2 + (c ^ dc)
                pairs.append((x * 8 + y * 2 + c, target))
    return pairs


def shift(array, dx=0, dy=0, dc=0):
    return lax.ppermute(array, ("x", "y", "core"), perm(dx, dy, dc))


def nt(left, right):
    return lax.dot_general(left, right, (((1,), (1,)), ((), ())), preferred_element_type=F4)


def nn(left, right):
    return lax.dot_general(left, right, (((1,), (0,)), ((), ())), preferred_element_type=F4)


def iota(shape, dim):
    return lax.broadcasted_iota(jnp.int32, shape, dim)


def flip(c, dc):
    return c if dc == 0 else 1 - c


def smem():
    return pl.BlockSpec(memory_space=pltpu.SMEM)


def vmem():
    return pl.BlockSpec(memory_space=pltpu.VMEM)


def tables_kernel(ids, parent, length, kbit, qanc, lists, counts, start, anc, kmask, qmask):
    x, y, c = ids[0], ids[1], ids[2]
    for block in range(TREE_BLOCKS):
        kmask[block] = 0
        qmask[block] = 0
    total = jnp.int32(0)
    for n in range(NODES):
        start[n] = total
        bits = jnp.int32(1 << n)
        if n > 0:
            bits = bits | anc[parent[0, n]]
        anc[n] = bits
        first = total // BLK
        total = total + length[0, n]
        last = (total - 1) // BLK

        def mark(block, carry):
            kmask[block] = kmask[block] | jnp.int32(1 << n)
            qmask[block] = qmask[block] | bits
            return carry

        lax.fori_loop(first, last + 1, mark, 0)
    positions = iota((TREE_BLOCKS, BLK), 0) * BLK + iota((TREE_BLOCKS, BLK), 1)
    table = jnp.full((TREE_BLOCKS, BLK), ROOT_BIT, jnp.int32)
    own_bits = jnp.zeros((TREE_BLOCKS, BLK), jnp.int32)
    for n in range(NODES):
        inside = positions >= start[n]
        table = jnp.where(inside, anc[n] | ROOT_BIT, table)
        own_bits = jnp.where(inside, jnp.int32(1 << n), own_bits)
    qanc[...] = table
    for block in range(TREE_BLOCKS):
        row = jnp.broadcast_to(own_bits[block : block + 1, :], (BLK, BLK))
        kbit[block] = row.T
    kbit[TREE_BLOCKS] = jnp.zeros((BLK, BLK), jnp.int32)
    for block in range(ROOT_BLOCK, ALL_BLOCKS):
        kbit[block] = jnp.full((BLK, BLK), ROOT_BIT, jnp.int32)
    for i in range(8):
        mine = (lax.rem(x - i // 2 + 4, 4)) * 8 + y * 2 + flip(c, i % 2)
        seen = qmask[mine]
        lists[i, 0] = ROOT_BLOCK
        lists[i, 1] = ROOT_BLOCK + 1

        def scan(block, found):
            hit = (seen & kmask[block]) != 0
            lists[i, found] = block
            return found + hit.astype(jnp.int32)

        found = lax.fori_loop(0, mine + 1, scan, jnp.int32(2))
        lists[i, found] = TREE_BLOCKS
        counts[i] = (found + 1) // 2


def make_tables(ids, parent, length):
    return pl.pallas_call(
        tables_kernel,
        in_specs=[smem(), smem(), smem()],
        out_specs=[vmem(), vmem(), smem(), smem()],
        out_shape=[
            jax.ShapeDtypeStruct((ALL_BLOCKS, BLK, BLK), jnp.int32),
            jax.ShapeDtypeStruct((TREE_BLOCKS, BLK), jnp.int32),
            jax.ShapeDtypeStruct((8, 40), jnp.int32),
            jax.ShapeDtypeStruct((8,), jnp.int32),
        ],
        scratch_shapes=[
            pltpu.SMEM((NODES,), jnp.int32),
            pltpu.SMEM((NODES,), jnp.int32),
            pltpu.SMEM((TREE_BLOCKS,), jnp.int32),
            pltpu.SMEM((TREE_BLOCKS,), jnp.int32),
        ],
        compiler_params=params(),
        cost_estimate=pl.CostEstimate(
            flops=10**6, bytes_accessed=4 * 10**6, transcendentals=0
        ),
        name="tables",
    )(ids, parent, length)


def pack_pairs_kernel(ids, pairs, root, *outs):
    x, c = ids[0], ids[2]
    for k in range(4):
        for s in range(2):
            col = flip(c, s) * 4 + lax.rem(x + k, 4)
            cols = pl.ds(pl.multiple_of(col * HD, HD), HD)
            outs[k][s, 0:BLK, :] = pairs[:, cols]
            row = jnp.broadcast_to(root[:, cols].astype(F4), (16, HD))
            tail = jnp.where(iota((16, HD), 0) == 0, row, 0.0)
            outs[k][s, BLK:PAIR, :] = tail.astype(BF)


def pack_pairs(ids, pairs, root):
    return pl.pallas_call(
        pack_pairs_kernel,
        in_specs=[smem()] + [vmem()] * 2,
        out_specs=[vmem()] * 4,
        out_shape=[jax.ShapeDtypeStruct((2, PAIR, HD), BF)] * 4,
        compiler_params=params(),
        name="pack_pairs",
    )(ids, pairs, root)


def split3(value):
    high = value.astype(BF)
    rest = value - high.astype(F4)
    middle = rest.astype(BF)
    low = (rest - middle.astype(F4)).astype(BF)
    return jnp.concatenate([high, middle, low], axis=0)


def pack_rows_kernel(ids, *refs):
    sources, keep, send, held, stage, sems = (
        refs[0:8],
        refs[8],
        refs[9],
        refs[10:18],
        refs[18],
        refs[19],
    )
    written = []
    x, c = ids[0], ids[2]

    def target(i):
        return lax.rem(x + i // 2, 4) * 2 + flip(c, i % 2)

    small = [
        pltpu.make_async_copy(sources[n], held[n], sems.at[8, n - 3]) for n in range(3, 8)
    ]
    pieces = []
    for i in range(8):
        cols = pl.ds(pl.multiple_of(target(i) * 512, 512), 512)
        pieces.append(
            [
                pltpu.make_async_copy(sources[n].at[:, cols], held[n].at[:, cols], sems.at[i, n])
                for n in range(3)
            ]
        )
    for copy in small + sum(pieces, []):
        copy.start()
    for copy in small:
        copy.wait()
    query, output, cotangent, norm, rquery, routput, rcotangent, rnorm = held
    norms = rnorm[...] * LOG2E
    for i in range(8):
        k, dc = i // 2, i % 2
        dest = target(i)
        for copy in pieces[i]:
            copy.wait()
        deltas = []
        for h in range(4):
            cols = pl.ds(pl.multiple_of(dest * 512 + h * HD, HD), HD)
            stage[i, Q0 + h * BLK : Q0 + (h + 1) * BLK, :] = query[:, cols]
            grad = cotangent[:, cols]
            stage[i, D0 + h * BLK : D0 + (h + 1) * BLK, :] = grad
            product = grad.astype(F4) * output[:, cols].astype(F4)
            deltas.append(jnp.sum(product.T, axis=0, keepdims=True))
        lane = iota((1, HD), 1)
        rnorm_row = jnp.zeros((1, HD), F4)
        rdelta_row = jnp.zeros((1, HD), F4)
        rquery_rows, rgrad_rows = [], []
        for h in range(4):
            cols = pl.ds(pl.multiple_of(dest * 512 + h * HD, HD), HD)
            rgrad = rcotangent[:, cols].astype(F4)
            rquery_rows.append(rquery[:, cols].astype(F4))
            rgrad_rows.append(rgrad)
            rdelta = jnp.sum(rgrad * routput[:, cols].astype(F4), axis=1, keepdims=True)
            here = lane == i * 4 + h
            mine = jnp.where(iota((1, 32), 1) == dest * 4 + h, norms, 0.0)
            mine = jnp.broadcast_to(jnp.sum(mine, axis=1, keepdims=True), (1, HD))
            rnorm_row = jnp.where(here, mine, rnorm_row)
            rdelta_row = jnp.where(here, jnp.broadcast_to(rdelta, (1, HD)), rdelta_row)
        rows = jnp.concatenate(
            [norm[pl.ds(dest * 4, 4), :] * LOG2E]
            + deltas
            + [rnorm_row, rdelta_row, jnp.zeros((6, HD), F4)],
            axis=0,
        )
        stage[i, T0 : T0 + 48, :] = split3(rows)
        tile = jnp.concatenate(rquery_rows + rgrad_rows + [jnp.zeros((8, HD), F4)], axis=0)
        stage[i, R0 : R0 + 16, :] = tile.astype(BF)
        home = (send if dc else keep).at[k]
        written.append(pltpu.make_async_copy(stage.at[i], home, sems.at[i, 3]))
        written[-1].start()
    for copy in written:
        copy.wait()


def pack_rows(ids, query, output, cotangent, norm, rquery, routput, rcotangent, rnorm):
    return pl.pallas_call(
        pack_rows_kernel,
        in_specs=[smem()] + [pl.BlockSpec(memory_space=pl.ANY)] * 8,
        out_specs=[pl.BlockSpec(memory_space=pl.ANY)] * 2,
        out_shape=[jax.ShapeDtypeStruct((4, MSG, HD), BF)] * 2,
        scratch_shapes=[pltpu.VMEM((BLK, 4096), BF)] * 3
        + [pltpu.VMEM((32, BLK), F4)]
        + [pltpu.VMEM((1, 4096), BF)] * 3
        + [
            pltpu.VMEM((1, 32), F4),
            pltpu.VMEM((8, MSG, HD), BF),
            pltpu.SemaphoreType.DMA((9, 5)),
        ],
        compiler_params=params(60 * 1024 * 1024),
        name="pack_rows",
    )(ids, query, output, cotangent, norm, rquery, routput, rcotangent, rnorm)


def merge_rows_kernel(keep, other, *outs):
    for k in range(4):
        outs[k][0] = keep[k]
        outs[k][1] = other[k]


def merge_rows(keep, other):
    return pl.pallas_call(
        merge_rows_kernel,
        in_specs=[vmem()] * 2,
        out_specs=[vmem()] * 4,
        out_shape=[jax.ShapeDtypeStruct((2, MSG, HD), BF)] * 4,
        compiler_params=params(),
        name="merge_rows",
    )(keep, other)


def unsplit(rows):
    wide = rows.astype(F4)
    return wide[0:16] + wide[16:32] + wide[32:48]


def join_pairs_kernel(ids, g0, g1, g2, g3, crossed, out, root_out):
    x, c = ids[0], ids[2]
    tile = jnp.zeros((16, HD), F4)
    for k, straight in enumerate((g0, g1, g2, g3)):
        for dc in range(2):
            block = lax.rem(x - k + 4, 4) * 2 + flip(c, dc)
            part = crossed[k] if dc else straight[0]
            out[block] = part[0:BLK]
            row = jnp.broadcast_to(part[BLK:PAIR].astype(F4)[0:1], (16, HD))
            tile = jnp.where(iota((16, HD), 0) == block, row, tile)
    for target in range(32):
        root_out[target] = tile.astype(BF)


def join_pairs(ids, parts, crossed):
    return pl.pallas_call(
        join_pairs_kernel,
        in_specs=[smem()] + [vmem()] * 5,
        out_specs=[vmem()] * 2,
        out_shape=[
            jax.ShapeDtypeStruct((8, BLK, HD), BF),
            jax.ShapeDtypeStruct((32, 16, HD), BF),
        ],
        compiler_params=params(),
        name="join_pairs",
    )(ids, *parts, crossed)


def place(y, ky, block):
    return (block // 2) * 8 + lax.rem(y - ky + 4, 4) * 2 + block % 2


def lanes_of(terms, start):
    return jnp.concatenate([terms[start + h : start + h + 1, :] for h in range(4)], axis=1)


def compute_kernel(ids, lists, counts, kbit, qanc, own, other, root_own, root_other, *refs):
    msgs, outs, refs = refs[0:4], refs[4:8], refs[8:]
    keep, send, root_keep, root_send, refs = *refs[0:4], refs[4:]
    keys, values, keys_t, root_rows, acc, dk, dv = refs
    x, y, c, z = ids[0], ids[1], ids[2], ids[3]
    first = c == 0

    def load(key_ref, value_ref):
        for ky in range(4):
            for block in range(8):
                to = place(y, ky, block)
                part = key_ref[ky, block]
                keys[to] = part
                keys_t[to] = part.astype(F4).T.astype(BF)
                values[to] = value_ref[ky, block]

    @pl.when(first)
    def _():
        load(own, other)

    @pl.when(c != 0)
    def _():
        load(other, own)

    keys[TREE_BLOCKS] = jnp.zeros((BLK, HD), BF)
    keys_t[TREE_BLOCKS] = jnp.zeros((BLK, HD), BF)
    values[TREE_BLOCKS] = jnp.zeros((BLK, HD), BF)
    dk[...] = jnp.zeros(dk.shape, F4)
    dv[...] = jnp.zeros(dv.shape, F4)

    rows_own = root_own[...].astype(F4)[:, 0:8, :].reshape(256, HD)
    rows_other = root_other[...].astype(F4)[:, 0:8, :].reshape(256, HD)
    key_wide = jnp.where(first, rows_own, rows_other)
    rkey, rkey_t = key_wide.astype(BF), key_wide.T.astype(BF)
    rvalue = jnp.where(first, rows_other, rows_own).astype(BF)
    for n in range(2):
        rows = slice(n * BLK, (n + 1) * BLK)
        keys[ROOT_BLOCK + n] = rkey[rows]
        values[ROOT_BLOCK + n] = rvalue[rows]
        keys_t[ROOT_BLOCK + n] = rkey_t[:, rows]

    root_rows[...] = jnp.zeros(root_rows.shape, F4)
    special = jnp.zeros((16, HD), F4)
    for i in range(8):
        msg, dc = msgs[i // 2], i % 2
        special = special + unsplit(msg[dc, T0 : T0 + 48, :])
        tile = msg[dc, R0 : R0 + 16, :].astype(F4)
        root_rows[0, i * 4 : i * 4 + 4, :] = tile[0:4]
        root_rows[1, i * 4 : i * 4 + 4, :] = tile[4:8]
    query = root_rows[0].astype(BF)
    grad = root_rows[1].astype(BF)
    lane, row = iota((256, HD), 1), iota((256, HD), 0)
    source = lane // 4
    source_x = lax.rem(x - source // 2 + 16, 4)
    source_c = jnp.where(source % 2 == 0, c, 1 - c)
    root_query_pos = z * 32 + source_x * 8 + y * 2 + source_c
    at = row // 8
    root_key_pos = (at // 4) * 32 + (row % 8 // 2) * 8 + (at % 4) * 2 + row % 2
    mask = (lane < 32) & (root_key_pos <= root_query_pos)
    prob = jnp.where(mask, jnp.exp2(nt(rkey, query) * SCALE2 - special[8:9, :]), 0.0)
    dscore = (prob * (nt(rvalue, grad) - special[9:10, :])).astype(BF)
    dv[ROOT_BLOCK : ROOT_BLOCK + 2] = nn(prob.astype(BF), grad).reshape(2, BLK, HD)
    dk[ROOT_BLOCK : ROOT_BLOCK + 2] = nn(dscore, query).reshape(2, BLK, HD)
    root_dq = nn(rkey_t, dscore).T * FACTOR

    pad = jnp.zeros((12, HD), F4)
    base = iota((BLK, BLK), 0)
    for k in range(4):
        msg, out = msgs[k], outs[k]
        for dc in range(2):
            tile = root_dq[8 * k + 4 * dc : 8 * k + 4 * dc + 4]
            out[dc, 512:528, :] = jnp.concatenate([tile, pad], axis=0).astype(BF)

        def query_block(dc, carry):
            i = k * 2 + dc
            mine = lax.rem(x - k + 4, 4) * 8 + y * 2 + jnp.where(dc == 0, c, 1 - c)
            anc_row = jnp.broadcast_to(qanc[pl.ds(mine, 1), :], (BLK, BLK))
            query_pos = iota((BLK, BLK), 1) + mine * BLK
            terms = unsplit(msg[dc, T0 : T0 + 48, :])
            norm, delta = lanes_of(terms, 0), lanes_of(terms, 4)

            def gradients(key, value, key_t, mask):
                query = msg[dc, Q0 : Q0 + 512, :]
                grad = msg[dc, D0 : D0 + 512, :]
                prob = jnp.exp2(nt(key, query) * SCALE2 - norm)
                prob = jnp.where(jnp.concatenate([mask] * 4, axis=1), prob, 0.0)
                dscore = (prob * (nt(value, grad) - delta)).astype(BF)
                return nn(dscore, query), nn(prob.astype(BF), grad), nn(key_t, dscore)

            acc[...] = jnp.zeros(acc.shape, F4)

            def position(block):
                return jnp.where(block < ROOT_BLOCK, block, -2) * BLK

            def unit(start, width):
                at = [lists[i, start + n] for n in range(width)]
                key = jnp.concatenate([keys[b] for b in at], axis=0)
                value = jnp.concatenate([values[b] for b in at], axis=0)
                key_t = jnp.concatenate([keys_t[b] for b in at], axis=1)
                masks = [
                    ((kbit[b] & anc_row) != 0) & (base + position(b) <= query_pos) for b in at
                ]
                mask = jnp.concatenate(masks, axis=0)
                dk_part, dv_part, dq_part = gradients(key, value, key_t, mask)
                acc[...] = acc[...] + dq_part
                for n, b in enumerate(at):
                    dk[b] = dk[b] + dk_part[n * BLK : (n + 1) * BLK]
                    dv[b] = dv[b] + dv_part[n * BLK : (n + 1) * BLK]

            def four(j, inner):
                unit(4 * j, 4)
                return inner

            count = counts[i]
            lax.fori_loop(0, count // 2, four, 0)

            @pl.when(count % 2 == 1)
            def _():
                unit(2 * count - 2, 2)

            for h in range(4):
                done = acc[:, h * BLK : (h + 1) * BLK].T * FACTOR
                out[dc, h * BLK : (h + 1) * BLK, :] = done.astype(BF)
            return carry

        lax.fori_loop(0, 2, query_block, 0)

    def store(keep_from, send_from):
        for ky in range(4):
            for block in range(8):
                at = place(y, ky, block)
                keep[ky * 8 + block] = keep_from[at]
                send[ky * 8 + block] = send_from[at].astype(BF)
        rows = slice(ROOT_BLOCK, ROOT_BLOCK + 2)
        root_keep[...] = keep_from[rows].reshape(32, 8, HD)
        root_send[...] = send_from[rows].reshape(32, 8, HD)

    @pl.when(first)
    def _():
        store(dk, dv)

    @pl.when(c != 0)
    def _():
        store(dv, dk)


def compute(ids, lists, counts, kbit, qanc, own, other, root_own, root_other, msgs):
    half = (TREE_BLOCKS, BLK, HD)
    blocks = pltpu.VMEM((ALL_BLOCKS, BLK, HD), BF)
    sums = pltpu.VMEM((ALL_BLOCKS, BLK, HD), F4)
    return pl.pallas_call(
        compute_kernel,
        in_specs=[smem()] * 3 + [vmem()] * 10,
        out_specs=[vmem()] * 8,
        out_shape=[jax.ShapeDtypeStruct((2, 528, HD), BF)] * 4
        + [jax.ShapeDtypeStruct(half, F4), jax.ShapeDtypeStruct(half, BF)]
        + [jax.ShapeDtypeStruct((32, 8, HD), F4)] * 2,
        scratch_shapes=[
            blocks,
            blocks,
            blocks,
            pltpu.VMEM((2, HD, HD), F4),
            pltpu.VMEM((HD, 512), F4),
            sums,
            sums,
        ],
        compiler_params=params(32 * 1024 * 1024),
        cost_estimate=pl.CostEstimate(
            flops=10**10, bytes_accessed=16 * 10**6, transcendentals=8 * 10**6
        ),
        name="compute",
    )(ids, lists, counts, kbit, qanc, own, other, root_own, root_other, *msgs)


def join_cores_kernel(keep, other, stay, *outs):
    for block in range(TREE_BLOCKS):
        ky, at = block // 8, block % 8
        total = keep[block] + other[block].astype(F4)
        if ky == 0:
            stay[at] = total
        else:
            outs[ky - 1][at] = total.astype(BF)


def join_cores(keep, other):
    return pl.pallas_call(
        join_cores_kernel,
        in_specs=[vmem()] * 2,
        out_specs=[vmem()] * 4,
        out_shape=[jax.ShapeDtypeStruct((8, BLK, HD), F4)]
        + [jax.ShapeDtypeStruct((8, BLK, HD), BF)] * 3,
        compiler_params=params(),
        name="join_cores",
    )(keep, other)


def sum_pairs_kernel(ids, stay, r1, r2, r3, roots, o0, o1, o2, o3, held):
    x, c = ids[0], ids[2]
    total = roots[0]
    for n in range(1, 32):
        total = total + roots[n]
    held[...] = total
    for k, out in enumerate((o0, o1, o2, o3)):
        for dc in range(2):
            block = lax.rem(x + k, 4) * 2 + flip(c, dc)
            rest = r1[block].astype(F4) + r2[block].astype(F4) + r3[block].astype(F4)
            out[dc, 0:BLK, :] = stay[block] + rest
            row = held[pl.ds(block, 1), :]
            out[dc, BLK : BLK + 8, :] = jnp.broadcast_to(row, (8, HD))


def sum_pairs(ids, stay, received, roots):
    return pl.pallas_call(
        sum_pairs_kernel,
        in_specs=[smem()] + [vmem()] * 5,
        out_specs=[vmem()] * 4,
        out_shape=[jax.ShapeDtypeStruct((2, BLK + 8, HD), F4)] * 4,
        scratch_shapes=[pltpu.VMEM((8, HD), F4)],
        compiler_params=params(),
        name="sum_pairs",
    )(ids, stay, *received, roots)


def unpack_kernel(ids, *refs):
    x, c = ids[0], ids[2]
    back, crossed, sums, crossed_sums = refs[0:4], refs[4], refs[5:9], refs[9]
    out, root_out, pair_out, root_pair_out, held, pairs, sems = refs[10:]
    for k in range(4):
        for dc in range(2):
            kind = flip(c, dc)
            part = crossed_sums[k] if dc else sums[k][0]
            scale = jnp.where(kind == 0, FACTOR, 1.0).astype(F4)
            col = kind * 512 + lax.rem(x - k + 4, 4) * HD
            cols = pl.ds(pl.multiple_of(col, HD), HD)
            pairs[:, cols] = part[0:BLK] * scale
            root_pair_out[:, cols] = part[BLK : BLK + 1] * scale
    copies = [pltpu.make_async_copy(pairs, pair_out, sems.at[8])]
    copies[0].start()
    for i in range(8):
        k, dc = i // 2, i % 2
        dest = lax.rem(x + k, 4) * 2 + flip(c, dc)
        part = crossed[k] if dc else back[k][0]
        for h in range(4):
            cols = pl.ds(pl.multiple_of(dest * 512 + h * HD, HD), HD)
            held[:, cols] = part[h * BLK : (h + 1) * BLK, :].astype(F4)
        root_out[dest] = part[512:528, :].astype(F4)[0:4]
        cols = pl.ds(pl.multiple_of(dest * 512, 512), 512)
        copies.append(pltpu.make_async_copy(held.at[:, cols], out.at[:, cols], sems.at[i]))
        copies[-1].start()
    for copy in copies:
        copy.wait()


def unpack(ids, back, crossed, sums, crossed_sums):
    anywhere = pl.BlockSpec(memory_space=pl.ANY)
    return pl.pallas_call(
        unpack_kernel,
        in_specs=[smem()] + [vmem()] * 10,
        out_specs=[anywhere, vmem(), anywhere, vmem()],
        out_shape=[
            jax.ShapeDtypeStruct((BLK, 4096), F4),
            jax.ShapeDtypeStruct((8, 4, HD), F4),
            jax.ShapeDtypeStruct((BLK, 1024), F4),
            jax.ShapeDtypeStruct((1, 1024), F4),
        ],
        scratch_shapes=[
            pltpu.VMEM((BLK, 4096), F4),
            pltpu.VMEM((BLK, 1024), F4),
            pltpu.SemaphoreType.DMA((9,)),
        ],
        compiler_params=params(),
        name="unpack",
    )(ids, *back, crossed, *sums, crossed_sums)


def along(array):
    return lax.all_to_all(array, ("leaf", "y"), 0, 0, tiled=True)


def shards(
    query_tree,
    output_tree,
    cotangent_tree,
    log_norm_tree,
    key_value_tree,
    query_root,
    output_root,
    cotangent_root,
    log_norm_root,
    key_value_root,
    parent,
    node_length,
):
    ids = jnp.stack([lax.axis_index(name) for name in ("x", "y", "core", "leaf")])
    ids = ids.astype(jnp.int32)
    together = lax.optimization_barrier

    pair_parts = pack_pairs(ids, key_value_tree, key_value_root)
    pair_parts = [pair_parts[0]] + [shift(pair_parts[k], dx=k) for k in range(1, 4)]
    keep, send = pack_rows(
        ids,
        query_tree,
        output_tree,
        cotangent_tree,
        log_norm_tree,
        query_root,
        output_root,
        cotangent_root,
        log_norm_root.reshape(1, 32),
    )
    keep, send, *pair_parts = together((keep, send, *pair_parts))

    merged = merge_rows(keep, shift(send, dc=1))
    crossed = shift(jnp.stack([part[1] for part in pair_parts], axis=0), dc=1)
    joined, root_rows = join_pairs(ids, pair_parts, crossed)
    joined, root_rows, *merged = together((joined, root_rows, *merged))

    msg2 = shift(merged[2], dx=2)
    own = [joined] + [shift(joined, dy=ky) for ky in range(1, 4)]
    root_own = along(root_rows)
    msg2, merged[1], merged[3], root_own, *own = together(
        (msg2, merged[1], merged[3], root_own, *own)
    )

    msgs = [merged[0], shift(merged[1], dx=1), msg2, shift(merged[3], dx=3)]
    own = jnp.stack(own, axis=0)
    other, root_other = shift(own, dc=1), shift(root_own, dc=1)
    kbit, qanc, lists, counts = make_tables(ids, parent, node_length)
    *parts, keep, send, root_keep, root_send = compute(
        ids, lists, counts, kbit, qanc, own, other, root_own, root_other, msgs
    )

    stay, *low = join_cores(keep, shift(send, dc=1))
    root_sums = root_keep + shift(root_send, dc=1)
    stay, root_sums, *rest = together((stay, root_sums, *low, *parts))
    low, parts = rest[0:3], rest[3:7]

    received = [shift(low[ky - 1], dy=-ky) for ky in range(1, 4)]
    back2 = shift(parts[2], dx=-2)
    roots = along(root_sums)
    stay, roots, back2, part1, part3, *received = together(
        (stay, roots, back2, parts[1], parts[3], *received)
    )

    sums = sum_pairs(ids, stay, received, roots)
    sums = [sums[0]] + [shift(sums[k], dx=k) for k in range(1, 4)]
    back1, back3 = shift(part1, dx=-1), shift(part3, dx=-3)
    back1, back3, *sums = together((back1, back3, *sums))

    back = [parts[0], back1, back2, back3]
    crossed = shift(jnp.stack([part[1] for part in back], axis=0), dc=1)
    crossed_sums = shift(jnp.stack([part[1] for part in sums], axis=0), dc=1)
    grad_query, grad_query_root, grad_pairs, grad_root = unpack(
        ids, back, crossed, sums, crossed_sums
    )
    return grad_query, grad_query_root.reshape(1, 4096), grad_pairs, grad_root


def solution(mesh):
    axes = ("leaf", "x", "y", "core")
    finer = Mesh(mesh.devices.reshape(8, 4, 4, 2), axes)
    rows = P(axes, None)
    lanes = P(None, axes)
    tree = P("leaf", None)
    return jax.shard_map(
        shards,
        mesh=finer,
        in_specs=(rows, rows, rows, lanes, rows, rows, rows, rows, lanes, rows, tree, tree),
        out_specs=(rows, rows, rows, rows),
        check_vma=False,
    )
```

```python
import functools
import math

import jax
import jax.numpy as jnp
from jax import lax
from jax.experimental import pallas as pl
from jax.experimental.pallas import tpu as pltpu
from jax.sharding import Mesh
from jax.sharding import PartitionSpec as P

HD = 128
NODES = 24
BLK = 128
ROOT_BIT = 1 << 24
TREE_BLOCKS = 32
ALL_BLOCKS = 35
ROOT_BLOCK = 33
FACTOR = HD ** (-0.5)
LOG2E = math.log2(math.e)
SCALE2 = FACTOR * LOG2E
BF = jnp.bfloat16
F4 = jnp.float32
Q0, D0, R0, T0, MSG = 0, 512, 1024, 1040, 1088
PAIR = 144
VMEM_LIMIT = 24 * 1024 * 1024


def params(limit=VMEM_LIMIT):
    return pltpu.CompilerParams(vmem_limit_bytes=limit)


def perm(dx, dy, dc):
    pairs = []
    for x in range(4):
        for y in range(4):
            for c in range(2):
                target = ((x + dx) % 4) * 8 + ((y + dy) % 4) * 2 + (c ^ dc)
                pairs.append((x * 8 + y * 2 + c, target))
    return pairs


def shift(array, dx=0, dy=0, dc=0):
    return lax.ppermute(array, ("x", "y", "core"), perm(dx, dy, dc))


def nt(left, right):
    return lax.dot_general(left, right, (((1,), (1,)), ((), ())), preferred_element_type=F4)


def nn(left, right):
    return lax.dot_general(left, right, (((1,), (0,)), ((), ())), preferred_element_type=F4)


def iota(shape, dim):
    return lax.broadcasted_iota(jnp.int32, shape, dim)


def flip(c, dc):
    return c if dc == 0 else 1 - c


def smem():
    return pl.BlockSpec(memory_space=pltpu.SMEM)


def vmem():
    return pl.BlockSpec(memory_space=pltpu.VMEM)


def tables_kernel(ids, parent, length, kbit, qanc, lists, counts, start, anc, kmask, qmask):
    x, y, c = ids[0], ids[1], ids[2]
    for block in range(TREE_BLOCKS):
        kmask[block] = 0
        qmask[block] = 0
    total = jnp.int32(0)
    for n in range(NODES):
        start[n] = total
        bits = jnp.int32(1 << n)
        if n > 0:
            bits = bits | anc[parent[0, n]]
        anc[n] = bits
        first = total // BLK
        total = total + length[0, n]
        last = (total - 1) // BLK

        def mark(block, carry):
            kmask[block] = kmask[block] | jnp.int32(1 << n)
            qmask[block] = qmask[block] | bits
            return carry

        lax.fori_loop(first, last + 1, mark, 0)
    positions = iota((TREE_BLOCKS, BLK), 0) * BLK + iota((TREE_BLOCKS, BLK), 1)
    table = jnp.full((TREE_BLOCKS, BLK), ROOT_BIT, jnp.int32)
    own_bits = jnp.zeros((TREE_BLOCKS, BLK), jnp.int32)
    for n in range(NODES):
        inside = positions >= start[n]
        table = jnp.where(inside, anc[n] | ROOT_BIT, table)
        own_bits = jnp.where(inside, jnp.int32(1 << n), own_bits)
    qanc[...] = table
    for block in range(TREE_BLOCKS):
        row = jnp.broadcast_to(own_bits[block : block + 1, :], (BLK, BLK))
        kbit[block] = row.T
    kbit[TREE_BLOCKS] = jnp.zeros((BLK, BLK), jnp.int32)
    for block in range(ROOT_BLOCK, ALL_BLOCKS):
        kbit[block] = jnp.full((BLK, BLK), ROOT_BIT, jnp.int32)
    for i in range(8):
        mine = (lax.rem(x - i // 2 + 4, 4)) * 8 + y * 2 + flip(c, i % 2)
        seen = qmask[mine]
        lists[i, 0] = ROOT_BLOCK
        lists[i, 1] = ROOT_BLOCK + 1

        def scan(block, found):
            hit = (seen & kmask[block]) != 0
            lists[i, found] = block
            return found + hit.astype(jnp.int32)

        found = lax.fori_loop(0, mine + 1, scan, jnp.int32(2))
        lists[i, found] = TREE_BLOCKS
        counts[i] = (found + 1) // 2


def make_tables(ids, parent, length):
    return pl.pallas_call(
        tables_kernel,
        in_specs=[smem(), smem(), smem()],
        out_specs=[vmem(), vmem(), smem(), smem()],
        out_shape=[
            jax.ShapeDtypeStruct((ALL_BLOCKS, BLK, BLK), jnp.int32),
            jax.ShapeDtypeStruct((TREE_BLOCKS, BLK), jnp.int32),
            jax.ShapeDtypeStruct((8, 40), jnp.int32),
            jax.ShapeDtypeStruct((8,), jnp.int32),
        ],
        scratch_shapes=[
            pltpu.SMEM((NODES,), jnp.int32),
            pltpu.SMEM((NODES,), jnp.int32),
            pltpu.SMEM((TREE_BLOCKS,), jnp.int32),
            pltpu.SMEM((TREE_BLOCKS,), jnp.int32),
        ],
        compiler_params=params(),
        cost_estimate=pl.CostEstimate(
            flops=10**6, bytes_accessed=4 * 10**6, transcendentals=0
        ),
        name="tables",
    )(ids, parent, length)


def pack_pairs_kernel(ids, pairs, root, *outs):
    x, c = ids[0], ids[2]
    for k in range(4):
        for s in range(2):
            col = flip(c, s) * 4 + lax.rem(x + k, 4)
            cols = pl.ds(pl.multiple_of(col * HD, HD), HD)
            outs[k][s, 0:BLK, :] = pairs[:, cols]
            row = jnp.broadcast_to(root[:, cols].astype(F4), (16, HD))
            tail = jnp.where(iota((16, HD), 0) == 0, row, 0.0)
            outs[k][s, BLK:PAIR, :] = tail.astype(BF)


def pack_pairs(ids, pairs, root):
    return pl.pallas_call(
        pack_pairs_kernel,
        in_specs=[smem()] + [vmem()] * 2,
        out_specs=[vmem()] * 4,
        out_shape=[jax.ShapeDtypeStruct((2, PAIR, HD), BF)] * 4,
        compiler_params=params(),
        name="pack_pairs",
    )(ids, pairs, root)


def split3(value):
    high = value.astype(BF)
    rest = value - high.astype(F4)
    middle = rest.astype(BF)
    low = (rest - middle.astype(F4)).astype(BF)
    return jnp.concatenate([high, middle, low], axis=0)


def pack_rows_kernel(ids, *refs):
    sources, keep, send, held, stage, sems = (
        refs[0:8],
        refs[8],
        refs[9],
        refs[10:18],
        refs[18],
        refs[19],
    )
    written = []
    x, c = ids[0], ids[2]

    def target(i):
        return lax.rem(x + i // 2, 4) * 2 + flip(c, i % 2)

    small = [
        pltpu.make_async_copy(sources[n], held[n], sems.at[8, n - 3]) for n in range(3, 8)
    ]
    pieces = []
    for i in range(8):
        cols = pl.ds(pl.multiple_of(target(i) * 512, 512), 512)
        pieces.append(
            [
                pltpu.make_async_copy(sources[n].at[:, cols], held[n].at[:, cols], sems.at[i, n])
                for n in range(3)
            ]
        )
    for copy in small + sum(pieces, []):
        copy.start()
    for copy in small:
        copy.wait()
    query, output, cotangent, norm, rquery, routput, rcotangent, rnorm = held
    norms = rnorm[...] * LOG2E
    for i in range(8):
        k, dc = i // 2, i % 2
        dest = target(i)
        for copy in pieces[i]:
            copy.wait()
        deltas = []
        for h in range(4):
            cols = pl.ds(pl.multiple_of(dest * 512 + h * HD, HD), HD)
            stage[i, Q0 + h * BLK : Q0 + (h + 1) * BLK, :] = query[:, cols]
            grad = cotangent[:, cols]
            stage[i, D0 + h * BLK : D0 + (h + 1) * BLK, :] = grad
            product = grad.astype(F4) * output[:, cols].astype(F4)
            deltas.append(jnp.sum(product.T, axis=0, keepdims=True))
        lane = iota((1, HD), 1)
        rnorm_row = jnp.zeros((1, HD), F4)
        rdelta_row = jnp.zeros((1, HD), F4)
        rquery_rows, rgrad_rows = [], []
        for h in range(4):
            cols = pl.ds(pl.multiple_of(dest * 512 + h * HD, HD), HD)
            rgrad = rcotangent[:, cols].astype(F4)
            rquery_rows.append(rquery[:, cols].astype(F4))
            rgrad_rows.append(rgrad)
            rdelta = jnp.sum(rgrad * routput[:, cols].astype(F4), axis=1, keepdims=True)
            here = lane == i * 4 + h
            mine = jnp.where(iota((1, 32), 1) == dest * 4 + h, norms, 0.0)
            mine = jnp.broadcast_to(jnp.sum(mine, axis=1, keepdims=True), (1, HD))
            rnorm_row = jnp.where(here, mine, rnorm_row)
            rdelta_row = jnp.where(here, jnp.broadcast_to(rdelta, (1, HD)), rdelta_row)
        rows = jnp.concatenate(
            [norm[pl.ds(dest * 4, 4), :] * LOG2E]
            + deltas
            + [rnorm_row, rdelta_row, jnp.zeros((6, HD), F4)],
            axis=0,
        )
        stage[i, T0 : T0 + 48, :] = split3(rows)
        tile = jnp.concatenate(rquery_rows + rgrad_rows + [jnp.zeros((8, HD), F4)], axis=0)
        stage[i, R0 : R0 + 16, :] = tile.astype(BF)
        home = (send if dc else keep).at[k]
        written.append(pltpu.make_async_copy(stage.at[i], home, sems.at[i, 3]))
        written[-1].start()
    for copy in written:
        copy.wait()


def pack_rows(ids, query, output, cotangent, norm, rquery, routput, rcotangent, rnorm):
    return pl.pallas_call(
        pack_rows_kernel,
        in_specs=[smem()] + [pl.BlockSpec(memory_space=pl.ANY)] * 8,
        out_specs=[pl.BlockSpec(memory_space=pl.ANY)] * 2,
        out_shape=[jax.ShapeDtypeStruct((4, MSG, HD), BF)] * 2,
        scratch_shapes=[pltpu.VMEM((BLK, 4096), BF)] * 3
        + [pltpu.VMEM((32, BLK), F4)]
        + [pltpu.VMEM((1, 4096), BF)] * 3
        + [
            pltpu.VMEM((1, 32), F4),
            pltpu.VMEM((8, MSG, HD), BF),
            pltpu.SemaphoreType.DMA((9, 5)),
        ],
        compiler_params=params(60 * 1024 * 1024),
        name="pack_rows",
    )(ids, query, output, cotangent, norm, rquery, routput, rcotangent, rnorm)


def merge_rows_kernel(keep, other, *outs):
    for k in range(4):
        outs[k][0] = keep[k]
        outs[k][1] = other[k]


def merge_rows(keep, other):
    return pl.pallas_call(
        merge_rows_kernel,
        in_specs=[vmem()] * 2,
        out_specs=[vmem()] * 4,
        out_shape=[jax.ShapeDtypeStruct((2, MSG, HD), BF)] * 4,
        compiler_params=params(),
        name="merge_rows",
    )(keep, other)


def unsplit(rows):
    wide = rows.astype(F4)
    return wide[0:16] + wide[16:32] + wide[32:48]


def join_pairs_kernel(ids, g0, g1, g2, g3, crossed, out, root_out):
    x, c = ids[0], ids[2]
    tile = jnp.zeros((16, HD), F4)
    for k, straight in enumerate((g0, g1, g2, g3)):
        for dc in range(2):
            block = lax.rem(x - k + 4, 4) * 2 + flip(c, dc)
            part = crossed[k] if dc else straight[0]
            out[block] = part[0:BLK]
            row = jnp.broadcast_to(part[BLK:PAIR].astype(F4)[0:1], (16, HD))
            tile = jnp.where(iota((16, HD), 0) == block, row, tile)
    for target in range(32):
        root_out[target] = tile.astype(BF)


def join_pairs(ids, parts, crossed):
    return pl.pallas_call(
        join_pairs_kernel,
        in_specs=[smem()] + [vmem()] * 5,
        out_specs=[vmem()] * 2,
        out_shape=[
            jax.ShapeDtypeStruct((8, BLK, HD), BF),
            jax.ShapeDtypeStruct((32, 16, HD), BF),
        ],
        compiler_params=params(),
        name="join_pairs",
    )(ids, *parts, crossed)


def place(y, ky, block):
    return (block // 2) * 8 + lax.rem(y - ky + 4, 4) * 2 + block % 2


def lanes_of(terms, start):
    return jnp.concatenate([terms[start + h : start + h + 1, :] for h in range(4)], axis=1)


def compute_kernel(ks, ids, lists, counts, kbit, qanc, own, other, root_own, root_other, *refs):
    msgs, refs = refs[0:2], refs[2:]
    prior, refs = (refs[0:2], refs[2:]) if ks[0] else ((), refs)
    outs, refs = refs[0:2], refs[2:]
    if prior:
        keep, send, root_keep, root_send, refs = *refs[0:4], refs[4:]
        keep_held, send_held, sems = refs[7:10]
        copies = [
            pltpu.make_async_copy(prior[0], keep_held, sems.at[0]),
            pltpu.make_async_copy(prior[1], send_held, sems.at[1]),
        ]
        for copy in copies:
            copy.start()
    else:
        keep, send, refs = refs[0], refs[1], refs[2:]
    keys, values, keys_t, root_rows, acc, dk, dv = refs[0:7]
    x, y, c, z = ids[0], ids[1], ids[2], ids[3]
    first = c == 0

    def load(key_ref, value_ref):
        for ky in range(4):
            for block in range(8):
                to = place(y, ky, block)
                part = key_ref[ky, block]
                keys[to] = part
                keys_t[to] = part.astype(F4).T.astype(BF)
                values[to] = value_ref[ky, block]

    @pl.when(first)
    def _():
        load(own, other)

    @pl.when(c != 0)
    def _():
        load(other, own)

    keys[TREE_BLOCKS] = jnp.zeros((BLK, HD), BF)
    keys_t[TREE_BLOCKS] = jnp.zeros((BLK, HD), BF)
    values[TREE_BLOCKS] = jnp.zeros((BLK, HD), BF)
    dk[...] = jnp.zeros(dk.shape, F4)
    dv[...] = jnp.zeros(dv.shape, F4)

    rows_own = root_own[...].astype(F4)[:, 0:8, :].reshape(256, HD)
    rows_other = root_other[...].astype(F4)[:, 0:8, :].reshape(256, HD)
    key_wide = jnp.where(first, rows_own, rows_other)
    rkey, rkey_t = key_wide.astype(BF), key_wide.T.astype(BF)
    rvalue = jnp.where(first, rows_other, rows_own).astype(BF)
    for n in range(2):
        rows = slice(n * BLK, (n + 1) * BLK)
        keys[ROOT_BLOCK + n] = rkey[rows]
        values[ROOT_BLOCK + n] = rvalue[rows]
        keys_t[ROOT_BLOCK + n] = rkey_t[:, rows]

    root_rows[...] = jnp.zeros(root_rows.shape, F4)
    special = jnp.zeros((16, HD), F4)
    for i in [2 * k + dc for k in ks for dc in range(2)]:
        msg, dc = msgs[ks.index(i // 2)], i % 2
        special = special + unsplit(msg[dc, T0 : T0 + 48, :])
        tile = msg[dc, R0 : R0 + 16, :].astype(F4)
        root_rows[0, i * 4 : i * 4 + 4, :] = tile[0:4]
        root_rows[1, i * 4 : i * 4 + 4, :] = tile[4:8]
    query = root_rows[0].astype(BF)
    grad = root_rows[1].astype(BF)
    lane, row = iota((256, HD), 1), iota((256, HD), 0)
    source = lane // 4
    source_x = lax.rem(x - source // 2 + 16, 4)
    source_c = jnp.where(source % 2 == 0, c, 1 - c)
    root_query_pos = z * 32 + source_x * 8 + y * 2 + source_c
    at = row // 8
    root_key_pos = (at // 4) * 32 + (row % 8 // 2) * 8 + (at % 4) * 2 + row % 2
    here = (source // 2 == ks[0]) | (source // 2 == ks[1])
    mask = here & (root_key_pos <= root_query_pos)
    prob = jnp.where(mask, jnp.exp2(nt(rkey, query) * SCALE2 - special[8:9, :]), 0.0)
    dscore = (prob * (nt(rvalue, grad) - special[9:10, :])).astype(BF)
    dv[ROOT_BLOCK : ROOT_BLOCK + 2] = nn(prob.astype(BF), grad).reshape(2, BLK, HD)
    dk[ROOT_BLOCK : ROOT_BLOCK + 2] = nn(dscore, query).reshape(2, BLK, HD)
    root_dq = nn(rkey_t, dscore).T * FACTOR

    pad = jnp.zeros((12, HD), F4)
    base = iota((BLK, BLK), 0)
    for slot, k in enumerate(ks):
        msg, out = msgs[slot], outs[slot]
        for dc in range(2):
            tile = root_dq[8 * k + 4 * dc : 8 * k + 4 * dc + 4]
            out[dc, 512:528, :] = jnp.concatenate([tile, pad], axis=0).astype(BF)

        def query_block(dc, carry):
            i = k * 2 + dc
            mine = lax.rem(x - k + 4, 4) * 8 + y * 2 + jnp.where(dc == 0, c, 1 - c)
            anc_row = jnp.broadcast_to(qanc[pl.ds(mine, 1), :], (BLK, BLK))
            query_pos = iota((BLK, BLK), 1) + mine * BLK
            terms = unsplit(msg[dc, T0 : T0 + 48, :])
            norm, delta = lanes_of(terms, 0), lanes_of(terms, 4)

            def gradients(key, value, key_t, mask):
                query = msg[dc, Q0 : Q0 + 512, :]
                grad = msg[dc, D0 : D0 + 512, :]
                prob = jnp.exp2(nt(key, query) * SCALE2 - norm)
                prob = jnp.where(jnp.concatenate([mask] * 4, axis=1), prob, 0.0)
                dscore = (prob * (nt(value, grad) - delta)).astype(BF)
                return nn(dscore, query), nn(prob.astype(BF), grad), nn(key_t, dscore)

            acc[...] = jnp.zeros(acc.shape, F4)

            def position(block):
                return jnp.where(block < ROOT_BLOCK, block, -2) * BLK

            def unit(start, width):
                at = [lists[i, start + n] for n in range(width)]
                key = jnp.concatenate([keys[b] for b in at], axis=0)
                value = jnp.concatenate([values[b] for b in at], axis=0)
                key_t = jnp.concatenate([keys_t[b] for b in at], axis=1)
                masks = [
                    ((kbit[b] & anc_row) != 0) & (base + position(b) <= query_pos) for b in at
                ]
                mask = jnp.concatenate(masks, axis=0)
                dk_part, dv_part, dq_part = gradients(key, value, key_t, mask)
                acc[...] = acc[...] + dq_part
                for n, b in enumerate(at):
                    dk[b] = dk[b] + dk_part[n * BLK : (n + 1) * BLK]
                    dv[b] = dv[b] + dv_part[n * BLK : (n + 1) * BLK]

            def four(j, inner):
                unit(4 * j, 4)
                return inner

            count = counts[i]
            lax.fori_loop(0, count // 2, four, 0)

            @pl.when(count % 2 == 1)
            def _():
                unit(2 * count - 2, 2)

            for h in range(4):
                done = acc[:, h * BLK : (h + 1) * BLK].T * FACTOR
                out[dc, h * BLK : (h + 1) * BLK, :] = done.astype(BF)
            return carry

        lax.fori_loop(0, 2, query_block, 0)

    def store(keep_from, send_from):
        rows = slice(ROOT_BLOCK, ROOT_BLOCK + 2)
        for ky in range(4):
            for block in range(8):
                at, to = place(y, ky, block), ky * 8 + block
                if prior:
                    keep[to] = keep_from[at] + keep_held[to]
                    send[to] = (send_from[at] + send_held[to]).astype(BF)
                else:
                    keep[to] = keep_from[at]
                    send[to] = send_from[at]
        if prior:
            root_keep[...] = (keep_from[rows] + keep_held[32:34]).reshape(32, 8, HD)
            root_send[...] = (send_from[rows] + send_held[32:34]).reshape(32, 8, HD)
        else:
            keep[32:34] = keep_from[rows]
            send[32:34] = send_from[rows]

    if prior:
        for copy in copies:
            copy.wait()

    @pl.when(first)
    def _():
        store(dk, dv)

    @pl.when(c != 0)
    def _():
        store(dv, dk)


def compute(ks, shared, msgs, prior):
    blocks = pltpu.VMEM((ALL_BLOCKS, BLK, HD), BF)
    sums = pltpu.VMEM((ALL_BLOCKS, BLK, HD), F4)
    part = jax.ShapeDtypeStruct((2, 528, HD), BF)
    half = jax.ShapeDtypeStruct((34, BLK, HD), F4)
    held = pltpu.VMEM((34, BLK, HD), F4)
    if prior:
        sides = [
            jax.ShapeDtypeStruct((TREE_BLOCKS, BLK, HD), F4),
            jax.ShapeDtypeStruct((TREE_BLOCKS, BLK, HD), BF),
        ] + [jax.ShapeDtypeStruct((32, 8, HD), F4)] * 2
    else:
        sides = [half, half]
    return pl.pallas_call(
        functools.partial(compute_kernel, ks),
        in_specs=[smem()] * 3
        + [vmem()] * 8
        + [pl.BlockSpec(memory_space=pl.ANY)] * len(prior),
        out_specs=[vmem()] * (2 + len(sides)),
        out_shape=[part, part] + sides,
        scratch_shapes=[
            blocks,
            blocks,
            blocks,
            pltpu.VMEM((2, HD, HD), F4),
            pltpu.VMEM((HD, 512), F4),
            sums,
            sums,
        ]
        + ([held, held, pltpu.SemaphoreType.DMA((2,))] if prior else []),
        compiler_params=params(32 * 1024 * 1024),
        cost_estimate=pl.CostEstimate(
            flops=10**10, bytes_accessed=16 * 10**6, transcendentals=8 * 10**6
        ),
        name="compute_late" if prior else "compute_early",
    )(*shared, *msgs, *prior)


def join_cores_kernel(keep, other, stay, *outs):
    for block in range(TREE_BLOCKS):
        ky, at = block // 8, block % 8
        total = keep[block] + other[block].astype(F4)
        if ky == 0:
            stay[at] = total
        else:
            outs[ky - 1][at] = total.astype(BF)


def join_cores(keep, other):
    return pl.pallas_call(
        join_cores_kernel,
        in_specs=[vmem()] * 2,
        out_specs=[vmem()] * 4,
        out_shape=[jax.ShapeDtypeStruct((8, BLK, HD), F4)]
        + [jax.ShapeDtypeStruct((8, BLK, HD), BF)] * 3,
        compiler_params=params(),
        name="join_cores",
    )(keep, other)


def sum_pairs_kernel(ids, stay, r1, r2, r3, roots, o0, o1, o2, o3, held):
    x, c = ids[0], ids[2]
    total = roots[0]
    for n in range(1, 32):
        total = total + roots[n]
    held[...] = total
    for k, out in enumerate((o0, o1, o2, o3)):
        for dc in range(2):
            block = lax.rem(x + k, 4) * 2 + flip(c, dc)
            rest = r1[block].astype(F4) + r2[block].astype(F4) + r3[block].astype(F4)
            out[dc, 0:BLK, :] = stay[block] + rest
            row = held[pl.ds(block, 1), :]
            out[dc, BLK : BLK + 8, :] = jnp.broadcast_to(row, (8, HD))


def sum_pairs(ids, stay, received, roots):
    return pl.pallas_call(
        sum_pairs_kernel,
        in_specs=[smem()] + [vmem()] * 5,
        out_specs=[vmem()] * 4,
        out_shape=[jax.ShapeDtypeStruct((2, BLK + 8, HD), F4)] * 4,
        scratch_shapes=[pltpu.VMEM((8, HD), F4)],
        compiler_params=params(),
        name="sum_pairs",
    )(ids, stay, *received, roots)


def unpack_kernel(ids, *refs):
    x, c = ids[0], ids[2]
    back, crossed, sums, crossed_sums = refs[0:4], refs[4], refs[5:9], refs[9]
    out, root_out, pair_out, root_pair_out, held, pairs, sems = refs[10:]
    for k in range(4):
        for dc in range(2):
            kind = flip(c, dc)
            part = crossed_sums[k] if dc else sums[k][0]
            scale = jnp.where(kind == 0, FACTOR, 1.0).astype(F4)
            col = kind * 512 + lax.rem(x - k + 4, 4) * HD
            cols = pl.ds(pl.multiple_of(col, HD), HD)
            pairs[:, cols] = part[0:BLK] * scale
            root_pair_out[:, cols] = part[BLK : BLK + 1] * scale
    copies = [pltpu.make_async_copy(pairs, pair_out, sems.at[8])]
    copies[0].start()
    for i in range(8):
        k, dc = i // 2, i % 2
        dest = lax.rem(x + k, 4) * 2 + flip(c, dc)
        part = crossed[k] if dc else back[k][0]
        for h in range(4):
            cols = pl.ds(pl.multiple_of(dest * 512 + h * HD, HD), HD)
            held[:, cols] = part[h * BLK : (h + 1) * BLK, :].astype(F4)
        root_out[dest] = part[512:528, :].astype(F4)[0:4]
        cols = pl.ds(pl.multiple_of(dest * 512, 512), 512)
        copies.append(pltpu.make_async_copy(held.at[:, cols], out.at[:, cols], sems.at[i]))
        copies[-1].start()
    for copy in copies:
        copy.wait()


def unpack(ids, back, crossed, sums, crossed_sums):
    anywhere = pl.BlockSpec(memory_space=pl.ANY)
    return pl.pallas_call(
        unpack_kernel,
        in_specs=[smem()] + [vmem()] * 10,
        out_specs=[anywhere, vmem(), anywhere, vmem()],
        out_shape=[
            jax.ShapeDtypeStruct((BLK, 4096), F4),
            jax.ShapeDtypeStruct((8, 4, HD), F4),
            jax.ShapeDtypeStruct((BLK, 1024), F4),
            jax.ShapeDtypeStruct((1, 1024), F4),
        ],
        scratch_shapes=[
            pltpu.VMEM((BLK, 4096), F4),
            pltpu.VMEM((BLK, 1024), F4),
            pltpu.SemaphoreType.DMA((9,)),
        ],
        compiler_params=params(),
        name="unpack",
    )(ids, *back, crossed, *sums, crossed_sums)


def along(array):
    return lax.all_to_all(array, ("leaf", "y"), 0, 0, tiled=True)


def shards(
    query_tree,
    output_tree,
    cotangent_tree,
    log_norm_tree,
    key_value_tree,
    query_root,
    output_root,
    cotangent_root,
    log_norm_root,
    key_value_root,
    parent,
    node_length,
):
    ids = jnp.stack([lax.axis_index(name) for name in ("x", "y", "core", "leaf")])
    ids = ids.astype(jnp.int32)
    together = lax.optimization_barrier

    pair_parts = pack_pairs(ids, key_value_tree, key_value_root)
    pair_parts = [pair_parts[0]] + [shift(pair_parts[k], dx=k) for k in range(1, 4)]
    keep, send = pack_rows(
        ids,
        query_tree,
        output_tree,
        cotangent_tree,
        log_norm_tree,
        query_root,
        output_root,
        cotangent_root,
        log_norm_root.reshape(1, 32),
    )
    keep, send, *pair_parts = together((keep, send, *pair_parts))

    merged = merge_rows(keep, shift(send, dc=1))
    crossed = shift(jnp.stack([part[1] for part in pair_parts], axis=0), dc=1)
    joined, root_rows = join_pairs(ids, pair_parts, crossed)
    tables = make_tables(ids, parent, node_length)
    joined, root_rows, *rest = together((joined, root_rows, *merged, *tables))
    merged, tables = rest[0:4], rest[4:8]
    kbit, qanc, lists, counts = tables

    msg2 = shift(merged[2], dx=2)
    own = [joined] + [shift(joined, dy=ky) for ky in range(1, 4)]
    root_own = along(root_rows)
    msg2, merged[1], merged[3], root_own, *own = together(
        (msg2, merged[1], merged[3], root_own, *own)
    )

    msgs = [merged[0], shift(merged[1], dx=1), msg2, shift(merged[3], dx=3)]
    own = jnp.stack(own, axis=0)
    other, root_other = shift(own, dc=1), shift(root_own, dc=1)
    shared = (ids, lists, counts, kbit, qanc, own, other, root_own, root_other)
    part0, part2, *prior = compute((0, 2), shared, (msgs[0], msgs[2]), ())
    msg1, msg3, part0, part2, *prior = together((msgs[1], msgs[3], part0, part2, *prior))

    part1, part3, keep, send, root_keep, root_send = compute((1, 3), shared, (msg1, msg3), prior)
    back2 = shift(part2, dx=-2)
    back2, part1, part3, keep, send, root_keep, root_send = together(
        (back2, part1, part3, keep, send, root_keep, root_send)
    )

    stay, *low = join_cores(keep, shift(send, dc=1))
    root_sums = root_keep + shift(root_send, dc=1)
    stay, root_sums, *low = together((stay, root_sums, *low))

    received = [shift(low[ky - 1], dy=-ky) for ky in range(1, 4)]
    roots = along(root_sums)
    stay, roots, part1, part3, *received = together((stay, roots, part1, part3, *received))

    sums = sum_pairs(ids, stay, received, roots)
    sums = [sums[0]] + [shift(sums[k], dx=k) for k in range(1, 4)]
    back1, back3 = shift(part1, dx=-1), shift(part3, dx=-3)
    back1, back3, *sums = together((back1, back3, *sums))

    back = [part0, back1, back2, back3]
    crossed = shift(jnp.stack([part[1] for part in back], axis=0), dc=1)
    crossed_sums = shift(jnp.stack([part[1] for part in sums], axis=0), dc=1)
    grad_query, grad_query_root, grad_pairs, grad_root = unpack(
        ids, back, crossed, sums, crossed_sums
    )
    return grad_query, grad_query_root.reshape(1, 4096), grad_pairs, grad_root


def solution(mesh):
    axes = ("leaf", "x", "y", "core")
    finer = Mesh(mesh.devices.reshape(8, 4, 4, 2), axes)
    rows = P(axes, None)
    lanes = P(None, axes)
    tree = P("leaf", None)
    return jax.shard_map(
        shards,
        mesh=finer,
        in_specs=(rows, rows, rows, lanes, rows, rows, rows, rows, lanes, rows, tree, tree),
        out_specs=(rows, rows, rows, rows),
        check_vma=False,
    )
```

```python
import functools
import math

import jax
import jax.numpy as jnp
from jax import lax
from jax.experimental import pallas as pl
from jax.experimental.pallas import tpu as pltpu
from jax.sharding import Mesh
from jax.sharding import PartitionSpec as P

HD = 128
NODES = 24
BLK = 128
ROOT_BIT = 1 << 24
TREE_BLOCKS = 32
ALL_BLOCKS = 35
ROOT_BLOCK = 33
FACTOR = HD ** (-0.5)
LOG2E = math.log2(math.e)
SCALE2 = FACTOR * LOG2E
BF = jnp.bfloat16
F4 = jnp.float32
Q0, D0, R0, T0, MSG = 0, 512, 1024, 1040, 1088
PAIR = 144
VMEM_LIMIT = 24 * 1024 * 1024


def params(limit=VMEM_LIMIT):
    return pltpu.CompilerParams(vmem_limit_bytes=limit)


def perm(dx, dy, dc):
    pairs = []
    for x in range(4):
        for y in range(4):
            for c in range(2):
                target = ((x + dx) % 4) * 8 + ((y + dy) % 4) * 2 + (c ^ dc)
                pairs.append((x * 8 + y * 2 + c, target))
    return pairs


def shift(array, dx=0, dy=0, dc=0):
    return lax.ppermute(array, ("x", "y", "core"), perm(dx, dy, dc))


def nt(left, right):
    return lax.dot_general(left, right, (((1,), (1,)), ((), ())), preferred_element_type=F4)


def nn(left, right):
    return lax.dot_general(left, right, (((1,), (0,)), ((), ())), preferred_element_type=F4)


def iota(shape, dim):
    return lax.broadcasted_iota(jnp.int32, shape, dim)


def flip(c, dc):
    return c if dc == 0 else 1 - c


def smem():
    return pl.BlockSpec(memory_space=pltpu.SMEM)


def vmem():
    return pl.BlockSpec(memory_space=pltpu.VMEM)


def tables_kernel(ids, parent, length, kbit, qanc, lists, counts, start, anc, kmask, qmask):
    x, y, c = ids[0], ids[1], ids[2]
    for block in range(TREE_BLOCKS):
        kmask[block] = 0
        qmask[block] = 0
    total = jnp.int32(0)
    for n in range(NODES):
        start[n] = total
        bits = jnp.int32(1 << n)
        if n > 0:
            bits = bits | anc[parent[0, n]]
        anc[n] = bits
        begin = total
        first = total // BLK
        total = total + length[0, n]
        last = (total - 1) // BLK

        def mark(block, carry):
            kmask[block] = kmask[block] | jnp.int32(1 << n)
            qmask[block] = qmask[block] | bits
            inside = iota((BLK, BLK), 0) + block * BLK >= begin
            kbit[block] = jnp.where(inside, jnp.int32(1 << n), kbit[block])
            return carry

        lax.fori_loop(first, last + 1, mark, 0)
    positions = iota((TREE_BLOCKS, BLK), 0) * BLK + iota((TREE_BLOCKS, BLK), 1)
    table = jnp.full((TREE_BLOCKS, BLK), ROOT_BIT, jnp.int32)
    for n in range(NODES):
        inside = positions >= start[n]
        table = jnp.where(inside, anc[n] | ROOT_BIT, table)
    qanc[...] = table
    kbit[TREE_BLOCKS] = jnp.zeros((BLK, BLK), jnp.int32)
    for block in range(ROOT_BLOCK, ALL_BLOCKS):
        kbit[block] = jnp.full((BLK, BLK), ROOT_BIT, jnp.int32)
    for i in range(8):
        mine = (lax.rem(x - i // 2 + 4, 4)) * 8 + y * 2 + flip(c, i % 2)
        seen = qmask[mine]
        lists[i, 0] = ROOT_BLOCK
        lists[i, 1] = ROOT_BLOCK + 1

        def scan(block, found):
            hit = (seen & kmask[block]) != 0
            lists[i, found] = block
            return found + hit.astype(jnp.int32)

        found = lax.fori_loop(0, mine + 1, scan, jnp.int32(2))
        lists[i, found] = TREE_BLOCKS
        counts[i] = (found + 1) // 2


def make_tables(ids, parent, length):
    return pl.pallas_call(
        tables_kernel,
        in_specs=[smem(), smem(), smem()],
        out_specs=[vmem(), vmem(), smem(), smem()],
        out_shape=[
            jax.ShapeDtypeStruct((ALL_BLOCKS, BLK, BLK), jnp.int32),
            jax.ShapeDtypeStruct((TREE_BLOCKS, BLK), jnp.int32),
            jax.ShapeDtypeStruct((8, 40), jnp.int32),
            jax.ShapeDtypeStruct((8,), jnp.int32),
        ],
        scratch_shapes=[
            pltpu.SMEM((NODES,), jnp.int32),
            pltpu.SMEM((NODES,), jnp.int32),
            pltpu.SMEM((TREE_BLOCKS,), jnp.int32),
            pltpu.SMEM((TREE_BLOCKS,), jnp.int32),
        ],
        compiler_params=params(),
        cost_estimate=pl.CostEstimate(
            flops=10**6, bytes_accessed=4 * 10**6, transcendentals=0
        ),
        name="tables",
    )(ids, parent, length)


def pack_pairs_kernel(ids, pairs, root, *outs):
    x, c = ids[0], ids[2]
    for k in range(4):
        for s in range(2):
            col = flip(c, s) * 4 + lax.rem(x + k, 4)
            cols = pl.ds(pl.multiple_of(col * HD, HD), HD)
            outs[k][s, 0:BLK, :] = pairs[:, cols]
            row = jnp.broadcast_to(root[:, cols].astype(F4), (16, HD))
            tail = jnp.where(iota((16, HD), 0) == 0, row, 0.0)
            outs[k][s, BLK:PAIR, :] = tail.astype(BF)


def pack_pairs(ids, pairs, root):
    return pl.pallas_call(
        pack_pairs_kernel,
        in_specs=[smem()] + [vmem()] * 2,
        out_specs=[vmem()] * 4,
        out_shape=[jax.ShapeDtypeStruct((2, PAIR, HD), BF)] * 4,
        compiler_params=params(),
        name="pack_pairs",
    )(ids, pairs, root)


def split3(value):
    high = value.astype(BF)
    rest = value - high.astype(F4)
    middle = rest.astype(BF)
    low = (rest - middle.astype(F4)).astype(BF)
    return jnp.concatenate([high, middle, low], axis=0)


def pack_rows_kernel(ids, *refs):
    sources, keep, send, held, stage, sems = (
        refs[0:8],
        refs[8],
        refs[9],
        refs[10:18],
        refs[18],
        refs[19],
    )
    written = []
    x, c = ids[0], ids[2]

    def target(i):
        return lax.rem(x + i // 2, 4) * 2 + flip(c, i % 2)

    small = [
        pltpu.make_async_copy(sources[n], held[n], sems.at[8, n - 3]) for n in range(3, 8)
    ]
    pieces = []
    for i in range(8):
        cols = pl.ds(pl.multiple_of(target(i) * 512, 512), 512)
        pieces.append(
            [
                pltpu.make_async_copy(sources[n].at[:, cols], held[n].at[:, cols], sems.at[i, n])
                for n in range(3)
            ]
        )
    for copy in small + sum(pieces, []):
        copy.start()
    for copy in small:
        copy.wait()
    query, output, cotangent, norm, rquery, routput, rcotangent, rnorm = held
    norms = rnorm[...] * LOG2E
    for i in range(8):
        k, dc = i // 2, i % 2
        dest = target(i)
        for copy in pieces[i]:
            copy.wait()
        deltas = []
        for h in range(4):
            cols = pl.ds(pl.multiple_of(dest * 512 + h * HD, HD), HD)
            stage[i, Q0 + h * BLK : Q0 + (h + 1) * BLK, :] = query[:, cols]
            grad = cotangent[:, cols]
            stage[i, D0 + h * BLK : D0 + (h + 1) * BLK, :] = grad
            product = grad.astype(F4) * output[:, cols].astype(F4)
            deltas.append(jnp.sum(product.T, axis=0, keepdims=True))
        lane = iota((1, HD), 1)
        rnorm_row = jnp.zeros((1, HD), F4)
        rdelta_row = jnp.zeros((1, HD), F4)
        rquery_rows, rgrad_rows = [], []
        for h in range(4):
            cols = pl.ds(pl.multiple_of(dest * 512 + h * HD, HD), HD)
            rgrad = rcotangent[:, cols].astype(F4)
            rquery_rows.append(rquery[:, cols].astype(F4))
            rgrad_rows.append(rgrad)
            rdelta = jnp.sum(rgrad * routput[:, cols].astype(F4), axis=1, keepdims=True)
            here = lane == i * 4 + h
            mine = jnp.where(iota((1, 32), 1) == dest * 4 + h, norms, 0.0)
            mine = jnp.broadcast_to(jnp.sum(mine, axis=1, keepdims=True), (1, HD))
            rnorm_row = jnp.where(here, mine, rnorm_row)
            rdelta_row = jnp.where(here, jnp.broadcast_to(rdelta, (1, HD)), rdelta_row)
        rows = jnp.concatenate(
            [norm[pl.ds(dest * 4, 4), :] * LOG2E]
            + deltas
            + [rnorm_row, rdelta_row, jnp.zeros((6, HD), F4)],
            axis=0,
        )
        stage[i, T0 : T0 + 48, :] = split3(rows)
        tile = jnp.concatenate(rquery_rows + rgrad_rows + [jnp.zeros((8, HD), F4)], axis=0)
        stage[i, R0 : R0 + 16, :] = tile.astype(BF)
        home = (send if dc else keep).at[k]
        written.append(pltpu.make_async_copy(stage.at[i], home, sems.at[i, 3]))
        written[-1].start()
    for copy in written:
        copy.wait()


def pack_rows(ids, query, output, cotangent, norm, rquery, routput, rcotangent, rnorm):
    return pl.pallas_call(
        pack_rows_kernel,
        in_specs=[smem()] + [pl.BlockSpec(memory_space=pl.ANY)] * 8,
        out_specs=[pl.BlockSpec(memory_space=pl.ANY)] * 2,
        out_shape=[jax.ShapeDtypeStruct((4, MSG, HD), BF)] * 2,
        scratch_shapes=[pltpu.VMEM((BLK, 4096), BF)] * 3
        + [pltpu.VMEM((32, BLK), F4)]
        + [pltpu.VMEM((1, 4096), BF)] * 3
        + [
            pltpu.VMEM((1, 32), F4),
            pltpu.VMEM((8, MSG, HD), BF),
            pltpu.SemaphoreType.DMA((9, 5)),
        ],
        compiler_params=params(60 * 1024 * 1024),
        name="pack_rows",
    )(ids, query, output, cotangent, norm, rquery, routput, rcotangent, rnorm)


def merge_rows_kernel(keep, other, *outs):
    for k in range(4):
        outs[k][0] = keep[k]
        outs[k][1] = other[k]


def merge_rows(keep, other):
    return pl.pallas_call(
        merge_rows_kernel,
        in_specs=[vmem()] * 2,
        out_specs=[vmem()] * 4,
        out_shape=[jax.ShapeDtypeStruct((2, MSG, HD), BF)] * 4,
        compiler_params=params(),
        name="merge_rows",
    )(keep, other)


def unsplit(rows):
    wide = rows.astype(F4)
    return wide[0:16] + wide[16:32] + wide[32:48]


def join_pairs_kernel(ids, g0, g1, g2, g3, crossed, out, root_out):
    x, c = ids[0], ids[2]
    tile = jnp.zeros((16, HD), F4)
    for k, straight in enumerate((g0, g1, g2, g3)):
        for dc in range(2):
            block = lax.rem(x - k + 4, 4) * 2 + flip(c, dc)
            part = crossed[k] if dc else straight[0]
            out[block] = part[0:BLK]
            row = jnp.broadcast_to(part[BLK:PAIR].astype(F4)[0:1], (16, HD))
            tile = jnp.where(iota((16, HD), 0) == block, row, tile)
    for target in range(32):
        root_out[target] = tile.astype(BF)


def join_pairs(ids, parts, crossed):
    return pl.pallas_call(
        join_pairs_kernel,
        in_specs=[smem()] + [vmem()] * 5,
        out_specs=[vmem()] * 2,
        out_shape=[
            jax.ShapeDtypeStruct((8, BLK, HD), BF),
            jax.ShapeDtypeStruct((32, 16, HD), BF),
        ],
        compiler_params=params(),
        name="join_pairs",
    )(ids, *parts, crossed)


def place(y, ky, block):
    return (block // 2) * 8 + lax.rem(y - ky + 4, 4) * 2 + block % 2


def lanes_of(terms, start):
    return jnp.concatenate([terms[start + h : start + h + 1, :] for h in range(4)], axis=1)


def compute_kernel(ks, ids, lists, counts, kbit, qanc, own, other, root_own, root_other, *refs):
    msgs, refs = refs[0:2], refs[2:]
    prior, refs = (refs[0:2], refs[2:]) if ks[0] else ((), refs)
    outs, refs = refs[0:2], refs[2:]
    if prior:
        keep, send, root_keep, root_send, refs = *refs[0:4], refs[4:]
        keep_held, send_held, sems = refs[7:10]
        copies = [
            pltpu.make_async_copy(prior[0], keep_held, sems.at[0]),
            pltpu.make_async_copy(prior[1], send_held, sems.at[1]),
        ]
        for copy in copies:
            copy.start()
    else:
        keep, send, refs = refs[0], refs[1], refs[2:]
    keys, values, keys_t, root_rows, acc, dk, dv = refs[0:7]
    x, y, c, z = ids[0], ids[1], ids[2], ids[3]
    first = c == 0

    def load(key_ref, value_ref):
        for ky in range(4):
            for block in range(8):
                to = place(y, ky, block)
                part = key_ref[ky, block]
                keys[to] = part
                keys_t[to] = part.astype(F4).T.astype(BF)
                values[to] = value_ref[ky, block]

    @pl.when(first)
    def _():
        load(own, other)

    @pl.when(c != 0)
    def _():
        load(other, own)

    keys[TREE_BLOCKS] = jnp.zeros((BLK, HD), BF)
    keys_t[TREE_BLOCKS] = jnp.zeros((BLK, HD), BF)
    values[TREE_BLOCKS] = jnp.zeros((BLK, HD), BF)
    dk[...] = jnp.zeros(dk.shape, F4)
    dv[...] = jnp.zeros(dv.shape, F4)

    rows_own = root_own[...].astype(F4)[:, 0:8, :].reshape(256, HD)
    rows_other = root_other[...].astype(F4)[:, 0:8, :].reshape(256, HD)
    key_wide = jnp.where(first, rows_own, rows_other)
    rkey, rkey_t = key_wide.astype(BF), key_wide.T.astype(BF)
    rvalue = jnp.where(first, rows_other, rows_own).astype(BF)
    for n in range(2):
        rows = slice(n * BLK, (n + 1) * BLK)
        keys[ROOT_BLOCK + n] = rkey[rows]
        values[ROOT_BLOCK + n] = rvalue[rows]
        keys_t[ROOT_BLOCK + n] = rkey_t[:, rows]

    root_rows[...] = jnp.zeros(root_rows.shape, F4)
    special = jnp.zeros((16, HD), F4)
    for i in [2 * k + dc for k in ks for dc in range(2)]:
        msg, dc = msgs[ks.index(i // 2)], i % 2
        special = special + unsplit(msg[dc, T0 : T0 + 48, :])
        tile = msg[dc, R0 : R0 + 16, :].astype(F4)
        root_rows[0, i * 4 : i * 4 + 4, :] = tile[0:4]
        root_rows[1, i * 4 : i * 4 + 4, :] = tile[4:8]
    query = root_rows[0].astype(BF)
    grad = root_rows[1].astype(BF)
    lane, row = iota((256, HD), 1), iota((256, HD), 0)
    source = lane // 4
    source_x = lax.rem(x - source // 2 + 16, 4)
    source_c = jnp.where(source % 2 == 0, c, 1 - c)
    root_query_pos = z * 32 + source_x * 8 + y * 2 + source_c
    at = row // 8
    root_key_pos = (at // 4) * 32 + (row % 8 // 2) * 8 + (at % 4) * 2 + row % 2
    here = (source // 2 == ks[0]) | (source // 2 == ks[1])
    mask = here & (root_key_pos <= root_query_pos)
    prob = jnp.where(mask, jnp.exp2(nt(rkey, query) * SCALE2 - special[8:9, :]), 0.0)
    dscore = (prob * (nt(rvalue, grad) - special[9:10, :])).astype(BF)
    dv[ROOT_BLOCK : ROOT_BLOCK + 2] = nn(prob.astype(BF), grad).reshape(2, BLK, HD)
    dk[ROOT_BLOCK : ROOT_BLOCK + 2] = nn(dscore, query).reshape(2, BLK, HD)
    root_dq = nn(rkey_t, dscore).T * FACTOR

    pad = jnp.zeros((12, HD), F4)
    base = iota((BLK, BLK), 0)
    for slot, k in enumerate(ks):
        msg, out = msgs[slot], outs[slot]
        for dc in range(2):
            tile = root_dq[8 * k + 4 * dc : 8 * k + 4 * dc + 4]
            out[dc, 512:528, :] = jnp.concatenate([tile, pad], axis=0).astype(BF)

        def query_block(dc, carry):
            i = k * 2 + dc
            mine = lax.rem(x - k + 4, 4) * 8 + y * 2 + jnp.where(dc == 0, c, 1 - c)
            anc_row = jnp.broadcast_to(qanc[pl.ds(mine, 1), :], (BLK, BLK))
            query_pos = iota((BLK, BLK), 1) + mine * BLK
            terms = unsplit(msg[dc, T0 : T0 + 48, :])
            norm, delta = lanes_of(terms, 0), lanes_of(terms, 4)

            def gradients(key, value, key_t, mask):
                query = msg[dc, Q0 : Q0 + 512, :]
                grad = msg[dc, D0 : D0 + 512, :]
                prob = jnp.exp2(nt(key, query) * SCALE2 - norm)
                prob = jnp.where(jnp.concatenate([mask] * 4, axis=1), prob, 0.0)
                dscore = (prob * (nt(value, grad) - delta)).astype(BF)
                return nn(dscore, query), nn(prob.astype(BF), grad), nn(key_t, dscore)

            acc[...] = jnp.zeros(acc.shape, F4)

            def position(block):
                return jnp.where(block < ROOT_BLOCK, block, -2) * BLK

            def unit(start, width):
                at = [lists[i, start + n] for n in range(width)]
                key = jnp.concatenate([keys[b] for b in at], axis=0)
                value = jnp.concatenate([values[b] for b in at], axis=0)
                key_t = jnp.concatenate([keys_t[b] for b in at], axis=1)
                masks = [
                    ((kbit[b] & anc_row) != 0) & (base + position(b) <= query_pos) for b in at
                ]
                mask = jnp.concatenate(masks, axis=0)
                dk_part, dv_part, dq_part = gradients(key, value, key_t, mask)
                acc[...] = acc[...] + dq_part
                for n, b in enumerate(at):
                    dk[b] = dk[b] + dk_part[n * BLK : (n + 1) * BLK]
                    dv[b] = dv[b] + dv_part[n * BLK : (n + 1) * BLK]

            def four(j, inner):
                unit(4 * j, 4)
                return inner

            count = counts[i]
            lax.fori_loop(0, count // 2, four, 0)

            @pl.when(count % 2 == 1)
            def _():
                unit(2 * count - 2, 2)

            for h in range(4):
                done = acc[:, h * BLK : (h + 1) * BLK].T * FACTOR
                out[dc, h * BLK : (h + 1) * BLK, :] = done.astype(BF)
            return carry

        lax.fori_loop(0, 2, query_block, 0)

    def store(keep_from, send_from):
        rows = slice(ROOT_BLOCK, ROOT_BLOCK + 2)
        for ky in range(4):
            for block in range(8):
                at, to = place(y, ky, block), ky * 8 + block
                if prior:
                    keep[to] = keep_from[at] + keep_held[to]
                    send[to] = (send_from[at] + send_held[to]).astype(BF)
                else:
                    keep[to] = keep_from[at]
                    send[to] = send_from[at]
        if prior:
            root_keep[...] = (keep_from[rows] + keep_held[32:34]).reshape(32, 8, HD)
            root_send[...] = (send_from[rows] + send_held[32:34]).reshape(32, 8, HD)
        else:
            keep[32:34] = keep_from[rows]
            send[32:34] = send_from[rows]

    if prior:
        for copy in copies:
            copy.wait()

    @pl.when(first)
    def _():
        store(dk, dv)

    @pl.when(c != 0)
    def _():
        store(dv, dk)


def compute(ks, shared, msgs, prior):
    blocks = pltpu.VMEM((ALL_BLOCKS, BLK, HD), BF)
    sums = pltpu.VMEM((ALL_BLOCKS, BLK, HD), F4)
    part = jax.ShapeDtypeStruct((2, 528, HD), BF)
    half = jax.ShapeDtypeStruct((34, BLK, HD), F4)
    held = pltpu.VMEM((34, BLK, HD), F4)
    if prior:
        sides = [
            jax.ShapeDtypeStruct((TREE_BLOCKS, BLK, HD), F4),
            jax.ShapeDtypeStruct((TREE_BLOCKS, BLK, HD), BF),
        ] + [jax.ShapeDtypeStruct((32, 8, HD), F4)] * 2
    else:
        sides = [half, half]
    return pl.pallas_call(
        functools.partial(compute_kernel, ks),
        in_specs=[smem()] * 3
        + [vmem()] * 8
        + [pl.BlockSpec(memory_space=pl.ANY)] * len(prior),
        out_specs=[vmem()] * (2 + len(sides)),
        out_shape=[part, part] + sides,
        scratch_shapes=[
            blocks,
            blocks,
            blocks,
            pltpu.VMEM((2, HD, HD), F4),
            pltpu.VMEM((HD, 512), F4),
            sums,
            sums,
        ]
        + ([held, held, pltpu.SemaphoreType.DMA((2,))] if prior else []),
        compiler_params=params(32 * 1024 * 1024),
        cost_estimate=pl.CostEstimate(
            flops=10**10, bytes_accessed=16 * 10**6, transcendentals=8 * 10**6
        ),
        name="compute_late" if prior else "compute_early",
    )(*shared, *msgs, *prior)


def join_cores_kernel(keep, other, stay, *outs):
    for block in range(TREE_BLOCKS):
        ky, at = block // 8, block % 8
        total = keep[block] + other[block].astype(F4)
        if ky == 0:
            stay[at] = total
        else:
            outs[ky - 1][at] = total.astype(BF)


def join_cores(keep, other):
    return pl.pallas_call(
        join_cores_kernel,
        in_specs=[vmem()] * 2,
        out_specs=[vmem()] * 4,
        out_shape=[jax.ShapeDtypeStruct((8, BLK, HD), F4)]
        + [jax.ShapeDtypeStruct((8, BLK, HD), BF)] * 3,
        compiler_params=params(),
        name="join_cores",
    )(keep, other)


def sum_pairs_kernel(ids, stay, r1, r2, r3, roots, o0, o1, o2, o3, held):
    x, c = ids[0], ids[2]
    total = roots[0]
    for n in range(1, 32):
        total = total + roots[n]
    held[...] = total
    for k, out in enumerate((o0, o1, o2, o3)):
        for dc in range(2):
            block = lax.rem(x + k, 4) * 2 + flip(c, dc)
            rest = r1[block].astype(F4) + r2[block].astype(F4) + r3[block].astype(F4)
            out[dc, 0:BLK, :] = stay[block] + rest
            row = held[pl.ds(block, 1), :]
            out[dc, BLK : BLK + 8, :] = jnp.broadcast_to(row, (8, HD))


def sum_pairs(ids, stay, received, roots):
    return pl.pallas_call(
        sum_pairs_kernel,
        in_specs=[smem()] + [vmem()] * 5,
        out_specs=[vmem()] * 4,
        out_shape=[jax.ShapeDtypeStruct((2, BLK + 8, HD), F4)] * 4,
        scratch_shapes=[pltpu.VMEM((8, HD), F4)],
        compiler_params=params(),
        name="sum_pairs",
    )(ids, stay, *received, roots)


def unpack_pairs_kernel(ids, s0, s1, s2, s3, crossed, out, root_out):
    x, c = ids[0], ids[2]
    for k, straight in enumerate((s0, s1, s2, s3)):
        for dc in range(2):
            kind = flip(c, dc)
            part = crossed[k] if dc else straight[0]
            scale = jnp.where(kind == 0, FACTOR, 1.0).astype(F4)
            col = kind * 512 + lax.rem(x - k + 4, 4) * HD
            cols = pl.ds(pl.multiple_of(col, HD), HD)
            out[:, cols] = part[0:BLK] * scale
            root_out[:, cols] = part[BLK : BLK + 1] * scale


def unpack_pairs(ids, sums, crossed):
    return pl.pallas_call(
        unpack_pairs_kernel,
        in_specs=[smem()] + [vmem()] * 5,
        out_specs=[vmem()] * 2,
        out_shape=[
            jax.ShapeDtypeStruct((BLK, 1024), F4),
            jax.ShapeDtypeStruct((1, 1024), F4),
        ],
        compiler_params=params(),
        name="unpack_pairs",
    )(ids, *sums, crossed)


def unpack_query_kernel(ids, *refs):
    x, c = ids[0], ids[2]
    back, crossed, out, root_out, held, sems = refs[0:4], *refs[4:]
    copies = []
    for i in range(8):
        k, dc = i // 2, i % 2
        dest = lax.rem(x + k, 4) * 2 + flip(c, dc)
        part = crossed[k] if dc else back[k][0]
        for h in range(4):
            cols = pl.ds(pl.multiple_of(dest * 512 + h * HD, HD), HD)
            held[:, cols] = part[h * BLK : (h + 1) * BLK, :].astype(F4)
        root_out[dest] = part[512:528, :].astype(F4)[0:4]
        cols = pl.ds(pl.multiple_of(dest * 512, 512), 512)
        copies.append(pltpu.make_async_copy(held.at[:, cols], out.at[:, cols], sems.at[i]))
        copies[-1].start()
    for copy in copies:
        copy.wait()


def unpack_query(ids, back, crossed):
    return pl.pallas_call(
        unpack_query_kernel,
        in_specs=[smem()] + [vmem()] * 5,
        out_specs=[pl.BlockSpec(memory_space=pl.ANY), vmem()],
        out_shape=[
            jax.ShapeDtypeStruct((BLK, 4096), F4),
            jax.ShapeDtypeStruct((8, 4, HD), F4),
        ],
        scratch_shapes=[pltpu.VMEM((BLK, 4096), F4), pltpu.SemaphoreType.DMA((8,))],
        compiler_params=params(),
        cost_estimate=pl.CostEstimate(
            flops=10**6, bytes_accessed=4 * 10**6, transcendentals=0
        ),
        name="unpack_query",
    )(ids, *back, crossed)


def along(array):
    return lax.all_to_all(array, ("leaf", "y"), 0, 0, tiled=True)


def shards(
    query_tree,
    output_tree,
    cotangent_tree,
    log_norm_tree,
    key_value_tree,
    query_root,
    output_root,
    cotangent_root,
    log_norm_root,
    key_value_root,
    parent,
    node_length,
):
    ids = jnp.stack([lax.axis_index(name) for name in ("x", "y", "core", "leaf")])
    ids = ids.astype(jnp.int32)
    together = lax.optimization_barrier

    pair_parts = pack_pairs(ids, key_value_tree, key_value_root)
    pair_parts = [pair_parts[0]] + [shift(pair_parts[k], dx=k) for k in range(1, 4)]
    keep, send = pack_rows(
        ids,
        query_tree,
        output_tree,
        cotangent_tree,
        log_norm_tree,
        query_root,
        output_root,
        cotangent_root,
        log_norm_root.reshape(1, 32),
    )
    keep, send, *pair_parts = together((keep, send, *pair_parts))

    merged = merge_rows(keep, shift(send, dc=1))
    crossed = shift(jnp.stack([part[1] for part in pair_parts], axis=0), dc=1)
    joined, root_rows = join_pairs(ids, pair_parts, crossed)
    tables = make_tables(ids, parent, node_length)
    joined, root_rows, *rest = together((joined, root_rows, *merged, *tables))
    merged, tables = rest[0:4], rest[4:8]
    kbit, qanc, lists, counts = tables

    msg2 = shift(merged[2], dx=2)
    own = [joined] + [shift(joined, dy=ky) for ky in range(1, 4)]
    root_own = along(root_rows)
    msg2, merged[1], merged[3], root_own, *own = together(
        (msg2, merged[1], merged[3], root_own, *own)
    )

    msgs = [merged[0], shift(merged[1], dx=1), msg2, shift(merged[3], dx=3)]
    own = jnp.stack(own, axis=0)
    other, root_other = shift(own, dc=1), shift(root_own, dc=1)
    shared = (ids, lists, counts, kbit, qanc, own, other, root_own, root_other)
    part0, part2, *prior = compute((0, 2), shared, (msgs[0], msgs[2]), ())
    msg1, msg3, part0, part2, *prior = together((msgs[1], msgs[3], part0, part2, *prior))

    part1, part3, keep, send, root_keep, root_send = compute((1, 3), shared, (msg1, msg3), prior)
    back2 = shift(part2, dx=-2)
    back2, part1, part3, keep, send, root_keep, root_send = together(
        (back2, part1, part3, keep, send, root_keep, root_send)
    )

    stay, *low = join_cores(keep, shift(send, dc=1))
    root_sums = root_keep + shift(root_send, dc=1)
    stay, root_sums, *low = together((stay, root_sums, *low))

    received = [shift(low[ky - 1], dy=-ky) for ky in range(1, 4)]
    back1, back3 = shift(part1, dx=-1), shift(part3, dx=-3)
    roots = along(root_sums)
    stay, roots, back1, back3, *received = together((stay, roots, back1, back3, *received))

    sums = sum_pairs(ids, stay, received, roots)
    sums = [sums[0]] + [shift(sums[k], dx=k) for k in range(1, 4)]
    back = [part0, back1, back2, back3]
    crossed = shift(jnp.stack([part[1] for part in back], axis=0), dc=1)
    grad_query, grad_query_root = unpack_query(ids, back, crossed)
    grad_query, grad_query_root, *sums = together((grad_query, grad_query_root, *sums))

    crossed_sums = shift(jnp.stack([part[1] for part in sums], axis=0), dc=1)
    grad_pairs, grad_root = unpack_pairs(ids, sums, crossed_sums)
    return grad_query, grad_query_root.reshape(1, 4096), grad_pairs, grad_root


def solution(mesh):
    axes = ("leaf", "x", "y", "core")
    finer = Mesh(mesh.devices.reshape(8, 4, 4, 2), axes)
    rows = P(axes, None)
    lanes = P(None, axes)
    tree = P("leaf", None)
    return jax.shard_map(
        shards,
        mesh=finer,
        in_specs=(rows, rows, rows, lanes, rows, rows, rows, rows, lanes, rows, tree, tree),
        out_specs=(rows, rows, rows, rows),
        check_vma=False,
    )
```

```python
import math

import jax
import jax.numpy as jnp
from jax import lax
from jax.experimental import pallas as pl
from jax.experimental.pallas import tpu as pltpu
from jax.sharding import Mesh
from jax.sharding import PartitionSpec as P

HD = 128
NODES = 24
BLK = 128
ROOT_BIT = 1 << 24
TREE_BLOCKS = 32
ALL_BLOCKS = 35
ROOT_BLOCK = 33
FACTOR = HD ** (-0.5)
LOG2E = math.log2(math.e)
SCALE2 = FACTOR * LOG2E
BF = jnp.bfloat16
F4 = jnp.float32
Q0, D0, R0, T0, MSG = 0, 512, 1024, 1040, 1088
PAIR = 144
VMEM_LIMIT = 24 * 1024 * 1024


def params(limit=VMEM_LIMIT):
    return pltpu.CompilerParams(vmem_limit_bytes=limit)


def perm(dx, dy, dc):
    pairs = []
    for x in range(4):
        for y in range(4):
            for c in range(2):
                target = ((x + dx) % 4) * 8 + ((y + dy) % 4) * 2 + (c ^ dc)
                pairs.append((x * 8 + y * 2 + c, target))
    return pairs


def shift(array, dx=0, dy=0, dc=0):
    return lax.ppermute(array, ("x", "y", "core"), perm(dx, dy, dc))


def nt(left, right):
    return lax.dot_general(left, right, (((1,), (1,)), ((), ())), preferred_element_type=F4)


def nn(left, right):
    return lax.dot_general(left, right, (((1,), (0,)), ((), ())), preferred_element_type=F4)


def iota(shape, dim):
    return lax.broadcasted_iota(jnp.int32, shape, dim)


def flip(c, dc):
    return c if dc == 0 else 1 - c


def smem():
    return pl.BlockSpec(memory_space=pltpu.SMEM)


def vmem():
    return pl.BlockSpec(memory_space=pltpu.VMEM)


def tables_kernel(ids, parent, length, kbit, qanc, lists, counts, start, anc, kmask, qmask):
    x, y, c = ids[0], ids[1], ids[2]
    for block in range(TREE_BLOCKS):
        kmask[block] = 0
        qmask[block] = 0
    total = jnp.int32(0)
    for n in range(NODES):
        start[n] = total
        bits = jnp.int32(1 << n)
        if n > 0:
            bits = bits | anc[parent[0, n]]
        anc[n] = bits
        begin = total
        first = total // BLK
        total = total + length[0, n]
        last = (total - 1) // BLK

        def mark(block, carry):
            kmask[block] = kmask[block] | jnp.int32(1 << n)
            qmask[block] = qmask[block] | bits
            inside = iota((BLK, BLK), 0) + block * BLK >= begin
            kbit[block] = jnp.where(inside, jnp.int32(1 << n), kbit[block])
            return carry

        lax.fori_loop(first, last + 1, mark, 0)
    positions = iota((TREE_BLOCKS, BLK), 0) * BLK + iota((TREE_BLOCKS, BLK), 1)
    table = jnp.full((TREE_BLOCKS, BLK), ROOT_BIT, jnp.int32)
    for n in range(NODES):
        inside = positions >= start[n]
        table = jnp.where(inside, anc[n] | ROOT_BIT, table)
    qanc[...] = table
    kbit[TREE_BLOCKS] = jnp.zeros((BLK, BLK), jnp.int32)
    for block in range(ROOT_BLOCK, ALL_BLOCKS):
        kbit[block] = jnp.full((BLK, BLK), ROOT_BIT, jnp.int32)
    for i in range(8):
        mine = (lax.rem(x - i // 2 + 4, 4)) * 8 + y * 2 + flip(c, i % 2)
        seen = qmask[mine]
        lists[i, 0] = ROOT_BLOCK
        lists[i, 1] = ROOT_BLOCK + 1

        def scan(block, found):
            hit = (seen & kmask[block]) != 0
            lists[i, found] = block
            return found + hit.astype(jnp.int32)

        found = lax.fori_loop(0, mine + 1, scan, jnp.int32(2))
        lists[i, found] = TREE_BLOCKS
        counts[i] = (found + 1) // 2


def make_tables(ids, parent, length):
    return pl.pallas_call(
        tables_kernel,
        in_specs=[smem(), smem(), smem()],
        out_specs=[vmem(), vmem(), smem(), smem()],
        out_shape=[
            jax.ShapeDtypeStruct((ALL_BLOCKS, BLK, BLK), jnp.int32),
            jax.ShapeDtypeStruct((TREE_BLOCKS, BLK), jnp.int32),
            jax.ShapeDtypeStruct((8, 40), jnp.int32),
            jax.ShapeDtypeStruct((8,), jnp.int32),
        ],
        scratch_shapes=[
            pltpu.SMEM((NODES,), jnp.int32),
            pltpu.SMEM((NODES,), jnp.int32),
            pltpu.SMEM((TREE_BLOCKS,), jnp.int32),
            pltpu.SMEM((TREE_BLOCKS,), jnp.int32),
        ],
        compiler_params=params(),
        cost_estimate=pl.CostEstimate(
            flops=10**6, bytes_accessed=4 * 10**6, transcendentals=0
        ),
        name="tables",
    )(ids, parent, length)


def pack_pairs_kernel(ids, pairs, root, *outs):
    x, c = ids[0], ids[2]
    for k in range(4):
        for s in range(2):
            col = flip(c, s) * 4 + lax.rem(x + k, 4)
            cols = pl.ds(pl.multiple_of(col * HD, HD), HD)
            outs[k][s, 0:BLK, :] = pairs[:, cols]
            row = jnp.broadcast_to(root[:, cols].astype(F4), (16, HD))
            tail = jnp.where(iota((16, HD), 0) == 0, row, 0.0)
            outs[k][s, BLK:PAIR, :] = tail.astype(BF)


def pack_pairs(ids, pairs, root):
    return pl.pallas_call(
        pack_pairs_kernel,
        in_specs=[smem()] + [vmem()] * 2,
        out_specs=[vmem()] * 4,
        out_shape=[jax.ShapeDtypeStruct((2, PAIR, HD), BF)] * 4,
        compiler_params=params(),
        name="pack_pairs",
    )(ids, pairs, root)


def split3(value):
    high = value.astype(BF)
    rest = value - high.astype(F4)
    middle = rest.astype(BF)
    low = (rest - middle.astype(F4)).astype(BF)
    return jnp.concatenate([high, middle, low], axis=0)


def pack_rows_kernel(ids, *refs):
    sources, keep, send, held, stage, sems = (
        refs[0:8],
        refs[8],
        refs[9],
        refs[10:18],
        refs[18],
        refs[19],
    )
    written = []
    x, c = ids[0], ids[2]

    def target(i):
        return lax.rem(x + i // 2, 4) * 2 + flip(c, i % 2)

    small = [
        pltpu.make_async_copy(sources[n], held[n], sems.at[8, n - 3]) for n in range(3, 8)
    ]
    pieces = []
    for i in range(8):
        cols = pl.ds(pl.multiple_of(target(i) * 512, 512), 512)
        pieces.append(
            [
                pltpu.make_async_copy(sources[n].at[:, cols], held[n].at[:, cols], sems.at[i, n])
                for n in range(3)
            ]
        )
    for copy in small + sum(pieces, []):
        copy.start()
    for copy in small:
        copy.wait()
    query, output, cotangent, norm, rquery, routput, rcotangent, rnorm = held
    norms = rnorm[...] * LOG2E
    for i in range(8):
        k, dc = i // 2, i % 2
        dest = target(i)
        for copy in pieces[i]:
            copy.wait()
        deltas = []
        for h in range(4):
            cols = pl.ds(pl.multiple_of(dest * 512 + h * HD, HD), HD)
            stage[i, Q0 + h * BLK : Q0 + (h + 1) * BLK, :] = query[:, cols]
            grad = cotangent[:, cols]
            stage[i, D0 + h * BLK : D0 + (h + 1) * BLK, :] = grad
            product = grad.astype(F4) * output[:, cols].astype(F4)
            deltas.append(jnp.sum(product.T, axis=0, keepdims=True))
        lane = iota((1, HD), 1)
        rnorm_row = jnp.zeros((1, HD), F4)
        rdelta_row = jnp.zeros((1, HD), F4)
        rquery_rows, rgrad_rows = [], []
        for h in range(4):
            cols = pl.ds(pl.multiple_of(dest * 512 + h * HD, HD), HD)
            rgrad = rcotangent[:, cols].astype(F4)
            rquery_rows.append(rquery[:, cols].astype(F4))
            rgrad_rows.append(rgrad)
            rdelta = jnp.sum(rgrad * routput[:, cols].astype(F4), axis=1, keepdims=True)
            here = lane == i * 4 + h
            mine = jnp.where(iota((1, 32), 1) == dest * 4 + h, norms, 0.0)
            mine = jnp.broadcast_to(jnp.sum(mine, axis=1, keepdims=True), (1, HD))
            rnorm_row = jnp.where(here, mine, rnorm_row)
            rdelta_row = jnp.where(here, jnp.broadcast_to(rdelta, (1, HD)), rdelta_row)
        rows = jnp.concatenate(
            [norm[pl.ds(dest * 4, 4), :] * LOG2E]
            + deltas
            + [rnorm_row, rdelta_row, jnp.zeros((6, HD), F4)],
            axis=0,
        )
        stage[i, T0 : T0 + 48, :] = split3(rows)
        tile = jnp.concatenate(rquery_rows + rgrad_rows + [jnp.zeros((8, HD), F4)], axis=0)
        stage[i, R0 : R0 + 16, :] = tile.astype(BF)
        home = (send if dc else keep).at[k]
        written.append(pltpu.make_async_copy(stage.at[i], home, sems.at[i, 3]))
        written[-1].start()
    for copy in written:
        copy.wait()


def pack_rows(ids, query, output, cotangent, norm, rquery, routput, rcotangent, rnorm):
    return pl.pallas_call(
        pack_rows_kernel,
        in_specs=[smem()] + [pl.BlockSpec(memory_space=pl.ANY)] * 8,
        out_specs=[pl.BlockSpec(memory_space=pl.ANY)] * 2,
        out_shape=[jax.ShapeDtypeStruct((4, MSG, HD), BF)] * 2,
        scratch_shapes=[pltpu.VMEM((BLK, 4096), BF)] * 3
        + [pltpu.VMEM((32, BLK), F4)]
        + [pltpu.VMEM((1, 4096), BF)] * 3
        + [
            pltpu.VMEM((1, 32), F4),
            pltpu.VMEM((8, MSG, HD), BF),
            pltpu.SemaphoreType.DMA((9, 5)),
        ],
        compiler_params=params(60 * 1024 * 1024),
        name="pack_rows",
    )(ids, query, output, cotangent, norm, rquery, routput, rcotangent, rnorm)


def merge_rows_kernel(keep, other, *outs):
    for k in range(4):
        outs[k][0] = keep[k]
        outs[k][1] = other[k]


def merge_rows(keep, other):
    return pl.pallas_call(
        merge_rows_kernel,
        in_specs=[vmem()] * 2,
        out_specs=[vmem()] * 4,
        out_shape=[jax.ShapeDtypeStruct((2, MSG, HD), BF)] * 4,
        compiler_params=params(),
        name="merge_rows",
    )(keep, other)


def unsplit(rows):
    wide = rows.astype(F4)
    return wide[0:16] + wide[16:32] + wide[32:48]


def join_pairs_kernel(ids, g0, g1, g2, g3, crossed, out, root_out):
    x, c = ids[0], ids[2]
    tile = jnp.zeros((16, HD), F4)
    for k, straight in enumerate((g0, g1, g2, g3)):
        for dc in range(2):
            block = lax.rem(x - k + 4, 4) * 2 + flip(c, dc)
            part = crossed[k] if dc else straight[0]
            out[block] = part[0:BLK]
            row = jnp.broadcast_to(part[BLK:PAIR].astype(F4)[0:1], (16, HD))
            tile = jnp.where(iota((16, HD), 0) == block, row, tile)
    for target in range(32):
        root_out[target] = tile.astype(BF)


def join_pairs(ids, parts, crossed):
    return pl.pallas_call(
        join_pairs_kernel,
        in_specs=[smem()] + [vmem()] * 5,
        out_specs=[vmem()] * 2,
        out_shape=[
            jax.ShapeDtypeStruct((8, BLK, HD), BF),
            jax.ShapeDtypeStruct((32, 16, HD), BF),
        ],
        compiler_params=params(),
        name="join_pairs",
    )(ids, *parts, crossed)


def place(y, ky, block):
    return (block // 2) * 8 + lax.rem(y - ky + 4, 4) * 2 + block % 2


def lanes_of(terms, start):
    return jnp.concatenate([terms[start + h : start + h + 1, :] for h in range(4)], axis=1)


def arrange(ids, own, other, root_own, root_other, keys, values, keys_t):
    y, c = ids[1], ids[2]
    first = c == 0

    def load(key_ref, value_ref):
        for ky in range(4):
            for block in range(8):
                to = place(y, ky, block)
                part = key_ref[ky, block]
                keys[to] = part
                keys_t[to] = part.astype(F4).T.astype(BF)
                values[to] = value_ref[ky, block]

    @pl.when(first)
    def _():
        load(own, other)

    @pl.when(c != 0)
    def _():
        load(other, own)

    keys[TREE_BLOCKS] = jnp.zeros((BLK, HD), BF)
    keys_t[TREE_BLOCKS] = jnp.zeros((BLK, HD), BF)
    values[TREE_BLOCKS] = jnp.zeros((BLK, HD), BF)

    rows_own = root_own[...].astype(F4)[:, 0:8, :].reshape(256, HD)
    rows_other = root_other[...].astype(F4)[:, 0:8, :].reshape(256, HD)
    key_wide = jnp.where(first, rows_own, rows_other)
    rkey, rkey_t = key_wide.astype(BF), key_wide.T.astype(BF)
    rvalue = jnp.where(first, rows_other, rows_own).astype(BF)
    for n in range(2):
        rows = slice(n * BLK, (n + 1) * BLK)
        keys[ROOT_BLOCK + n] = rkey[rows]
        values[ROOT_BLOCK + n] = rvalue[rows]
        keys_t[ROOT_BLOCK + n] = rkey_t[:, rows]


def early_kernel(ids, lists, counts, kbit, qanc, own, other, root_own, root_other, m0, m1,
                 o0, o1, dk, dv, keys, values, keys_t, root_rows, acc):
    arrange(ids, own, other, root_own, root_other, keys, values, keys_t)
    dk[...] = jnp.zeros(dk.shape, F4)
    dv[...] = jnp.zeros(dv.shape, F4)
    work((0, 2), ids, lists, counts, kbit, qanc, keys, values, keys_t, (m0, m1), (o0, o1),
         root_rows, acc, dk, dv)


def late_kernel(ids, lists, counts, kbit, qanc, keys, values, keys_t, dk0, dv0, m0, m1,
                o0, o1, keep, send, root_keep, root_send, root_rows, acc, dk, dv):
    dk[...] = dk0[...]
    dv[...] = dv0[...]
    work((1, 3), ids, lists, counts, kbit, qanc, keys, values, keys_t, (m0, m1), (o0, o1),
         root_rows, acc, dk, dv)
    y = ids[1]

    def store(keep_from, send_from):
        rows = slice(ROOT_BLOCK, ROOT_BLOCK + 2)
        for ky in range(4):
            for block in range(8):
                at, to = place(y, ky, block), ky * 8 + block
                keep[to] = keep_from[at]
                send[to] = send_from[at].astype(BF)
        root_keep[...] = keep_from[rows].reshape(32, 8, HD)
        root_send[...] = send_from[rows].reshape(32, 8, HD)

    @pl.when(ids[2] == 0)
    def _():
        store(dk, dv)

    @pl.when(ids[2] != 0)
    def _():
        store(dv, dk)


def work(ks, ids, lists, counts, kbit, qanc, keys, values, keys_t, msgs, outs, root_rows, acc,
         dk, dv):
    x, y, c, z = ids[0], ids[1], ids[2], ids[3]
    rkey = jnp.concatenate([keys[ROOT_BLOCK], keys[ROOT_BLOCK + 1]], axis=0)
    rvalue = jnp.concatenate([values[ROOT_BLOCK], values[ROOT_BLOCK + 1]], axis=0)
    rkey_t = jnp.concatenate([keys_t[ROOT_BLOCK], keys_t[ROOT_BLOCK + 1]], axis=1)
    root_rows[...] = jnp.zeros(root_rows.shape, F4)
    special = jnp.zeros((16, HD), F4)
    for i in [2 * k + dc for k in ks for dc in range(2)]:
        msg, dc = msgs[ks.index(i // 2)], i % 2
        special = special + unsplit(msg[dc, T0 : T0 + 48, :])
        tile = msg[dc, R0 : R0 + 16, :].astype(F4)
        root_rows[0, i * 4 : i * 4 + 4, :] = tile[0:4]
        root_rows[1, i * 4 : i * 4 + 4, :] = tile[4:8]
    query = root_rows[0].astype(BF)
    grad = root_rows[1].astype(BF)
    lane, row = iota((256, HD), 1), iota((256, HD), 0)
    source = lane // 4
    source_x = lax.rem(x - source // 2 + 16, 4)
    source_c = jnp.where(source % 2 == 0, c, 1 - c)
    root_query_pos = z * 32 + source_x * 8 + y * 2 + source_c
    at = row // 8
    root_key_pos = (at // 4) * 32 + (row % 8 // 2) * 8 + (at % 4) * 2 + row % 2
    here = (source // 2 == ks[0]) | (source // 2 == ks[1])
    mask = here & (root_key_pos <= root_query_pos)
    prob = jnp.where(mask, jnp.exp2(nt(rkey, query) * SCALE2 - special[8:9, :]), 0.0)
    dscore = (prob * (nt(rvalue, grad) - special[9:10, :])).astype(BF)
    rows = slice(ROOT_BLOCK, ROOT_BLOCK + 2)
    dv[rows] = dv[rows] + nn(prob.astype(BF), grad).reshape(2, BLK, HD)
    dk[rows] = dk[rows] + nn(dscore, query).reshape(2, BLK, HD)
    root_dq = nn(rkey_t, dscore).T * FACTOR

    pad = jnp.zeros((12, HD), F4)
    base = iota((BLK, BLK), 0)
    for slot, k in enumerate(ks):
        msg, out = msgs[slot], outs[slot]
        for dc in range(2):
            tile = root_dq[8 * k + 4 * dc : 8 * k + 4 * dc + 4]
            out[dc, 512:528, :] = jnp.concatenate([tile, pad], axis=0).astype(BF)

        def query_block(dc, carry):
            i = k * 2 + dc
            mine = lax.rem(x - k + 4, 4) * 8 + y * 2 + jnp.where(dc == 0, c, 1 - c)
            anc_row = jnp.broadcast_to(qanc[pl.ds(mine, 1), :], (BLK, BLK))
            query_pos = iota((BLK, BLK), 1) + mine * BLK
            terms = unsplit(msg[dc, T0 : T0 + 48, :])
            norm, delta = lanes_of(terms, 0), lanes_of(terms, 4)

            def gradients(key, value, key_t, mask):
                query = msg[dc, Q0 : Q0 + 512, :]
                grad = msg[dc, D0 : D0 + 512, :]
                prob = jnp.exp2(nt(key, query) * SCALE2 - norm)
                prob = jnp.where(jnp.concatenate([mask] * 4, axis=1), prob, 0.0)
                dscore = (prob * (nt(value, grad) - delta)).astype(BF)
                return nn(dscore, query), nn(prob.astype(BF), grad), nn(key_t, dscore)

            acc[...] = jnp.zeros(acc.shape, F4)

            def position(block):
                return jnp.where(block < ROOT_BLOCK, block, -2) * BLK

            def unit(start, width):
                at = [lists[i, start + n] for n in range(width)]
                key = jnp.concatenate([keys[b] for b in at], axis=0)
                value = jnp.concatenate([values[b] for b in at], axis=0)
                key_t = jnp.concatenate([keys_t[b] for b in at], axis=1)
                masks = [
                    ((kbit[b] & anc_row) != 0) & (base + position(b) <= query_pos) for b in at
                ]
                mask = jnp.concatenate(masks, axis=0)
                dk_part, dv_part, dq_part = gradients(key, value, key_t, mask)
                acc[...] = acc[...] + dq_part
                for n, b in enumerate(at):
                    dk[b] = dk[b] + dk_part[n * BLK : (n + 1) * BLK]
                    dv[b] = dv[b] + dv_part[n * BLK : (n + 1) * BLK]

            def four(j, inner):
                unit(4 * j, 4)
                return inner

            count = counts[i]
            lax.fori_loop(0, count // 2, four, 0)

            @pl.when(count % 2 == 1)
            def _():
                unit(2 * count - 2, 2)

            for h in range(4):
                done = acc[:, h * BLK : (h + 1) * BLK].T * FACTOR
                out[dc, h * BLK : (h + 1) * BLK, :] = done.astype(BF)
            return carry

        lax.fori_loop(0, 2, query_block, 0)


def compute(kernel, name, arrays, outs, scratch):
    part = jax.ShapeDtypeStruct((2, 528, HD), BF)
    return pl.pallas_call(
        kernel,
        in_specs=[smem()] * 3 + [vmem()] * (len(arrays) - 3),
        out_specs=[vmem()] * (2 + len(outs)),
        out_shape=[part, part] + outs,
        scratch_shapes=[pltpu.VMEM((2, HD, HD), F4), pltpu.VMEM((HD, 512), F4)] + scratch,
        compiler_params=params(32 * 1024 * 1024),
        cost_estimate=pl.CostEstimate(
            flops=10**10, bytes_accessed=16 * 10**6, transcendentals=8 * 10**6
        ),
        name=name,
    )(*arrays)


def compute_early(shared, pairs, msgs):
    sums = jax.ShapeDtypeStruct((ALL_BLOCKS, BLK, HD), F4)
    blocks = jax.ShapeDtypeStruct((ALL_BLOCKS, BLK, HD), BF)
    outs = [sums, sums, blocks, blocks, blocks]
    return compute(early_kernel, "compute_early", (*shared, *pairs, *msgs), outs, [])


def compute_late(shared, arranged, sums, msgs):
    outs = [
        jax.ShapeDtypeStruct((TREE_BLOCKS, BLK, HD), F4),
        jax.ShapeDtypeStruct((TREE_BLOCKS, BLK, HD), BF),
    ] + [jax.ShapeDtypeStruct((32, 8, HD), F4)] * 2
    held = pltpu.VMEM((ALL_BLOCKS, BLK, HD), F4)
    arrays = (*shared, *arranged, *sums, *msgs)
    return compute(late_kernel, "compute_late", arrays, outs, [held, held])


def join_cores_kernel(keep, other, stay, *outs):
    for block in range(TREE_BLOCKS):
        ky, at = block // 8, block % 8
        total = keep[block] + other[block].astype(F4)
        if ky == 0:
            stay[at] = total
        else:
            outs[ky - 1][at] = total.astype(BF)


def join_cores(keep, other):
    return pl.pallas_call(
        join_cores_kernel,
        in_specs=[vmem()] * 2,
        out_specs=[vmem()] * 4,
        out_shape=[jax.ShapeDtypeStruct((8, BLK, HD), F4)]
        + [jax.ShapeDtypeStruct((8, BLK, HD), BF)] * 3,
        compiler_params=params(),
        name="join_cores",
    )(keep, other)


def sum_pairs_kernel(ids, stay, r1, r2, r3, roots, o0, o1, o2, o3, held):
    x, c = ids[0], ids[2]
    total = roots[0]
    for n in range(1, 32):
        total = total + roots[n]
    held[...] = total
    for k, out in enumerate((o0, o1, o2, o3)):
        for dc in range(2):
            block = lax.rem(x + k, 4) * 2 + flip(c, dc)
            rest = r1[block].astype(F4) + r2[block].astype(F4) + r3[block].astype(F4)
            out[dc, 0:BLK, :] = stay[block] + rest
            row = held[pl.ds(block, 1), :]
            out[dc, BLK : BLK + 8, :] = jnp.broadcast_to(row, (8, HD))


def sum_pairs(ids, stay, received, roots):
    return pl.pallas_call(
        sum_pairs_kernel,
        in_specs=[smem()] + [vmem()] * 5,
        out_specs=[vmem()] * 4,
        out_shape=[jax.ShapeDtypeStruct((2, BLK + 8, HD), F4)] * 4,
        scratch_shapes=[pltpu.VMEM((8, HD), F4)],
        compiler_params=params(),
        name="sum_pairs",
    )(ids, stay, *received, roots)


def unpack_pairs_kernel(ids, s0, s1, s2, s3, crossed, out, root_out):
    x, c = ids[0], ids[2]
    for k, straight in enumerate((s0, s1, s2, s3)):
        for dc in range(2):
            kind = flip(c, dc)
            part = crossed[k] if dc else straight[0]
            scale = jnp.where(kind == 0, FACTOR, 1.0).astype(F4)
            col = kind * 512 + lax.rem(x - k + 4, 4) * HD
            cols = pl.ds(pl.multiple_of(col, HD), HD)
            out[:, cols] = part[0:BLK] * scale
            root_out[:, cols] = part[BLK : BLK + 1] * scale


def unpack_pairs(ids, sums, crossed):
    return pl.pallas_call(
        unpack_pairs_kernel,
        in_specs=[smem()] + [vmem()] * 5,
        out_specs=[vmem()] * 2,
        out_shape=[
            jax.ShapeDtypeStruct((BLK, 1024), F4),
            jax.ShapeDtypeStruct((1, 1024), F4),
        ],
        compiler_params=params(),
        name="unpack_pairs",
    )(ids, *sums, crossed)


def unpack_query_kernel(ids, *refs):
    x, c = ids[0], ids[2]
    back, crossed, out, root_out, held, sems = refs[0:4], *refs[4:]
    copies = []
    for i in range(8):
        k, dc = i // 2, i % 2
        dest = lax.rem(x + k, 4) * 2 + flip(c, dc)
        part = crossed[k] if dc else back[k][0]
        for h in range(4):
            cols = pl.ds(pl.multiple_of(dest * 512 + h * HD, HD), HD)
            held[:, cols] = part[h * BLK : (h + 1) * BLK, :].astype(F4)
        root_out[dest] = part[512:528, :].astype(F4)[0:4]
        cols = pl.ds(pl.multiple_of(dest * 512, 512), 512)
        copies.append(pltpu.make_async_copy(held.at[:, cols], out.at[:, cols], sems.at[i]))
        copies[-1].start()
    for copy in copies:
        copy.wait()


def unpack_query(ids, back, crossed):
    return pl.pallas_call(
        unpack_query_kernel,
        in_specs=[smem()] + [vmem()] * 5,
        out_specs=[pl.BlockSpec(memory_space=pl.ANY), vmem()],
        out_shape=[
            jax.ShapeDtypeStruct((BLK, 4096), F4),
            jax.ShapeDtypeStruct((8, 4, HD), F4),
        ],
        scratch_shapes=[pltpu.VMEM((BLK, 4096), F4), pltpu.SemaphoreType.DMA((8,))],
        compiler_params=params(),
        cost_estimate=pl.CostEstimate(
            flops=10**6, bytes_accessed=4 * 10**6, transcendentals=0
        ),
        name="unpack_query",
    )(ids, *back, crossed)


def along(array):
    return lax.all_to_all(array, ("leaf", "y"), 0, 0, tiled=True)


def shards(
    query_tree,
    output_tree,
    cotangent_tree,
    log_norm_tree,
    key_value_tree,
    query_root,
    output_root,
    cotangent_root,
    log_norm_root,
    key_value_root,
    parent,
    node_length,
):
    ids = jnp.stack([lax.axis_index(name) for name in ("x", "y", "core", "leaf")])
    ids = ids.astype(jnp.int32)
    together = lax.optimization_barrier

    pair_parts = pack_pairs(ids, key_value_tree, key_value_root)
    pair_parts = [pair_parts[0]] + [shift(pair_parts[k], dx=k) for k in range(1, 4)]
    keep, send = pack_rows(
        ids,
        query_tree,
        output_tree,
        cotangent_tree,
        log_norm_tree,
        query_root,
        output_root,
        cotangent_root,
        log_norm_root.reshape(1, 32),
    )
    keep, send, *pair_parts = together((keep, send, *pair_parts))

    merged = merge_rows(keep, shift(send, dc=1))
    crossed = shift(jnp.stack([part[1] for part in pair_parts], axis=0), dc=1)
    joined, root_rows = join_pairs(ids, pair_parts, crossed)
    tables = make_tables(ids, parent, node_length)
    joined, root_rows, *rest = together((joined, root_rows, *merged, *tables))
    merged, tables = rest[0:4], rest[4:8]
    kbit, qanc, lists, counts = tables

    msg2 = shift(merged[2], dx=2)
    own = [joined] + [shift(joined, dy=ky) for ky in range(1, 4)]
    root_own = along(root_rows)
    msg2, merged[1], merged[3], root_own, *own = together(
        (msg2, merged[1], merged[3], root_own, *own)
    )

    msgs = [merged[0], shift(merged[1], dx=1), msg2, shift(merged[3], dx=3)]
    own = jnp.stack(own, axis=0)
    other, root_other = shift(own, dc=1), shift(root_own, dc=1)
    shared = (ids, lists, counts, kbit, qanc)
    pairs = (own, other, root_own, root_other)
    part0, part2, *state = compute_early(shared, pairs, (msgs[0], msgs[2]))
    msg1, msg3, part0, part2, *state = together((msgs[1], msgs[3], part0, part2, *state))

    part1, part3, keep, send, root_keep, root_send = compute_late(
        shared, state[2:5], state[0:2], (msg1, msg3)
    )
    back2 = shift(part2, dx=-2)
    back2, part1, part3, keep, send, root_keep, root_send = together(
        (back2, part1, part3, keep, send, root_keep, root_send)
    )

    stay, *low = join_cores(keep, shift(send, dc=1))
    root_sums = root_keep + shift(root_send, dc=1)
    stay, root_sums, *low = together((stay, root_sums, *low))

    received = [shift(low[ky - 1], dy=-ky) for ky in range(1, 4)]
    back1, back3 = shift(part1, dx=-1), shift(part3, dx=-3)
    roots = along(root_sums)
    stay, roots, back1, back3, *received = together((stay, roots, back1, back3, *received))

    sums = sum_pairs(ids, stay, received, roots)
    sums = [sums[0]] + [shift(sums[k], dx=k) for k in range(1, 4)]
    back = [part0, back1, back2, back3]
    crossed = shift(jnp.stack([part[1] for part in back], axis=0), dc=1)
    grad_query, grad_query_root = unpack_query(ids, back, crossed)
    grad_query, grad_query_root, *sums = together((grad_query, grad_query_root, *sums))

    crossed_sums = shift(jnp.stack([part[1] for part in sums], axis=0), dc=1)
    grad_pairs, grad_root = unpack_pairs(ids, sums, crossed_sums)
    return grad_query, grad_query_root.reshape(1, 4096), grad_pairs, grad_root


def solution(mesh):
    axes = ("leaf", "x", "y", "core")
    finer = Mesh(mesh.devices.reshape(8, 4, 4, 2), axes)
    rows = P(axes, None)
    lanes = P(None, axes)
    tree = P("leaf", None)
    return jax.shard_map(
        shards,
        mesh=finer,
        in_specs=(rows, rows, rows, lanes, rows, rows, rows, rows, lanes, rows, tree, tree),
        out_specs=(rows, rows, rows, rows),
        check_vma=False,
    )
```

```python
import math

import jax
import jax.numpy as jnp
from jax import lax
from jax.experimental import pallas as pl
from jax.experimental.pallas import tpu as pltpu
from jax.sharding import Mesh
from jax.sharding import PartitionSpec as P

HD = 128
NODES = 24
BLK = 128
ROOT_BIT = 1 << 24
TREE_BLOCKS = 32
ALL_BLOCKS = 35
ROOT_BLOCK = 33
FACTOR = HD ** (-0.5)
LOG2E = math.log2(math.e)
SCALE2 = FACTOR * LOG2E
BF = jnp.bfloat16
F4 = jnp.float32
Q0, D0, R0, T0, MSG = 0, 512, 1024, 1040, 1088
PAIR = 144
VMEM_LIMIT = 24 * 1024 * 1024


def params(limit=VMEM_LIMIT):
    return pltpu.CompilerParams(vmem_limit_bytes=limit)


def perm(dx, dy, dc):
    pairs = []
    for x in range(4):
        for y in range(4):
            for c in range(2):
                target = ((x + dx) % 4) * 8 + ((y + dy) % 4) * 2 + (c ^ dc)
                pairs.append((x * 8 + y * 2 + c, target))
    return pairs


def shift(array, dx=0, dy=0, dc=0):
    return lax.ppermute(array, ("x", "y", "core"), perm(dx, dy, dc))


def nt(left, right):
    return lax.dot_general(left, right, (((1,), (1,)), ((), ())), preferred_element_type=F4)


def nn(left, right):
    return lax.dot_general(left, right, (((1,), (0,)), ((), ())), preferred_element_type=F4)


def iota(shape, dim):
    return lax.broadcasted_iota(jnp.int32, shape, dim)


def flip(c, dc):
    return c if dc == 0 else 1 - c


def smem():
    return pl.BlockSpec(memory_space=pltpu.SMEM)


def vmem():
    return pl.BlockSpec(memory_space=pltpu.VMEM)


def tables_kernel(ids, parent, length, kbit, qanc, lists, counts, start, anc, kmask, qmask):
    x, y, c = ids[0], ids[1], ids[2]
    for block in range(TREE_BLOCKS):
        kmask[block] = 0
        qmask[block] = 0
    total = jnp.int32(0)
    for n in range(NODES):
        start[n] = total
        bits = jnp.int32(1 << n)
        if n > 0:
            bits = bits | anc[parent[0, n]]
        anc[n] = bits
        begin = total
        first = total // BLK
        total = total + length[0, n]
        last = (total - 1) // BLK

        def mark(block, carry):
            kmask[block] = kmask[block] | jnp.int32(1 << n)
            qmask[block] = qmask[block] | bits
            inside = iota((BLK, BLK), 0) + block * BLK >= begin
            kbit[block] = jnp.where(inside, jnp.int32(1 << n), kbit[block])
            return carry

        lax.fori_loop(first, last + 1, mark, 0)
    positions = iota((TREE_BLOCKS, BLK), 0) * BLK + iota((TREE_BLOCKS, BLK), 1)
    table = jnp.full((TREE_BLOCKS, BLK), ROOT_BIT, jnp.int32)
    for n in range(NODES):
        inside = positions >= start[n]
        table = jnp.where(inside, anc[n] | ROOT_BIT, table)
    qanc[...] = table
    kbit[TREE_BLOCKS] = jnp.zeros((BLK, BLK), jnp.int32)
    for block in range(ROOT_BLOCK, ALL_BLOCKS):
        kbit[block] = jnp.full((BLK, BLK), ROOT_BIT, jnp.int32)
    for i in range(8):
        mine = (lax.rem(x - i // 2 + 4, 4)) * 8 + y * 2 + flip(c, i % 2)
        seen = qmask[mine]
        lists[i, 0] = ROOT_BLOCK
        lists[i, 1] = ROOT_BLOCK + 1

        found = jnp.int32(2)
        for block in range(TREE_BLOCKS):
            hit = ((seen & kmask[block]) != 0) & (block <= mine)
            lists[i, found] = block
            found = found + hit.astype(jnp.int32)
        lists[i, found] = TREE_BLOCKS
        counts[i] = (found + 1) // 2


def make_tables(ids, parent, length):
    return pl.pallas_call(
        tables_kernel,
        in_specs=[smem(), smem(), smem()],
        out_specs=[vmem(), vmem(), smem(), smem()],
        out_shape=[
            jax.ShapeDtypeStruct((ALL_BLOCKS, BLK, BLK), jnp.int32),
            jax.ShapeDtypeStruct((TREE_BLOCKS, BLK), jnp.int32),
            jax.ShapeDtypeStruct((8, 40), jnp.int32),
            jax.ShapeDtypeStruct((8,), jnp.int32),
        ],
        scratch_shapes=[
            pltpu.SMEM((NODES,), jnp.int32),
            pltpu.SMEM((NODES,), jnp.int32),
            pltpu.SMEM((TREE_BLOCKS,), jnp.int32),
            pltpu.SMEM((TREE_BLOCKS,), jnp.int32),
        ],
        compiler_params=params(),
        cost_estimate=pl.CostEstimate(
            flops=10**6, bytes_accessed=4 * 10**6, transcendentals=0
        ),
        name="tables",
    )(ids, parent, length)


def pack_pairs_kernel(ids, pairs, root, *outs):
    x, c = ids[0], ids[2]
    for k in range(4):
        for s in range(2):
            col = flip(c, s) * 4 + lax.rem(x + k, 4)
            cols = pl.ds(pl.multiple_of(col * HD, HD), HD)
            outs[k][s, 0:BLK, :] = pairs[:, cols]
            row = jnp.broadcast_to(root[:, cols].astype(F4), (16, HD))
            tail = jnp.where(iota((16, HD), 0) == 0, row, 0.0)
            outs[k][s, BLK:PAIR, :] = tail.astype(BF)


def pack_pairs(ids, pairs, root):
    return pl.pallas_call(
        pack_pairs_kernel,
        in_specs=[smem()] + [vmem()] * 2,
        out_specs=[vmem()] * 4,
        out_shape=[jax.ShapeDtypeStruct((2, PAIR, HD), BF)] * 4,
        compiler_params=params(),
        name="pack_pairs",
    )(ids, pairs, root)


def split3(value):
    high = value.astype(BF)
    rest = value - high.astype(F4)
    middle = rest.astype(BF)
    low = (rest - middle.astype(F4)).astype(BF)
    return jnp.concatenate([high, middle, low], axis=0)


def pack_rows_kernel(ids, *refs):
    sources, keep, send, held, stage, sems = (
        refs[0:8],
        refs[8],
        refs[9],
        refs[10:18],
        refs[18],
        refs[19],
    )
    written = []
    x, c = ids[0], ids[2]

    def target(i):
        return lax.rem(x + i // 2, 4) * 2 + flip(c, i % 2)

    small = [
        pltpu.make_async_copy(sources[n], held[n], sems.at[8, n - 3]) for n in range(3, 8)
    ]
    pieces = []
    for i in range(8):
        cols = pl.ds(pl.multiple_of(target(i) * 512, 512), 512)
        pieces.append(
            [
                pltpu.make_async_copy(sources[n].at[:, cols], held[n].at[:, cols], sems.at[i, n])
                for n in range(3)
            ]
        )
    for copy in small + sum(pieces, []):
        copy.start()
    for copy in small:
        copy.wait()
    query, output, cotangent, norm, rquery, routput, rcotangent, rnorm = held
    norms = rnorm[...] * LOG2E
    for i in range(8):
        k, dc = i // 2, i % 2
        dest = target(i)
        for copy in pieces[i]:
            copy.wait()
        deltas = []
        for h in range(4):
            cols = pl.ds(pl.multiple_of(dest * 512 + h * HD, HD), HD)
            stage[i, Q0 + h * BLK : Q0 + (h + 1) * BLK, :] = query[:, cols]
            grad = cotangent[:, cols]
            stage[i, D0 + h * BLK : D0 + (h + 1) * BLK, :] = grad
            product = grad.astype(F4) * output[:, cols].astype(F4)
            deltas.append(jnp.sum(product.T, axis=0, keepdims=True))
        lane = iota((1, HD), 1)
        rnorm_row = jnp.zeros((1, HD), F4)
        rdelta_row = jnp.zeros((1, HD), F4)
        rquery_rows, rgrad_rows = [], []
        for h in range(4):
            cols = pl.ds(pl.multiple_of(dest * 512 + h * HD, HD), HD)
            rgrad = rcotangent[:, cols].astype(F4)
            rquery_rows.append(rquery[:, cols].astype(F4))
            rgrad_rows.append(rgrad)
            rdelta = jnp.sum(rgrad * routput[:, cols].astype(F4), axis=1, keepdims=True)
            here = lane == i * 4 + h
            mine = jnp.where(iota((1, 32), 1) == dest * 4 + h, norms, 0.0)
            mine = jnp.broadcast_to(jnp.sum(mine, axis=1, keepdims=True), (1, HD))
            rnorm_row = jnp.where(here, mine, rnorm_row)
            rdelta_row = jnp.where(here, jnp.broadcast_to(rdelta, (1, HD)), rdelta_row)
        rows = jnp.concatenate(
            [norm[pl.ds(dest * 4, 4), :] * LOG2E]
            + deltas
            + [rnorm_row, rdelta_row, jnp.zeros((6, HD), F4)],
            axis=0,
        )
        stage[i, T0 : T0 + 48, :] = split3(rows)
        tile = jnp.concatenate(rquery_rows + rgrad_rows + [jnp.zeros((8, HD), F4)], axis=0)
        stage[i, R0 : R0 + 16, :] = tile.astype(BF)
        home = (send if dc else keep).at[k]
        written.append(pltpu.make_async_copy(stage.at[i], home, sems.at[i, 3]))
        written[-1].start()
    for copy in written:
        copy.wait()


def pack_rows(ids, query, output, cotangent, norm, rquery, routput, rcotangent, rnorm):
    return pl.pallas_call(
        pack_rows_kernel,
        in_specs=[smem()] + [pl.BlockSpec(memory_space=pl.ANY)] * 8,
        out_specs=[pl.BlockSpec(memory_space=pl.ANY)] * 2,
        out_shape=[jax.ShapeDtypeStruct((4, MSG, HD), BF)] * 2,
        scratch_shapes=[pltpu.VMEM((BLK, 4096), BF)] * 3
        + [pltpu.VMEM((32, BLK), F4)]
        + [pltpu.VMEM((1, 4096), BF)] * 3
        + [
            pltpu.VMEM((1, 32), F4),
            pltpu.VMEM((8, MSG, HD), BF),
            pltpu.SemaphoreType.DMA((9, 5)),
        ],
        compiler_params=params(60 * 1024 * 1024),
        name="pack_rows",
    )(ids, query, output, cotangent, norm, rquery, routput, rcotangent, rnorm)


def merge_rows_kernel(keep, other, *outs):
    for k in range(4):
        outs[k][0] = keep[k]
        outs[k][1] = other[k]


def merge_rows(keep, other):
    return pl.pallas_call(
        merge_rows_kernel,
        in_specs=[vmem()] * 2,
        out_specs=[vmem()] * 4,
        out_shape=[jax.ShapeDtypeStruct((2, MSG, HD), BF)] * 4,
        compiler_params=params(),
        name="merge_rows",
    )(keep, other)


def unsplit(rows):
    wide = rows.astype(F4)
    return wide[0:16] + wide[16:32] + wide[32:48]


def join_pairs_kernel(ids, g0, g1, g2, g3, crossed, out, root_out):
    x, c = ids[0], ids[2]
    tile = jnp.zeros((16, HD), F4)
    for k, straight in enumerate((g0, g1, g2, g3)):
        for dc in range(2):
            block = lax.rem(x - k + 4, 4) * 2 + flip(c, dc)
            part = crossed[k] if dc else straight[0]
            out[block] = part[0:BLK]
            row = jnp.broadcast_to(part[BLK:PAIR].astype(F4)[0:1], (16, HD))
            tile = jnp.where(iota((16, HD), 0) == block, row, tile)
    for target in range(32):
        root_out[target] = tile.astype(BF)


def join_pairs(ids, parts, crossed):
    return pl.pallas_call(
        join_pairs_kernel,
        in_specs=[smem()] + [vmem()] * 5,
        out_specs=[vmem()] * 2,
        out_shape=[
            jax.ShapeDtypeStruct((8, BLK, HD), BF),
            jax.ShapeDtypeStruct((32, 16, HD), BF),
        ],
        compiler_params=params(),
        name="join_pairs",
    )(ids, *parts, crossed)


def place(y, ky, block):
    return (block // 2) * 8 + lax.rem(y - ky + 4, 4) * 2 + block % 2


def lanes_of(terms, start):
    return jnp.concatenate([terms[start + h : start + h + 1, :] for h in range(4)], axis=1)


def arrange(ids, own, other, root_own, root_other, keys, values, keys_t):
    y, c = ids[1], ids[2]
    first = c == 0

    def load(key_ref, value_ref):
        for ky in range(4):
            for block in range(8):
                to = place(y, ky, block)
                part = key_ref[ky, block]
                keys[to] = part
                keys_t[to] = part.astype(F4).T.astype(BF)
                values[to] = value_ref[ky, block]

    @pl.when(first)
    def _():
        load(own, other)

    @pl.when(c != 0)
    def _():
        load(other, own)

    keys[TREE_BLOCKS] = jnp.zeros((BLK, HD), BF)
    keys_t[TREE_BLOCKS] = jnp.zeros((BLK, HD), BF)
    values[TREE_BLOCKS] = jnp.zeros((BLK, HD), BF)

    rows_own = root_own[...].astype(F4)[:, 0:8, :].reshape(256, HD)
    rows_other = root_other[...].astype(F4)[:, 0:8, :].reshape(256, HD)
    key_wide = jnp.where(first, rows_own, rows_other)
    rkey, rkey_t = key_wide.astype(BF), key_wide.T.astype(BF)
    rvalue = jnp.where(first, rows_other, rows_own).astype(BF)
    for n in range(2):
        rows = slice(n * BLK, (n + 1) * BLK)
        keys[ROOT_BLOCK + n] = rkey[rows]
        values[ROOT_BLOCK + n] = rvalue[rows]
        keys_t[ROOT_BLOCK + n] = rkey_t[:, rows]


def early_kernel(ids, lists, counts, kbit, qanc, own, other, root_own, root_other, m0, m1,
                 o0, o1, dk, dv, keys, values, keys_t, root_rows, acc):
    arrange(ids, own, other, root_own, root_other, keys, values, keys_t)
    dk[...] = jnp.zeros(dk.shape, F4)
    dv[...] = jnp.zeros(dv.shape, F4)
    work((0, 2), ids, lists, counts, kbit, qanc, keys, values, keys_t, (m0, m1), (o0, o1),
         root_rows, acc, dk, dv)


def late_kernel(ids, lists, counts, kbit, qanc, keys, values, keys_t, dk0, dv0, m0, m1,
                o0, o1, keep, send, root_keep, root_send, root_rows, acc, dk, dv):
    dk[...] = dk0[...]
    dv[...] = dv0[...]
    work((1, 3), ids, lists, counts, kbit, qanc, keys, values, keys_t, (m0, m1), (o0, o1),
         root_rows, acc, dk, dv)
    y = ids[1]

    def store(keep_from, send_from):
        rows = slice(ROOT_BLOCK, ROOT_BLOCK + 2)
        for ky in range(4):
            for block in range(8):
                at, to = place(y, ky, block), ky * 8 + block
                keep[to] = keep_from[at]
                send[to] = send_from[at].astype(BF)
        root_keep[...] = keep_from[rows].reshape(32, 8, HD)
        root_send[...] = send_from[rows].reshape(32, 8, HD)

    @pl.when(ids[2] == 0)
    def _():
        store(dk, dv)

    @pl.when(ids[2] != 0)
    def _():
        store(dv, dk)


def work(ks, ids, lists, counts, kbit, qanc, keys, values, keys_t, msgs, outs, root_rows, acc,
         dk, dv):
    x, y, c, z = ids[0], ids[1], ids[2], ids[3]
    rkey = jnp.concatenate([keys[ROOT_BLOCK], keys[ROOT_BLOCK + 1]], axis=0)
    rvalue = jnp.concatenate([values[ROOT_BLOCK], values[ROOT_BLOCK + 1]], axis=0)
    rkey_t = jnp.concatenate([keys_t[ROOT_BLOCK], keys_t[ROOT_BLOCK + 1]], axis=1)
    root_rows[...] = jnp.zeros(root_rows.shape, F4)
    special = jnp.zeros((16, HD), F4)
    for i in [2 * k + dc for k in ks for dc in range(2)]:
        msg, dc = msgs[ks.index(i // 2)], i % 2
        special = special + unsplit(msg[dc, T0 : T0 + 48, :])
        tile = msg[dc, R0 : R0 + 16, :].astype(F4)
        root_rows[0, i * 4 : i * 4 + 4, :] = tile[0:4]
        root_rows[1, i * 4 : i * 4 + 4, :] = tile[4:8]
    query = root_rows[0].astype(BF)
    grad = root_rows[1].astype(BF)
    lane, row = iota((256, HD), 1), iota((256, HD), 0)
    source = lane // 4
    source_x = lax.rem(x - source // 2 + 16, 4)
    source_c = jnp.where(source % 2 == 0, c, 1 - c)
    root_query_pos = z * 32 + source_x * 8 + y * 2 + source_c
    at = row // 8
    root_key_pos = (at // 4) * 32 + (row % 8 // 2) * 8 + (at % 4) * 2 + row % 2
    here = (source // 2 == ks[0]) | (source // 2 == ks[1])
    mask = here & (root_key_pos <= root_query_pos)
    prob = jnp.where(mask, jnp.exp2(nt(rkey, query) * SCALE2 - special[8:9, :]), 0.0)
    dscore = (prob * (nt(rvalue, grad) - special[9:10, :])).astype(BF)
    rows = slice(ROOT_BLOCK, ROOT_BLOCK + 2)
    dv[rows] = dv[rows] + nn(prob.astype(BF), grad).reshape(2, BLK, HD)
    dk[rows] = dk[rows] + nn(dscore, query).reshape(2, BLK, HD)
    root_dq = nn(rkey_t, dscore).T * FACTOR

    pad = jnp.zeros((12, HD), F4)
    base = iota((BLK, BLK), 0)
    for slot, k in enumerate(ks):
        msg, out = msgs[slot], outs[slot]
        for dc in range(2):
            tile = root_dq[8 * k + 4 * dc : 8 * k + 4 * dc + 4]
            out[dc, 512:528, :] = jnp.concatenate([tile, pad], axis=0).astype(BF)

        def query_block(dc, carry):
            i = k * 2 + dc
            mine = lax.rem(x - k + 4, 4) * 8 + y * 2 + jnp.where(dc == 0, c, 1 - c)
            anc_row = jnp.broadcast_to(qanc[pl.ds(mine, 1), :], (BLK, BLK))
            query_pos = iota((BLK, BLK), 1) + mine * BLK
            terms = unsplit(msg[dc, T0 : T0 + 48, :])
            norm, delta = lanes_of(terms, 0), lanes_of(terms, 4)

            def gradients(key, value, key_t, mask):
                query = msg[dc, Q0 : Q0 + 512, :]
                grad = msg[dc, D0 : D0 + 512, :]
                prob = jnp.exp2(nt(key, query) * SCALE2 - norm)
                prob = jnp.where(jnp.concatenate([mask] * 4, axis=1), prob, 0.0)
                dscore = (prob * (nt(value, grad) - delta)).astype(BF)
                return nn(dscore, query), nn(prob.astype(BF), grad), nn(key_t, dscore)

            acc[...] = jnp.zeros(acc.shape, F4)

            def position(block):
                return jnp.where(block < ROOT_BLOCK, block, -2) * BLK

            def unit(start, width):
                at = [lists[i, start + n] for n in range(width)]
                key = jnp.concatenate([keys[b] for b in at], axis=0)
                value = jnp.concatenate([values[b] for b in at], axis=0)
                key_t = jnp.concatenate([keys_t[b] for b in at], axis=1)
                masks = [
                    ((kbit[b] & anc_row) != 0) & (base + position(b) <= query_pos) for b in at
                ]
                mask = jnp.concatenate(masks, axis=0)
                dk_part, dv_part, dq_part = gradients(key, value, key_t, mask)
                acc[...] = acc[...] + dq_part
                for n, b in enumerate(at):
                    dk[b] = dk[b] + dk_part[n * BLK : (n + 1) * BLK]
                    dv[b] = dv[b] + dv_part[n * BLK : (n + 1) * BLK]

            def four(j, inner):
                unit(4 * j, 4)
                return inner

            count = counts[i]
            lax.fori_loop(0, count // 2, four, 0)

            @pl.when(count % 2 == 1)
            def _():
                unit(2 * count - 2, 2)

            for h in range(4):
                done = acc[:, h * BLK : (h + 1) * BLK].T * FACTOR
                out[dc, h * BLK : (h + 1) * BLK, :] = done.astype(BF)
            return carry

        lax.fori_loop(0, 2, query_block, 0)


def compute(kernel, name, arrays, outs, scratch):
    part = jax.ShapeDtypeStruct((2, 528, HD), BF)
    return pl.pallas_call(
        kernel,
        in_specs=[smem()] * 3 + [vmem()] * (len(arrays) - 3),
        out_specs=[vmem()] * (2 + len(outs)),
        out_shape=[part, part] + outs,
        scratch_shapes=[pltpu.VMEM((2, HD, HD), F4), pltpu.VMEM((HD, 512), F4)] + scratch,
        compiler_params=params(32 * 1024 * 1024),
        cost_estimate=pl.CostEstimate(
            flops=10**10, bytes_accessed=16 * 10**6, transcendentals=8 * 10**6
        ),
        name=name,
    )(*arrays)


def compute_early(shared, pairs, msgs):
    sums = jax.ShapeDtypeStruct((ALL_BLOCKS, BLK, HD), F4)
    blocks = jax.ShapeDtypeStruct((ALL_BLOCKS, BLK, HD), BF)
    outs = [sums, sums, blocks, blocks, blocks]
    return compute(early_kernel, "compute_early", (*shared, *pairs, *msgs), outs, [])


def compute_late(shared, arranged, sums, msgs):
    outs = [
        jax.ShapeDtypeStruct((TREE_BLOCKS, BLK, HD), F4),
        jax.ShapeDtypeStruct((TREE_BLOCKS, BLK, HD), BF),
    ] + [jax.ShapeDtypeStruct((32, 8, HD), F4)] * 2
    held = pltpu.VMEM((ALL_BLOCKS, BLK, HD), F4)
    arrays = (*shared, *arranged, *sums, *msgs)
    return compute(late_kernel, "compute_late", arrays, outs, [held, held])


def join_cores_kernel(keep, other, stay, *outs):
    for block in range(TREE_BLOCKS):
        ky, at = block // 8, block % 8
        total = keep[block] + other[block].astype(F4)
        if ky == 0:
            stay[at] = total
        else:
            outs[ky - 1][at] = total.astype(BF)


def join_cores(keep, other):
    return pl.pallas_call(
        join_cores_kernel,
        in_specs=[vmem()] * 2,
        out_specs=[vmem()] * 4,
        out_shape=[jax.ShapeDtypeStruct((8, BLK, HD), F4)]
        + [jax.ShapeDtypeStruct((8, BLK, HD), BF)] * 3,
        compiler_params=params(),
        name="join_cores",
    )(keep, other)


def sum_pairs_kernel(ids, stay, r1, r2, r3, roots, o0, o1, o2, o3, held):
    x, c = ids[0], ids[2]
    total = roots[0]
    for n in range(1, 32):
        total = total + roots[n]
    held[...] = total
    for k, out in enumerate((o0, o1, o2, o3)):
        for dc in range(2):
            block = lax.rem(x + k, 4) * 2 + flip(c, dc)
            rest = r1[block].astype(F4) + r2[block].astype(F4) + r3[block].astype(F4)
            out[dc, 0:BLK, :] = stay[block] + rest
            row = held[pl.ds(block, 1), :]
            out[dc, BLK : BLK + 8, :] = jnp.broadcast_to(row, (8, HD))


def sum_pairs(ids, stay, received, roots):
    return pl.pallas_call(
        sum_pairs_kernel,
        in_specs=[smem()] + [vmem()] * 5,
        out_specs=[vmem()] * 4,
        out_shape=[jax.ShapeDtypeStruct((2, BLK + 8, HD), F4)] * 4,
        scratch_shapes=[pltpu.VMEM((8, HD), F4)],
        compiler_params=params(),
        name="sum_pairs",
    )(ids, stay, *received, roots)


def unpack_pairs_kernel(ids, s0, s1, s2, s3, crossed, out, root_out):
    x, c = ids[0], ids[2]
    for k, straight in enumerate((s0, s1, s2, s3)):
        for dc in range(2):
            kind = flip(c, dc)
            part = crossed[k] if dc else straight[0]
            scale = jnp.where(kind == 0, FACTOR, 1.0).astype(F4)
            col = kind * 512 + lax.rem(x - k + 4, 4) * HD
            cols = pl.ds(pl.multiple_of(col, HD), HD)
            out[:, cols] = part[0:BLK] * scale
            root_out[:, cols] = part[BLK : BLK + 1] * scale


def unpack_pairs(ids, sums, crossed):
    return pl.pallas_call(
        unpack_pairs_kernel,
        in_specs=[smem()] + [vmem()] * 5,
        out_specs=[vmem()] * 2,
        out_shape=[
            jax.ShapeDtypeStruct((BLK, 1024), F4),
            jax.ShapeDtypeStruct((1, 1024), F4),
        ],
        compiler_params=params(),
        name="unpack_pairs",
    )(ids, *sums, crossed)


def unpack_query_kernel(ids, *refs):
    x, c = ids[0], ids[2]
    back, crossed, out, root_out, held, sems = refs[0:4], *refs[4:]
    copies = []
    for i in range(8):
        k, dc = i // 2, i % 2
        dest = lax.rem(x + k, 4) * 2 + flip(c, dc)
        part = crossed[k] if dc else back[k][0]
        for h in range(4):
            cols = pl.ds(pl.multiple_of(dest * 512 + h * HD, HD), HD)
            held[:, cols] = part[h * BLK : (h + 1) * BLK, :].astype(F4)
        root_out[dest] = part[512:528, :].astype(F4)[0:4]
        cols = pl.ds(pl.multiple_of(dest * 512, 512), 512)
        copies.append(pltpu.make_async_copy(held.at[:, cols], out.at[:, cols], sems.at[i]))
        copies[-1].start()
    for copy in copies:
        copy.wait()


def unpack_query(ids, back, crossed):
    return pl.pallas_call(
        unpack_query_kernel,
        in_specs=[smem()] + [vmem()] * 5,
        out_specs=[pl.BlockSpec(memory_space=pl.ANY), vmem()],
        out_shape=[
            jax.ShapeDtypeStruct((BLK, 4096), F4),
            jax.ShapeDtypeStruct((8, 4, HD), F4),
        ],
        scratch_shapes=[pltpu.VMEM((BLK, 4096), F4), pltpu.SemaphoreType.DMA((8,))],
        compiler_params=params(),
        cost_estimate=pl.CostEstimate(
            flops=10**6, bytes_accessed=4 * 10**6, transcendentals=0
        ),
        name="unpack_query",
    )(ids, *back, crossed)


def stack_kernel(*refs):
    out = refs[-1]
    for n, part in enumerate(refs[:-1]):
        out[n] = part[1] if part.shape[0] == 2 else part[...]


def stack(parts, shape):
    return pl.pallas_call(
        stack_kernel,
        in_specs=[vmem()] * len(parts),
        out_specs=vmem(),
        out_shape=jax.ShapeDtypeStruct((len(parts), *shape), parts[0].dtype),
        compiler_params=params(),
        name="stack",
    )(*parts)


def along(array):
    return lax.all_to_all(array, ("leaf", "y"), 0, 0, tiled=True)


def shards(
    query_tree,
    output_tree,
    cotangent_tree,
    log_norm_tree,
    key_value_tree,
    query_root,
    output_root,
    cotangent_root,
    log_norm_root,
    key_value_root,
    parent,
    node_length,
):
    ids = jnp.stack([lax.axis_index(name) for name in ("x", "y", "core", "leaf")])
    ids = ids.astype(jnp.int32)
    together = lax.optimization_barrier

    pair_parts = pack_pairs(ids, key_value_tree, key_value_root)
    pair_parts = [pair_parts[0]] + [shift(pair_parts[k], dx=k) for k in range(1, 4)]
    keep, send = pack_rows(
        ids,
        query_tree,
        output_tree,
        cotangent_tree,
        log_norm_tree,
        query_root,
        output_root,
        cotangent_root,
        log_norm_root.reshape(1, 32),
    )
    keep, send, *pair_parts = together((keep, send, *pair_parts))

    merged = merge_rows(keep, shift(send, dc=1))
    crossed = shift(stack(pair_parts, (PAIR, HD)), dc=1)
    joined, root_rows = join_pairs(ids, pair_parts, crossed)
    tables = make_tables(ids, parent, node_length)
    joined, root_rows, *rest = together((joined, root_rows, *merged, *tables))
    merged, tables = rest[0:4], rest[4:8]
    kbit, qanc, lists, counts = tables

    msg2 = shift(merged[2], dx=2)
    own = [joined] + [shift(joined, dy=ky) for ky in range(1, 4)]
    root_own = along(root_rows)
    msg2, merged[1], merged[3], root_own, *own = together(
        (msg2, merged[1], merged[3], root_own, *own)
    )

    msgs = [merged[0], shift(merged[1], dx=1), msg2, shift(merged[3], dx=3)]
    own = stack(own, (8, BLK, HD))
    other, root_other = shift(own, dc=1), shift(root_own, dc=1)
    shared = (ids, lists, counts, kbit, qanc)
    pairs = (own, other, root_own, root_other)
    part0, part2, *state = compute_early(shared, pairs, (msgs[0], msgs[2]))
    msg1, msg3, part0, part2, *state = together((msgs[1], msgs[3], part0, part2, *state))

    part1, part3, keep, send, root_keep, root_send = compute_late(
        shared, state[2:5], state[0:2], (msg1, msg3)
    )
    back2 = shift(part2, dx=-2)
    back2, part1, part3, keep, send, root_keep, root_send = together(
        (back2, part1, part3, keep, send, root_keep, root_send)
    )

    stay, *low = join_cores(keep, shift(send, dc=1))
    root_sums = root_keep + shift(root_send, dc=1)
    stay, root_sums, *low = together((stay, root_sums, *low))

    received = [shift(low[ky - 1], dy=-ky) for ky in range(1, 4)]
    back1, back3 = shift(part1, dx=-1), shift(part3, dx=-3)
    roots = along(root_sums)
    stay, roots, back1, back3, *received = together((stay, roots, back1, back3, *received))

    sums = sum_pairs(ids, stay, received, roots)
    sums = [sums[0]] + [shift(sums[k], dx=k) for k in range(1, 4)]
    back = [part0, back1, back2, back3]
    crossed = shift(stack(back, (528, HD)), dc=1)
    grad_query, grad_query_root = unpack_query(ids, back, crossed)
    grad_query, grad_query_root, *sums = together((grad_query, grad_query_root, *sums))

    crossed_sums = shift(stack(sums, (BLK + 8, HD)), dc=1)
    grad_pairs, grad_root = unpack_pairs(ids, sums, crossed_sums)
    return grad_query, grad_query_root.reshape(1, 4096), grad_pairs, grad_root


def solution(mesh):
    axes = ("leaf", "x", "y", "core")
    finer = Mesh(mesh.devices.reshape(8, 4, 4, 2), axes)
    rows = P(axes, None)
    lanes = P(None, axes)
    tree = P("leaf", None)
    return jax.shard_map(
        shards,
        mesh=finer,
        in_specs=(rows, rows, rows, lanes, rows, rows, rows, rows, lanes, rows, tree, tree),
        out_specs=(rows, rows, rows, rows),
        check_vma=False,
    )
```
